32 devices in a mesh: fsdp: 16 (over z, y, core), rep: 2 (over x).
Axes of the slice: x: 2, y: 2, z: 4, core: 2. Of those that a mesh axis runs over, the one named last changes fastest.
Arguments:
- hidden_states: bfloat16 [64, 512, 768], P(('fsdp', 'rep')), may hold values from -6 to 6
- page_counts: int32 [64], P(('fsdp', 'rep')), may hold values from 128 to 512, as said below
- cotangent: bfloat16 [64, 512, 768], P(('fsdp', 'rep')), may hold values from -6 to 6
- attn_in_weight: bfloat16 [768, 2304], P('fsdp'), may hold values from -0.21875 to 0.21875
- attn_in_bias: bfloat16 [1536], P('fsdp'), may hold values from -3 to 3
- attn_out_weight: bfloat16 [768, 768], P('fsdp'), may hold values from -2 to 2
- attn_out_bias: bfloat16 [768], P('fsdp'), may hold values from -3 to 3
- first_gain: bfloat16 [768], P('fsdp'), may hold values from 0.099609375 to 1.8984375
- first_shift: bfloat16 [768], P('fsdp'), may hold values from -3 to 3
- up_weight: bfloat16 [768, 3072], P('fsdp'), may hold values from -0.21875 to 0.21875
- up_bias: bfloat16 [3072], P('fsdp'), may hold values from -3 to 3
- down_weight: bfloat16 [3072, 768], P('fsdp'), may hold values from -0.109375 to 0.109375
- down_bias: bfloat16 [768], P('fsdp'), may hold values from -3 to 3
- second_gain: bfloat16 [768], P('fsdp'), may hold values from 0.099609375 to 1.8984375
- second_shift: bfloat16 [768], P('fsdp'), may hold values from -3 to 3
Outputs:
- layer_output: bfloat16 [64, 512, 768], P(('fsdp', 'rep'))
- input_grad: bfloat16 [64, 512, 768], P(('fsdp', 'rep'))
- grad_attn_in_weight: float32 [768, 2304], P('fsdp')
- grad_attn_in_bias: float32 [1536], P('fsdp')
- grad_attn_out_weight: float32 [768, 768], P('fsdp')
- grad_attn_out_bias: float32 [768], P('fsdp')
- grad_first_gain: float32 [768], P('fsdp')
- grad_first_shift: float32 [768], P('fsdp')
- grad_up_weight: float32 [768, 3072], P('fsdp')
- grad_up_bias: float32 [3072], P('fsdp')
- grad_down_weight: float32 [3072, 768], P('fsdp')
- grad_down_bias: float32 [768], P('fsdp')
- grad_second_gain: float32 [768], P('fsdp')
- grad_second_shift: float32 [768], P('fsdp')
The draws below stay inside these ranges and needn't reach their ends.
Inputs may be any that keep to these rules, and one draw needn't show every extreme that they name: The real tokens of a page fill its first page_counts slots; some page of every draw has all 512 slots real.
All inputs are finite; a program needn't handle non-finite values.
Results may differ from the reference program's by a relative error of at most 0.019.
Values may be sent and summed in bfloat16 or wider, within the bound.
No kernel may reach another device: no remote copies, remote signals or barrier semaphores. Data moves between devices by JAX's collectives and lax.ppermute only.
A program may use at most 128 MiB of HBM per device.

```python
import math
import jax
import jax.numpy as jnp
from jax import lax

D = 768
HEADS = 12
HEAD_DIM = 64
FF = 3072
SEQ = 512
PAGES = 64


def draw_page_counts(key, part):
    key = jax.random.fold_in(key, 7)
    first_key, second_key = jax.random.split(key)
    counts = jax.random.randint(first_key, (PAGES,), SEQ // 4, SEQ + 1)
    full_page = jax.random.randint(second_key, (), 0, PAGES)
    return jnp.where(jnp.arange(PAGES) == full_page, SEQ, counts).astype(jnp.int32)


def block_levels(key, dims, shards, least, largest):
    loudness = 1.0
    for dim, shards_of in shards:
        draws = jax.random.uniform(jax.random.fold_in(jax.random.fold_in(key, 6), dim), (shards_of,), jnp.float32, least / len(shards), largest / len(shards))
        loudness = loudness * jnp.repeat(jnp.exp(draws), dims[dim] // shards_of).reshape((-1,) + (1,) * (len(dims) - 1 - dim))
    return loudness


def normal_values(own_key, shape, spread, limit, pieces=(), held_as=jnp.bfloat16):
    entries = spread * jax.random.normal(own_key, shape, jnp.float32)
    if pieces:
        entries = entries * block_levels(own_key, shape, pieces, -0.22, 0.18)
    return jnp.clip(entries, -limit, limit).astype(held_as)


def setup_inputs(seed: int = 0) -> dict:
    splits = jax.random.split(jax.random.key(seed), 16)
    hidden_states = normal_values(splits[0], (PAGES, SEQ, D), 1.0, 6.0, ((0, 32),))
    page_counts = draw_page_counts(jax.random.fold_in(splits[15], 71), 0)
    cotangent = normal_values(splits[2], (PAGES, SEQ, D), 1.0, 6.0, ((0, 32),))
    attn_in_weight = normal_values(splits[3], (D, 3 * D), D ** -0.5, 0.21875, ((0, 16),))
    attn_in_bias = normal_values(splits[4], (2 * D,), 0.5, 3.0, ((0, 16),))
    attn_out_weight = normal_values(splits[5], (D, D), (max(D // 96, 4)) ** -0.5, 2.0, ((0, 16),))
    attn_out_bias = normal_values(splits[6], (D,), 0.5, 3.0, ((0, 16),))
    first_gain = jnp.clip(1.0 + 0.18 * jax.random.normal(splits[7], (D,), jnp.float32), 0.099609375, 1.8984375).astype(jnp.bfloat16)
    first_shift = normal_values(splits[8], (D,), 0.5, 3.0, ((0, 16),))
    up_weight = normal_values(splits[9], (D, FF), D ** -0.5, 0.21875, ((0, 16),))
    up_bias = normal_values(splits[10], (FF,), 0.5, 3.0, ((0, 16),))
    down_weight = normal_values(splits[11], (FF, D), FF ** -0.5, 0.109375, ((0, 16),))
    down_bias = normal_values(splits[12], (D,), 0.5, 3.0, ((0, 16),))
    second_gain = jnp.clip(1.0 + 0.18 * jax.random.normal(splits[13], (D,), jnp.float32), 0.099609375, 1.8984375).astype(jnp.bfloat16)
    second_shift = normal_values(splits[14], (D,), 0.5, 3.0, ((0, 16),))
    return {"hidden_states": hidden_states, "page_counts": page_counts, "cotangent": cotangent, "attn_in_weight": attn_in_weight, "attn_in_bias": attn_in_bias, "attn_out_weight": attn_out_weight, "attn_out_bias": attn_out_bias, "first_gain": first_gain, "first_shift": first_shift, "up_weight": up_weight, "up_bias": up_bias, "down_weight": down_weight, "down_bias": down_bias, "second_gain": second_gain, "second_shift": second_shift}


@jax.custom_vjp
def low(v):
    return lax.optimization_barrier(v.astype(jnp.bfloat16)).astype(jnp.float32)

@jax.custom_vjp
def low_back(v):
    return v

def low_keep(v):
    return (low(v), None)

def low_pass(kept, grad):
    return (grad,)

def back_keep(v):
    return (v, None)

def back_low(kept, grad):
    return (low(grad),)
low.defvjp(low_keep, low_pass)
low_back.defvjp(back_keep, back_low)
norm_epsilon = 1e-12

def product(left_side, right_side):
    return jnp.dot(left_side, right_side, precision=lax.Precision.HIGHEST, preferred_element_type=jnp.float32)

def layer_norm(tensor, norm_gain, norm_shift):
    average = lax.optimization_barrier(jnp.mean(tensor, axis=-1, keepdims=True))
    centred = tensor - average
    variance = lax.optimization_barrier(jnp.mean(centred * centred, axis=-1, keepdims=True))
    return centred * lax.rsqrt(variance + norm_epsilon) * norm_gain + norm_shift

def page_attention(queries, key_rows, value_rows, valid_count):
    query_heads = queries.reshape(SEQ, HEADS, HEAD_DIM)
    key_heads = key_rows.reshape(SEQ, HEADS, HEAD_DIM)
    value_heads = value_rows.reshape(SEQ, HEADS, HEAD_DIM)
    scores = jnp.einsum('qhd,khd->hqk', query_heads, key_heads, precision=lax.Precision.HIGHEST) * (1.0 / math.sqrt(HEAD_DIM))
    is_valid = jnp.arange(SEQ, dtype=jnp.int32) < valid_count
    scores = jnp.where(is_valid[None, None, :], scores, -1e+30)
    scores = low_back(scores)
    attn_weights = low(jax.nn.softmax(scores, axis=-1))
    attended = jnp.einsum('hqk,khd->qhd', attn_weights, value_heads, precision=lax.Precision.HIGHEST)
    return attended.reshape(SEQ, D)

def forward(hidden_block, count_block, params):
    attn_in_weight, attn_in_bias, attn_out_weight, attn_out_bias, first_gain, first_shift, up_weight, up_bias, down_weight, down_bias, second_gain, second_shift = params
    block_pages = hidden_block.shape[0]
    token_rows = hidden_block.reshape(-1, D)
    projected = low_back(product(token_rows, attn_in_weight))
    queries = low(projected[:, :D] + attn_in_bias[:D])
    key_rows = low(projected[:, D:2 * D])
    value_rows = low(projected[:, 2 * D:] + attn_in_bias[D:])
    attend_page = jax.checkpoint(page_attention)
    attended = lax.map(lambda element: attend_page(*element), (queries.reshape(block_pages, SEQ, D), key_rows.reshape(block_pages, SEQ, D), value_rows.reshape(block_pages, SEQ, D), count_block))
    attended = low(low_back(attended.reshape(-1, D)))
    first_sum = token_rows + low_back(product(attended, attn_out_weight)) + attn_out_bias
    normed = layer_norm(first_sum, first_gain, first_shift)
    pre_act = low_back(product(low(normed), up_weight)) + up_bias
    activated = low(jax.nn.gelu(pre_act, approximate=False))
    second_sum = normed + low_back(product(activated, down_weight)) + down_bias
    return layer_norm(second_sum, second_gain, second_shift).reshape(hidden_block.shape)

def reference(hidden_states, page_counts, cotangent, attn_in_weight, attn_in_bias, attn_out_weight, attn_out_bias, first_gain, first_shift, up_weight, up_bias, down_weight, down_bias, second_gain, second_shift):
    params = tuple((weight.astype(jnp.float32) for weight in (attn_in_weight, attn_in_bias, attn_out_weight, attn_out_bias, first_gain, first_shift, up_weight, up_bias, down_weight, down_bias, second_gain, second_shift)))
    page_group = 8
    group_count = PAGES // page_group
    hidden_blocks = hidden_states.astype(jnp.float32).reshape(group_count, page_group, SEQ, D)
    count_blocks = page_counts.astype(jnp.int32).reshape(group_count, page_group)
    grad_blocks = cotangent.astype(jnp.float32).reshape(group_count, page_group, SEQ, D)

    def one_group(totals, element):
        hidden_block, count_block, grad_block = element

        def apply_layer(inputs, weights):
            return forward(inputs, count_block, weights)
        result, pullback = jax.vjp(apply_layer, hidden_block, params)
        input_block, weight_grads = pullback(grad_block)
        totals = jax.tree.map(jnp.add, totals, weight_grads)
        return (totals, (result.astype(jnp.bfloat16), input_block.astype(jnp.bfloat16)))
    initial = tuple((jnp.zeros(weight.shape, jnp.float32) for weight in params))
    totals, (results, input_blocks) = lax.scan(one_group, initial, (hidden_blocks, count_blocks, grad_blocks))
    layer_output = results.reshape(PAGES, SEQ, D)
    input_grad = input_blocks.reshape(PAGES, SEQ, D)
    return (layer_output, input_grad, totals[0], totals[1], totals[2], totals[3], totals[4], totals[5], totals[6], totals[7], totals[8], totals[9], totals[10], totals[11])
```

```python
import math

import jax
import jax.numpy as jnp
from jax import lax
from jax.experimental import pallas as pl
from jax.experimental.pallas import tpu as pltpu
from jax.sharding import PartitionSpec as P

HEADS = 12
BF = jnp.bfloat16
F32 = jnp.float32
NT = (((1,), (1,)), ((), ()))
TN = (((0,), (0,)), ((), ()))
CW = 384
THIRDS = 3
LINE = 4
TINY = 128
AXES = ("fsdp", "rep")


def dg(a, b, dims):
    return lax.dot_general(a, b, dims, preferred_element_type=F32)


def mm(a, b):
    return jnp.dot(a, b, preferred_element_type=F32)


def params():
    return pltpu.CompilerParams(vmem_limit_bytes=60 * 1024 * 1024)


def cost(us):
    return pl.CostEstimate(flops=int(us * 1.15e9), bytes_accessed=int(us * 1e6), transcendentals=0)


def flat_index(z, y, c, x):
    return (z * 4 + y * 2 + c) * 2 + x


def permutation(target):
    pairs = []
    for z in range(LINE):
        for y in range(2):
            for c in range(2):
                for x in range(2):
                    pairs.append((flat_index(z, y, c, x), flat_index(*target(z, y, c, x))))
    return pairs


def to_core(z, y, c, x):
    return (z, y, 1 - c, x)


def to_x(z, y, c, x):
    return (z, y, c, 1 - x)


def to_first(z, y, c, x):
    return (z, y, c, 1 - x) if c == 0 else (z, 1 - y, c, x)


def to_second(z, y, c, x):
    return (z, 1 - y, c, x) if c == 0 else (z, y, c, 1 - x)


def to_line(step):
    return lambda z, y, c, x: ((z + step) % LINE, y, c, x)


def move(value, target):
    return lax.ppermute(value, AXES, permutation(target))


def after(values, *earlier):
    return lax.optimization_barrier((values, earlier))[0]


def along_line(half):
    return [half] + [move(half, to_line(k)) for k in range(1, LINE)]


def over_core(parts):
    return tuple(parts) + tuple(move(part, to_core) for part in parts)


def add_core(keep, got):
    keep, got = keep.astype(F32), got.astype(F32)
    return (keep[1] + got[1]).astype(BF), (keep[0] + got[0]).astype(BF)


def add_last(stay, got):
    return (stay.astype(F32) + got.astype(F32)).astype(BF)


def add_line(low, parts):
    total = low[0].astype(F32)
    for part in parts:
        total = total + part.astype(F32)
    return total.astype(BF)


def move_line(low):
    return [move(low[k], to_line(k)) for k in range(1, LINE)]


FIELDS = (((0, 0, 96), (4, 1, 192)), tuple((n, i, 48) for i, n in enumerate((1, 2, 3, 5, 6, 7))))


def rows_of(width):
    return [(i, at, min(TINY, width - at)) for i, at in enumerate(range(0, width, TINY))]


def pack_kernel(pos, inw, outw, upw, downw, *refs):
    vectors, (one, two, three) = refs[:8], refs[8:]

    def fill(x):
        width = inw.shape[1] // 2
        one[:, :width] = inw[:, x * width : (x + 1) * width]
        row = lax.broadcasted_iota(jnp.int32, (48, TINY), 0)
        block = jnp.zeros((48, TINY), F32)
        for place, top, size in FIELDS[x]:
            for i, at, n in rows_of(size):
                piece = vectors[place][:, at : at + n].astype(F32)
                if n < TINY:
                    piece = jnp.concatenate([piece, jnp.zeros((1, TINY - n), F32)], axis=1)
                block = jnp.where(row == top + i, jnp.broadcast_to(piece, (48, TINY)), block)
        one[:, width:] = block.astype(BF)
        two[:, :CW] = outw[:, x * CW : (x + 1) * CW]
        width = upw.shape[1] // 2
        two[:, CW:] = upw[:, x * width : (x + 1) * width]
        three[...] = downw[:, x * CW : (x + 1) * CW]

    @pl.when(pos[3] == 0)
    def _():
        fill(0)

    @pl.when(pos[3] == 1)
    def _():
        fill(1)


def pack(pos, weights, vectors):
    shapes = [
        (48, weights[0].shape[1] // 2 + TINY),
        (48, weights[1].shape[1] // 2 + weights[2].shape[1] // 2),
        (weights[3].shape[0], CW),
    ]
    arrays = tuple(weights) + tuple(v.reshape(1, -1) for v in vectors)
    full = lambda a: pl.BlockSpec(a, lambda i, p: (0, 0))
    return pl.pallas_call(
        pack_kernel,
        grid_spec=pltpu.PrefetchScalarGridSpec(
            num_scalar_prefetch=1,
            grid=(1,),
            in_specs=[full(a.shape) for a in arrays],
            out_specs=[full(a) for a in shapes],
        ),
        out_shape=[jax.ShapeDtypeStruct(a, BF) for a in shapes],
        compiler_params=params(),
        name="pack",
    )(pos, *arrays)


def sources(pos):
    z, y, c, x = pos[0], pos[1], pos[2], pos[3]
    found = []
    for other in range(2):
        core = c ^ 1 if other else c
        swap = core == 0
        for first in range(2):
            for second in range(2):
                dx = jnp.where(swap, first, second)
                dy = jnp.where(swap, second, first)
                buffer = other * 4 + second * 2 + first
                for k in range(LINE):
                    shard = ((z - k) & (LINE - 1)) * 4 + (y ^ dy) * 2 + core
                    found.append((buffer, k, shard, x ^ dx))
    return found


def fetch(pos, buffers, target, rows, column, width, sem):
    return [
        pltpu.make_async_copy(
            buffers[buffer].at[k, :, pl.ds(column, width)],
            target.at[
                pl.ds(pl.multiple_of(shard * rows, 16), rows),
                pl.ds(pl.multiple_of(x * width, 128), width),
            ],
            sem,
        )
        for buffer, k, shard, x in sources(pos)
    ]


def fetch_tiny(pos, buffers, target, column, sem):
    return [
        pltpu.make_async_copy(
            buffers[buffer].at[k, pl.ds(0, 16), pl.ds(column, TINY)], target.at[x, shard], sem
        )
        for buffer, k, shard, x in sources(pos)
    ]


def run_all(copies):
    for copy in copies:
        copy.start()
    for copy in copies:
        copy.wait()


def unpack_vectors(tiny, targets):
    shards = tiny.shape[1]
    for half in range(2):
        for place, top, size in FIELDS[half]:
            total = shards * size
            tiled = jnp.zeros((shards, total), F32)
            for i, at, n in rows_of(size):
                lane = lax.broadcasted_iota(jnp.int32, (TINY, total), 0)
                spot = lax.broadcasted_iota(jnp.int32, (TINY, total), 1) % size
                spot = jnp.where((lane + at == spot) & (lane < n), 1.0, 0.0).astype(BF)
                tiled = tiled + mm(tiny[half, :, top + i, :], spot)
            owner = lax.broadcasted_iota(jnp.int32, (shards, total), 0)
            place_of = lax.broadcasted_iota(jnp.int32, (shards, total), 1) // size
            targets[place][...] = jnp.sum(jnp.where(place_of == owner, tiled, 0.0), axis=0, keepdims=True)


def scatter_tile(pos, tile, keep, send, x_target, column, rows, shards):
    z, y, c, x = pos[0], pos[1], pos[2], pos[3]
    dx = x_target ^ x
    width = tile.shape[1]
    for i, shard in enumerate(shards):
        piece = tile[rows * i : rows * (i + 1)]
        sz, sy, sc = shard
        dy = sy ^ y
        dz = (sz - z) & (LINE - 1)
        first, second = (dx, dy) if sc == 0 else (dy, dx)

        @pl.when(c == sc)
        def _(piece=piece, first=first, second=second, dz=dz):
            keep[first, second, dz, :, pl.ds(column, width)] = piece

        @pl.when(c != sc)
        def _(piece=piece, first=first, second=second, dz=dz):
            send[first, second, dz, :, pl.ds(column, width)] = piece


ALL = [(s // 4, s // 2 % 2, s % 2) for s in range(16)]


def grad_down_kernel(pos, act, low, keep, send):
    j, i = pl.program_id(0), pl.program_id(1)
    tile = dg(act[...], low[...], TN).astype(BF)
    rows = tile.shape[0] // 4
    scatter_tile(pos, tile, keep, send, j, 0, rows, [(i, s // 2, s % 2) for s in range(4)])


def grad_up_kernel(pos, low, pre, *refs):
    att, (first_low, keep, send) = refs[:-3], refs[-3:]
    j = pl.program_id(0)
    ups = pl.num_programs(0) - 2

    @pl.when(j < ups)
    def _():
        tile = dg(low[...], pre[...], TN).astype(BF)
        column = pl.multiple_of(CW + CW * (j % 4), 128)
        scatter_tile(pos, tile, keep, send, j // 4, column, 48, ALL)

    @pl.when(j >= ups)
    def _():
        tile = dg(joined(att), first_low[...], TN).astype(BF)
        scatter_tile(pos, tile, keep, send, j - ups, 0, 48, ALL)


def tiny_rows(vectors, fields):
    block = jnp.zeros((16 * 48, TINY), F32)
    row = lax.broadcasted_iota(jnp.int32, (16 * 48, 16), 0)
    shard = lax.broadcasted_iota(jnp.int32, (16 * 48, 16), 1)
    for vector, (_, top, size) in zip(vectors, fields):
        length = vector.shape[1]
        owner = lax.broadcasted_iota(jnp.int32, (16, length), 0)
        place = lax.broadcasted_iota(jnp.int32, (16, length), 1)
        own = jnp.where(place // size == owner, jnp.broadcast_to(vector, (16, length)), 0.0).astype(BF)
        place = lax.broadcasted_iota(jnp.int32, (length, TINY), 0) % size
        lane = lax.broadcasted_iota(jnp.int32, (length, TINY), 1)
        for i, at, n in rows_of(size):
            spot = jnp.where((lane + at == place) & (lane < n), 1.0, 0.0).astype(BF)
            lift = jnp.where(row == shard * 48 + top + i, 1.0, 0.0).astype(BF)
            block = block + mm(lift, mm(own, spot).astype(BF))
    return block.astype(BF)


def grad_in_kernel(pos, x, *refs):
    parts, (bq, bv, upb, outb, g1, s1, downb, g2, s2, keep, send) = refs[:-11], refs[-11:]
    j = pl.program_id(0)
    width = parts[0].shape[1] // 128
    half = len(parts) * width // 2
    base = keep.shape[4] - TINY
    for i, ref in enumerate(parts):

        @pl.when(j == i)
        def _(i=i, ref=ref):
            tile = dg(x[...], ref[...], TN).astype(BF)
            for n in range(width):
                at = i * width + n
                piece = tile[:, 128 * n : 128 * (n + 1)]
                scatter_tile(pos, piece, keep, send, at // half, 128 * (at % half), 48, ALL)

    @pl.when(j == 0)
    def _():
        vectors = (jnp.concatenate([bq[...], bv[...]], axis=1), upb[...])
        scatter_tile(pos, tiny_rows(vectors, FIELDS[0]), keep, send, 0, base, 48, ALL)

    @pl.when(j == len(parts) - 1)
    def _():
        vectors = [r[...] for r in (outb, g1, s1, downb, g2, s2)]
        scatter_tile(pos, tiny_rows(vectors, FIELDS[1]), keep, send, 1, base, 48, ALL)


def outputs_of(rows, width):
    shape = (2, 2, LINE, rows, width)
    return (
        [pl.BlockSpec(shape, lambda *a: (0, 0, 0, 0, 0))] * 2,
        [jax.ShapeDtypeStruct(shape, BF)] * 2,
    )


def grad_down(pos, act, low):
    tokens, hidden = act.shape
    model = low.shape[1]
    specs, shapes = outputs_of(hidden // 16, CW)
    return pl.pallas_call(
        grad_down_kernel,
        grid_spec=pltpu.PrefetchScalarGridSpec(
            num_scalar_prefetch=1,
            grid=(2, LINE),
            in_specs=[
                pl.BlockSpec((tokens, hidden // LINE), lambda j, i, p: (0, i)),
                pl.BlockSpec((tokens, CW), lambda j, i, p: (0, j)),
            ],
            out_specs=specs,
        ),
        out_shape=shapes,
        compiler_params=params(),
        cost_estimate=cost(13),
        name="grad_down",
    )(pos, act, low)


def joined(refs):
    return jnp.concatenate([r[...] for r in refs], axis=1)


def grad_up(pos, low, pre, att, first_low):
    tokens, model = low.shape
    hidden = pre.shape[1]
    ups = hidden // CW
    specs, shapes = outputs_of(48, CW + hidden // 2)
    full = pl.BlockSpec((tokens, model), lambda j, p: (0, 0))
    return pl.pallas_call(
        grad_up_kernel,
        grid_spec=pltpu.PrefetchScalarGridSpec(
            num_scalar_prefetch=1,
            grid=(ups + 2,),
            in_specs=[
                full,
                pl.BlockSpec((tokens, CW), lambda j, p: (0, jnp.minimum(j, ups - 1))),
            ]
            + [pl.BlockSpec(a.shape, lambda j, p: (0, 0)) for a in att]
            + [pl.BlockSpec((tokens, CW), lambda j, p: (0, jnp.maximum(j - ups, 0)))],
            out_specs=specs,
        ),
        out_shape=shapes,
        compiler_params=params(),
        cost_estimate=cost(16),
        name="grad_up",
    )(pos, low, pre, *att, first_low)


def grad_in(pos, x, parts, vectors):
    tokens, model = x.shape
    specs, shapes = outputs_of(48, 3 * CW + TINY)
    return pl.pallas_call(
        grad_in_kernel,
        grid_spec=pltpu.PrefetchScalarGridSpec(
            num_scalar_prefetch=1,
            grid=(len(parts),),
            in_specs=[pl.BlockSpec(a.shape, lambda j, p: (0, 0)) for a in (x, *parts, *vectors)],
            out_specs=specs,
        ),
        out_shape=shapes,
        compiler_params=params(),
        cost_estimate=cost(14),
        name="grad_in",
    )(pos, x, *parts, *vectors)


def halves(pos, mine, got):
    swap = pos[3] == 0
    return jnp.where(swap, mine, got).astype(F32), jnp.where(swap, got, mine).astype(F32)


def finish_down_kernel(pos, mine, got, down):
    for x, half in enumerate(halves(pos, mine[...], got[...])):
        down[:, CW * x : CW * (x + 1)] = half


def finish_up_kernel(pos, mine, got, out, up):
    width = up.shape[1] // 2
    for x, half in enumerate(halves(pos, mine[...], got[...])):
        out[:, CW * x : CW * (x + 1)] = half[:, :CW]
        up[:, width * x : width * (x + 1)] = half[:, CW:]


def finish_in_kernel(pos, mine, got, weight, *vectors):
    width = weight.shape[1] // 2
    for x, half in enumerate(halves(pos, mine[...], got[...])):
        weight[:, width * x : width * (x + 1)] = half[:, :width]
        for place, top, size in FIELDS[x]:
            for i, at, n in rows_of(size):
                vectors[place][:, at : at + n] = half[top + i : top + i + 1, width : width + n]


def finish(kernel, name, pos, mine, got, shapes):
    full = lambda shape: pl.BlockSpec(shape, lambda i, p: (0, 0))
    return pl.pallas_call(
        kernel,
        grid_spec=pltpu.PrefetchScalarGridSpec(
            num_scalar_prefetch=1,
            grid=(1,),
            in_specs=[full(mine.shape)] * 2,
            out_specs=[full(shape) for shape in shapes],
        ),
        out_shape=[jax.ShapeDtypeStruct(shape, F32) for shape in shapes],
        compiler_params=params(),
        name=name,
    )(pos, mine, got)


def qkv_rows(x, weight, bias, out):
    model = x.shape[1]
    y = mm(x[...], weight[...])
    scaled = (y[:, :model] + bias[:, :model]).astype(BF) * jnp.asarray(1.0 / math.sqrt(model // HEADS), BF)
    out[:, :model] = scaled
    out[:, model : 2 * model] = y[:, model : 2 * model].astype(BF)
    out[:, 2 * model :] = (y[:, 2 * model :] + bias[:, model:]).astype(BF)


def qkv_fetch_kernel(pos, x, *refs):
    buffers, out, vectors = refs[:8], refs[8], refs[9:17]
    weight, tiny, sem, sem_tiny = refs[17:]

    @pl.when(pl.program_id(0) == 0)
    def _():
        width = weight.shape[1] // 2
        copies = fetch(pos, buffers, weight, 48, 0, width, sem)
        small = fetch_tiny(pos, buffers, tiny, width, sem_tiny)
        for copy in small + copies:
            copy.start()
        for copy in small:
            copy.wait()
        unpack_vectors(tiny, vectors)
        for copy in copies:
            copy.wait()

    qkv_rows(x, weight, vectors[0], out)


def qkv_fetch(pos, x, buffers, shards, block=256):
    tokens, model = x.shape
    vec = lambda n: (pl.BlockSpec((1, n), lambda i, p: (0, 0)), jax.ShapeDtypeStruct((1, n), F32))
    vecs = [vec(model * n) for n in (2, 1, 1, 1, 4, 1, 1, 1)]
    return pl.pallas_call(
        qkv_fetch_kernel,
        grid_spec=pltpu.PrefetchScalarGridSpec(
            num_scalar_prefetch=1,
            grid=(tokens // block,),
            in_specs=[pl.BlockSpec((block, model), lambda i, p: (i, 0))]
            + [pl.BlockSpec(memory_space=pl.ANY)] * 8,
            out_specs=[pl.BlockSpec((block, 3 * model), lambda i, p: (i, 0))] + [v[0] for v in vecs],
            scratch_shapes=[
                pltpu.VMEM((model, 3 * model), BF),
                pltpu.VMEM((2, shards, 16, TINY), BF),
                pltpu.SemaphoreType.DMA,
                pltpu.SemaphoreType.DMA,
            ],
        ),
        out_shape=[jax.ShapeDtypeStruct((tokens, 3 * model), BF)] + [v[1] for v in vecs],
        compiler_params=params(),
        cost_estimate=cost(9),
        name="qkv_fetch",
    )(pos, x, *buffers)


def qkv(x, w, b, R=256):
    T, D = x.shape
    return pl.pallas_call(qkv_rows, grid=(T // R,),
      in_specs=[pl.BlockSpec((R, D), lambda i: (i, 0)), pl.BlockSpec(w.shape, lambda i: (0, 0)), pl.BlockSpec(b.shape, lambda i: (0, 0))],
      out_specs=pl.BlockSpec((R, w.shape[1]), lambda i: (i, 0)),
      out_shape=jax.ShapeDtypeStruct((T, w.shape[1]), BF), compiler_params=params())(x, w, b)


def aug(q,k,h,bias,lane):
    own=(lane>=64) if h else (lane<64)
    j0=0 if h else 64
    z=jnp.zeros_like(q)
    one=jnp.where(lane==j0,jnp.ones_like(q),z)
    qa=jnp.where(own,q,one)
    ka=jnp.where(own,k,jnp.where(lane==j0,bias,z))
    return qa,ka,own
def attn_fwd_kernel(cnt,q_ref,k_ref,v_ref,o_ref,l_ref):
    p=pl.program_id(0)
    q=q_ref[...];k=k_ref[...];v=v_ref[...]
    S=q.shape[0]
    lane=lax.broadcasted_iota(jnp.int32,q.shape,1)
    row=lax.broadcasted_iota(jnp.int32,q.shape,0)
    bias=jnp.where(row<cnt[p],0.0,-1e30).astype(BF)
    vt=v.T
    outs=[]
    for h in range(2):
        qa,ka,own=aug(q,k,h,bias,lane)
        s=dg(ka,qa,NT)
        m=jnp.max(s,axis=0,keepdims=True)
        e=jnp.exp(s-m)
        l=jnp.sum(e,axis=0,keepdims=True)
        ot=mm(vt[64*h:64*h+64],e.astype(BF))
        outs.append(ot*(1.0/l))
        l_ref[0,0,h:h+1,:]=m+jnp.log(l)
    o_ref[...]=jnp.concatenate(outs,axis=0).T.astype(BF)
def attn_fwd(rows, counts, pages, at, pairs):
    tokens, width = rows.shape
    length, every = tokens // pages, width // 3 // 128
    block = lambda o: pl.BlockSpec((length, 128), lambda p, h, c: (p, h + o + at))
    return pl.pallas_call(
        attn_fwd_kernel,
        grid_spec=pltpu.PrefetchScalarGridSpec(
            num_scalar_prefetch=1,
            grid=(pages, pairs),
            in_specs=[block(0), block(every), block(2 * every)],
            out_specs=[
                pl.BlockSpec((length, 128), lambda p, h, c: (p, h)),
                pl.BlockSpec((1, 1, 2, length), lambda p, h, c: (p, h, 0, 0)),
            ],
        ),
        out_shape=[
            jax.ShapeDtypeStruct((tokens, pairs * 128), BF),
            jax.ShapeDtypeStruct((pages, pairs, 2, length), F32),
        ],
        compiler_params=params(),
        cost_estimate=cost(3 * pairs),
        name="attn_fwd",
    )(counts, rows, rows, rows)


def attn_bwd_kernel(cnt,q_ref,k_ref,v_ref,g_ref,o_ref,l_ref,dq_ref,dk_ref,dv_ref,bq_ref,bv_ref):
    p=pl.program_id(1)
    q=q_ref[...];k=k_ref[...];v=v_ref[...];g=g_ref[...]
    lane=lax.broadcasted_iota(jnp.int32,q.shape,1)
    row=lax.broadcasted_iota(jnp.int32,q.shape,0)
    bias=jnp.where(row<cnt[p],0.0,-1e30).astype(BF)
    prod=g.astype(F32)*o_ref[...].astype(F32)
    hi=prod.astype(BF); lo=(prod-hi.astype(F32)).astype(BF)
    r8=lax.broadcasted_iota(jnp.int32,(16,128),0); l8=lax.broadcasted_iota(jnp.int32,(16,128),1)
    sel=jnp.where(r8==l8//64,1.0,0.0).astype(BF)
    delta=dg(sel,hi,NT)+dg(sel,lo,NT)
    kt=k.T
    dv=[];dk=[];dqt=[]
    for h in range(2):
        qa,ka,own=aug(q,k,h,bias,lane)
        s=dg(ka,qa,NT)
        pr=jnp.exp(s-l_ref[0,0,h:h+1,:])
        va=jnp.where(own,v,jnp.zeros_like(v))
        dp=dg(va,g,NT)
        ds=(pr*(dp-delta[h:h+1])).astype(BF)
        dv.append(mm(pr.astype(BF),g)); dk.append(mm(ds,q))
        dqt.append(mm(kt[64*h:64*h+64],ds))
    first=lane<64
    dvv=jnp.where(first,dv[0],dv[1])
    dq=jnp.concatenate(dqt,axis=0).T*0.125
    dq_ref[...]=dq.astype(BF); dv_ref[...]=dvv.astype(BF)
    dk_ref[...]=jnp.where(first,dk[0],dk[1]).astype(BF)
    sq=jnp.sum(dq,axis=0,keepdims=True); sv=jnp.sum(dvv,axis=0,keepdims=True)
    @pl.when(p==0)
    def _():
        bq_ref[...]=sq; bv_ref[...]=sv
    @pl.when(p>0)
    def _():
        bq_ref[...]+=sq; bv_ref[...]+=sv
def attn_bwd(rows, counts, grad, out, totals, pages, at, pairs):
    tokens, width = rows.shape
    length, every = tokens // pages, width // 3 // 128
    block = lambda o: pl.BlockSpec((length, 128), lambda h, p, c: (p, h + o))
    line = pl.BlockSpec((1, 128), lambda h, p, c: (0, h))
    return pl.pallas_call(
        attn_bwd_kernel,
        grid_spec=pltpu.PrefetchScalarGridSpec(
            num_scalar_prefetch=1,
            grid=(pairs, pages),
            in_specs=[block(at), block(every + at), block(2 * every + at), block(at), block(0)]
            + [pl.BlockSpec((1, 1, 2, length), lambda h, p, c: (p, h, 0, 0))],
            out_specs=[block(0)] * 3 + [line] * 2,
        ),
        out_shape=[jax.ShapeDtypeStruct((tokens, pairs * 128), BF)] * 3
        + [jax.ShapeDtypeStruct((1, pairs * 128), F32)] * 2,
        compiler_params=params(),
        cost_estimate=cost(4 * pairs),
        name="attn_bwd",
    )(counts, rows, rows, rows, grad, out, totals)


def norm(t):
    m=jnp.mean(t,axis=-1,keepdims=True); c=t-m
    v=jnp.mean(c*c,axis=-1,keepdims=True); inv=lax.rsqrt(v+1e-12)
    return c*inv,inv
def norm_back(e,hat,inv):
    return inv*(e-jnp.mean(e,axis=-1,keepdims=True)-hat*jnp.mean(e*hat,axis=-1,keepdims=True))
def col(t): return jnp.sum(t,axis=0,keepdims=True)
C=512
def main_fetch_kernel(pos, *refs):
    att, (x, cot), refs = refs[:-45], refs[-45:-43], refs[-43:]
    two, three, rest = refs[:8], refs[8:16], refs[16:]
    vecs, outs, scratch = rest[:7], rest[7:22], rest[22:]
    slope, ow, uw, dw, sem = scratch

    @pl.when(pl.program_id(0) == 0)
    def _():
        run_all(
            fetch(pos, two, ow, 48, 0, ow.shape[1] // 2, sem)
            + fetch(pos, two, uw, 48, ow.shape[1] // 2, uw.shape[1] // 2, sem)
            + fetch(pos, three, dw, dw.shape[0] // 16, 0, dw.shape[1] // 2, sem)
        )

    main_kernel(att, x, cot, ow, uw, dw, *vecs, *outs, slope)


def main_plain_kernel(*refs):
    main_kernel(refs[:-28], *refs[-28:])


def main_kernel(att,x,cot,ow,uw,dw,ob,g1,s1,ub,db,g2,s2,
                lo_ref,act_ref,sl_ref,nl_ref,pl_ref,fl_ref,gf_ref,ga_ref,
                vg2,vs2,vdb,vub,vg1,vs1,vob,slope):
    i=pl.program_id(0)
    FF=uw.shape[1]
    fs=x[...].astype(F32)+mm(joined(att),ow[...])+ob[...]
    fh,fi=norm(fs)
    normed=fh*g1[...]+s1[...]
    nl=normed.astype(BF); nl_ref[...]=nl
    acc=normed+db[...]
    for j in range(0,FF,C):
        pre=mm(nl,uw[:,j:j+C])+ub[:,j:j+C]
        phi=0.5*(1.0+lax.erf(pre*(1.0/math.sqrt(2.0))))
        a=(pre*phi).astype(BF)
        act_ref[:,j:j+C]=a
        slope[:,j:j+C]=phi+pre*jnp.exp(-0.5*pre*pre)*(1.0/math.sqrt(2.0*math.pi))
        acc=acc+mm(a,dw[j:j+C,:])
    sh,si=norm(acc)
    lo_ref[...]=(sh*g2[...]+s2[...]).astype(BF)
    gr=cot[...].astype(F32)
    gs=norm_back(gr*g2[...],sh,si)
    sl=gs.astype(BF); sl_ref[...]=sl
    gn=gs
    ubs=[]
    for j in range(0,FF,C):
        gp=dg(sl,dw[j:j+C,:],NT)*slope[:,j:j+C]
        ubs.append(col(gp))
        gpl=gp.astype(BF); pl_ref[:,j:j+C]=gpl
        gn=gn+dg(gpl,uw[:,j:j+C],NT)
    gf=norm_back(gn*g1[...],fh,fi)
    fl=gf.astype(BF); fl_ref[...]=fl; gf_ref[...]=gf
    ga_ref[...]=dg(fl,ow[...],NT).astype(BF)
    vals=[(vg2,col(gr*sh)),(vs2,col(gr)),(vdb,col(gs)),(vub,jnp.concatenate(ubs,1)),(vg1,col(gn*fh)),(vs1,col(gn)),(vob,col(gf))]
    @pl.when(i==0)
    def _():
        for r,v in vals: r[...]=v
    @pl.when(i>0)
    def _():
        for r,v in vals: r[...]+=v
def main(att, x, cot, weights, vecs, pos=None, R=256):
    T, D = x.shape
    FF = vecs[3].shape[1]
    rb = lambda n: pl.BlockSpec((R, n), lambda i, *p: (i, 0))
    full = lambda a: pl.BlockSpec(a.shape, lambda i, *p: (0, 0))
    sds = lambda n, t=BF: jax.ShapeDtypeStruct((T, n), t)
    vec = lambda n: (pl.BlockSpec((1, n), lambda i, *p: (0, 0)), jax.ShapeDtypeStruct((1, n), F32))
    vs = [vec(n) for n in (D, D, D, FF, D, D, D)]
    fetched = pos is not None
    scratch = [pltpu.VMEM((R, FF), F32)]
    if fetched:
        scratch += [pltpu.VMEM((D, D), BF), pltpu.VMEM((D, FF), BF), pltpu.VMEM((FF, D), BF), pltpu.SemaphoreType.DMA]
    return pl.pallas_call(
        main_fetch_kernel if fetched else main_plain_kernel,
        grid_spec=pltpu.PrefetchScalarGridSpec(
            num_scalar_prefetch=1 if fetched else 0,
            grid=(T // R,),
            in_specs=[rb(a.shape[1]) for a in (*att, x, cot)]
            + [pl.BlockSpec(memory_space=pl.ANY) if fetched else full(w) for w in weights]
            + [full(v) for v in vecs],
            out_specs=[rb(D), rb(FF), rb(D), rb(D), rb(FF), rb(D), rb(D), rb(D)] + [v[0] for v in vs],
            scratch_shapes=scratch,
        ),
        out_shape=[sds(D), sds(FF), sds(D), sds(D), sds(FF), sds(D), sds(D, F32), sds(D)] + [v[1] for v in vs],
        compiler_params=params(),
        cost_estimate=cost(45),
        name="main",
    )(*([pos] if fetched else []), *att, x, cot, *weights, *vecs)


def tn_kernel(a,b,o): o[...]=dg(a[...],b[...],TN).astype(BF)
def tn(a,b,bm,bn):
    T,M=a.shape;N=b.shape[1]
    return pl.pallas_call(tn_kernel,grid=(M//bm,N//bn),
      in_specs=[pl.BlockSpec((T,bm),lambda i,j:(0,i)),pl.BlockSpec((T,bn),lambda i,j:(0,j))],
      out_specs=pl.BlockSpec((bm,bn),lambda i,j:(i,j)),out_shape=jax.ShapeDtypeStruct((M,N),BF),compiler_params=params())(a,b)
def ig_kernel(gf, parts, w, o):
    o[...] = (gf[...] + dg(joined(parts), w[...], NT)).astype(BF)


def ig_plain_kernel(gf, *refs):
    ig_kernel(gf, refs[:-2], refs[-2], refs[-1])


def ig_fetch_kernel(pos, gf, *refs):
    parts, buffers, (o, weight, sem) = refs[:-11], refs[-11:-3], refs[-3:]

    @pl.when(pl.program_id(0) == 0)
    def _():
        run_all(fetch(pos, buffers, weight, 48, 0, weight.shape[1] // 2, sem))

    ig_kernel(gf, parts, weight, o)


def ig(parts, gf, weights, pos=None, R=256):
    T, D = gf.shape
    rb = lambda n: pl.BlockSpec((R, n), lambda i, *p: (i, 0))
    fetched = pos is not None
    return pl.pallas_call(
        ig_fetch_kernel if fetched else ig_plain_kernel,
        grid_spec=pltpu.PrefetchScalarGridSpec(
            num_scalar_prefetch=1 if fetched else 0,
            grid=(T // R,),
            in_specs=[rb(a.shape[1]) for a in (gf, *parts)]
            + [pl.BlockSpec(memory_space=pl.ANY) if fetched else pl.BlockSpec(w.shape, lambda i, *p: (0, 0)) for w in weights],
            out_specs=rb(D),
            scratch_shapes=[pltpu.VMEM((D, 3 * D), BF), pltpu.SemaphoreType.DMA] if fetched else [],
        ),
        out_shape=jax.ShapeDtypeStruct((T, D), BF),
        compiler_params=params(),
        cost_estimate=cost(10),
        name="ig",
    )(*([pos] if fetched else []), gf, *parts, *weights)


def local(
    hidden_states,
    page_counts,
    cotangent,
    attn_in_weight,
    attn_in_bias,
    attn_out_weight,
    attn_out_bias,
    first_gain,
    first_shift,
    up_weight,
    up_bias,
    down_weight,
    down_bias,
    second_gain,
    second_shift,
):
    pages, length, model = hidden_states.shape
    hidden = up_weight.shape[1]
    x = hidden_states.reshape(-1, model)
    grad_rows = cotangent.reshape(-1, model)
    weights = (attn_in_weight, attn_out_weight, up_weight, down_weight)
    vectors = (
        attn_in_bias,
        attn_out_bias,
        first_gain,
        first_shift,
        up_bias,
        down_bias,
        second_gain,
        second_shift,
    )
    lined = lax.axis_size("fsdp") == 4 * LINE and lax.axis_size("rep") == 2
    pairs = HEADS // 2 // THIRDS
    starts = [pairs * t for t in range(THIRDS)]
    forward = [None] * THIRDS
    backward = [None] * THIRDS

    def ahead(t, rows):
        forward[t] = attn_fwd(rows, page_counts, pages, starts[t], pairs)

    def back(t, rows):
        backward[t] = attn_bwd(rows, page_counts, grad_att, *forward[t], pages, starts[t], pairs)

    if lined:
        index = lax.axis_index("fsdp")
        pos = jnp.stack([index // 4, index // 2 % 2, index % 2, lax.axis_index("rep")]).astype(jnp.int32)
        one, two, three = pack(pos, weights, vectors)
        line_one = jnp.stack(along_line(one))
        parts_two = along_line(two)
        second_one = move(line_one, to_second)
        first_one = move(line_one, to_first)
        both_one = move(second_one, to_first)
        in_w = over_core((line_one, first_one, second_one, both_one))
        line_two = jnp.stack(after(parts_two, first_one))
        parts_three = along_line(three)
        second_two = move(line_two, to_second)
        first_two = move(line_two, to_first)
        rows, *full = qkv_fetch(pos, x, after(in_w, line_two), 16)
        ahead(0, rows)
        ahead(1, after(rows, forward[0]))
        both_two = move(after(second_two, forward[1]), to_first)
        line_three = jnp.stack(after(parts_three, forward[1]))
        second_three = move(line_three, to_second)
        first_three = move(line_three, to_first)
        ahead(2, after(rows, second_two, line_three))
        both_three = move(after(second_three, forward[2]), to_first)
        later = over_core((line_two, first_two, second_two, both_two))
        later += over_core((line_three, first_three, second_three, both_three))
    else:
        pos = None
        whole = lambda a: lax.all_gather(a, "fsdp", axis=0, tiled=True)
        in_w = (whole(attn_in_weight),)
        full = [whole(v).astype(F32).reshape(1, -1) for v in vectors]
        later = tuple(whole(w) for w in weights[1:])
        rows = qkv(x, in_w[0], full[0])
        for t in range(THIRDS):
            ahead(t, rows)
    attended = [f[0] for f in forward]
    (
        output, act, second_low, normed_low, pre_low, first_low, grad_first, grad_att,
        vg2, vs2, vdb, vub, vg1, vs1, vob,
    ) = main(attended, x, grad_rows, later, full[1:], pos)
    if lined:
        keep_d, send_d = grad_down(pos, act, second_low)
        core_d = move(send_d, to_core)
        keep_u, send_u = grad_up(pos, *after((normed_low, pre_low), keep_d), attended, first_low)
        go_d, stay_d = add_core(keep_d, core_d)
        core_u = move(send_u, to_core)
        first_d = move(go_d, to_first)
        back(0, after(rows, go_d, stay_d, keep_u))
        go_u, stay_u = add_core(*after((keep_u, core_u), backward[0]))
        first_u = move(go_u, to_first)
        back(1, after(rows, go_u, stay_u))
        go_d, stay_d = add_core(*after((stay_d, first_d), backward[1]))
        second_d = move(go_d, to_second)
        back(2, after(rows, go_d, stay_d))
    else:
        for t in range(THIRDS):
            back(t, rows)
    parts = tuple(b[n] for n in range(3) for b in backward)
    vbq = jnp.concatenate([b[3] for b in backward], axis=1)
    vbv = jnp.concatenate([b[4] for b in backward], axis=1)
    if lined:
        low_d = add_last(*after((stay_d, second_d), backward[2]))
        line_d = move_line(low_d)
        keep_i, send_i = grad_in(
            pos, x, after(parts, low_d), (vbq, vbv, vub, vob, vg1, vs1, vdb, vg2, vs2)
        )
        core_i = move(send_i, to_core)
        go_u, stay_u = add_core(*after((stay_u, first_u), keep_i))
        second_u = move(go_u, to_second)
        go_i, stay_i = add_core(keep_i, after(core_i, go_u))
        first_i = move(go_i, to_first)
        input_grad = ig(parts, after(grad_first, go_i, stay_i), in_w, pos)
        mine_d = add_line(low_d, after(line_d, input_grad))
        got_d = move(mine_d, to_x)
        low_u = add_last(*after((stay_u, second_u), mine_d))
        line_u = move_line(low_u)
        go_i, stay_i = add_core(*after((stay_i, first_i), low_u))
        second_i = move(go_i, to_second)
        mine_u = add_line(low_u, after(line_u, go_i))
        got_u = move(mine_u, to_x)
        (t_down,) = finish(
            finish_down_kernel, "finish_down", pos, mine_d, after(got_d, mine_u), [down_weight.shape]
        )
        low_i = add_last(*after((stay_i, second_i), t_down))
        line_i = move_line(low_i)
        t_out, t_up = finish(
            finish_up_kernel, "finish_up", pos, mine_u, after(got_u, low_i),
            [attn_out_weight.shape, up_weight.shape],
        )
        mine_i = add_line(low_i, after(line_i, t_up))
        got_i = move(mine_i, to_x)
        shapes = [attn_in_weight.shape] + [(1, v.shape[0]) for v in vectors]
        t_in, *small = finish(finish_in_kernel, "finish_in", pos, mine_i, got_i, shapes)
        small = [b.reshape(-1) for b in small]
    else:
        input_grad = ig(parts, grad_first, in_w)

        def total(a):
            share = lax.psum_scatter(a.astype(BF), "fsdp", scatter_dimension=0, tiled=True)
            return lax.psum(share, "rep").astype(F32)

        att = jnp.concatenate(attended, axis=1)
        t_down = total(tn(act, second_low, 768, 768))
        t_up = total(tn(normed_low, pre_low, 768, 768))
        t_out = total(tn(att, first_low, 768, 768))
        t_in = total(jnp.concatenate([tn(x, d, 768, 256) for d in parts], axis=1))
        small = [
            total(v.reshape(-1))
            for v in (jnp.concatenate([vbq, vbv], axis=1), vob, vg1, vs1, vub, vdb, vg2, vs2)
        ]
    b_in, b_out, b_g1, b_s1, b_up, b_down, b_g2, b_s2 = small
    return (
        output.reshape(hidden_states.shape),
        input_grad.reshape(hidden_states.shape),
        t_in, b_in, t_out, b_out, b_g1, b_s1, t_up, b_up, t_down, b_down, b_g2, b_s2,
    )


def solution(mesh):
    return jax.shard_map(
        local,
        mesh=mesh,
        in_specs=(
            P(("fsdp", "rep"), None, None),
            P(("fsdp", "rep")),
            P(("fsdp", "rep"), None, None),
            P("fsdp", None),
            P("fsdp"),
            P("fsdp", None),
            P("fsdp"),
            P("fsdp"),
            P("fsdp"),
            P("fsdp", None),
            P("fsdp"),
            P("fsdp", None),
            P("fsdp"),
            P("fsdp"),
            P("fsdp"),
        ),
        out_specs=(
            P(("fsdp", "rep"), None, None),
            P(("fsdp", "rep"), None, None),
            P("fsdp", None),
            P("fsdp"),
            P("fsdp", None),
            P("fsdp"),
            P("fsdp"),
            P("fsdp"),
            P("fsdp", None),
            P("fsdp"),
            P("fsdp", None),
            P("fsdp"),
            P("fsdp"),
            P("fsdp"),
        ),
        check_vma=False,
    )
```

```python
import math

import jax
import jax.numpy as jnp
from jax import lax
from jax.experimental import pallas as pl
from jax.experimental.pallas import tpu as pltpu
from jax.sharding import PartitionSpec as P

HEADS = 12
BF = jnp.bfloat16
F32 = jnp.float32
NT = (((1,), (1,)), ((), ()))
TN = (((0,), (0,)), ((), ()))
CW = 384
THIRDS = 3
LINE = 4
TINY = 128
AXES = ("fsdp", "rep")


def dg(a, b, dims):
    return lax.dot_general(a, b, dims, preferred_element_type=F32)


def mm(a, b):
    return jnp.dot(a, b, preferred_element_type=F32)


def params():
    return pltpu.CompilerParams(vmem_limit_bytes=60 * 1024 * 1024)


def cost(us):
    return pl.CostEstimate(flops=int(us * 1.15e9), bytes_accessed=int(us * 1e6), transcendentals=0)


def flat_index(z, y, c, x):
    return (z * 4 + y * 2 + c) * 2 + x


def permutation(target):
    pairs = []
    for z in range(LINE):
        for y in range(2):
            for c in range(2):
                for x in range(2):
                    pairs.append((flat_index(z, y, c, x), flat_index(*target(z, y, c, x))))
    return pairs


def to_core(z, y, c, x):
    return (z, y, 1 - c, x)


def to_x(z, y, c, x):
    return (z, y, c, 1 - x)


def to_first(z, y, c, x):
    return (z, y, c, 1 - x) if c == 0 else (z, 1 - y, c, x)


def to_second(z, y, c, x):
    return (z, 1 - y, c, x) if c == 0 else (z, y, c, 1 - x)


def to_line(step):
    return lambda z, y, c, x: ((z + step) % LINE, y, c, x)


def move(value, target):
    return lax.ppermute(value, AXES, permutation(target))


def after(values, *earlier):
    return lax.optimization_barrier((values, earlier))[0]


def along_line(half):
    return [half] + [move(half, to_line(k)) for k in range(1, LINE)]


def over_core(parts):
    return tuple(parts) + tuple(move(part, to_core) for part in parts)


def add_core(keep, got):
    keep, got = keep.astype(F32), got.astype(F32)
    return (keep[1] + got[1]).astype(BF), (keep[0] + got[0]).astype(BF)


def add_last(stay, got):
    return (stay.astype(F32) + got.astype(F32)).astype(BF)


def add_line(low, parts):
    total = low[0].astype(F32)
    for part in parts:
        total = total + part.astype(F32)
    return total.astype(BF)


def move_line(low):
    return [move(low[k], to_line(k)) for k in range(1, LINE)]


FIELDS = (((0, 0, 96), (4, 1, 192)), tuple((n, i, 48) for i, n in enumerate((1, 2, 3, 5, 6, 7))))


def rows_of(width):
    return [(i, at, min(TINY, width - at)) for i, at in enumerate(range(0, width, TINY))]


def pack_kernel(pos, inw, outw, upw, downw, *refs):
    vectors, (one, two, three) = refs[:8], refs[8:]

    def fill(x):
        third = inw.shape[1] // 3
        for t in range(THIRDS):
            for part in range(3):
                start = part * third + (2 * t + x) * 128
                piece = inw[:, start : start + 128]
                one[:, t * CW + part * 128 : t * CW + (part + 1) * 128] = piece
        row = lax.broadcasted_iota(jnp.int32, (48, TINY), 0)
        block = jnp.zeros((48, TINY), F32)
        for place, top, size in FIELDS[x]:
            for i, at, n in rows_of(size):
                piece = vectors[place][:, at : at + n].astype(F32)
                if n < TINY:
                    piece = jnp.concatenate([piece, jnp.zeros((1, TINY - n), F32)], axis=1)
                block = jnp.where(row == top + i, jnp.broadcast_to(piece, (48, TINY)), block)
        one[:, THIRDS * CW :] = block.astype(BF)
        two[:, :CW] = outw[:, x * CW : (x + 1) * CW]
        width = upw.shape[1] // 2
        two[:, CW:] = upw[:, x * width : (x + 1) * width]
        three[...] = downw[:, x * CW : (x + 1) * CW]

    @pl.when(pos[3] == 0)
    def _():
        fill(0)

    @pl.when(pos[3] == 1)
    def _():
        fill(1)


def pack(pos, weights, vectors):
    shapes = [
        (48, weights[0].shape[1] // 2 + TINY),
        (48, weights[1].shape[1] // 2 + weights[2].shape[1] // 2),
        (weights[3].shape[0], CW),
    ]
    arrays = tuple(weights) + tuple(v.reshape(1, -1) for v in vectors)
    full = lambda a: pl.BlockSpec(a, lambda i, p: (0, 0))
    return pl.pallas_call(
        pack_kernel,
        grid_spec=pltpu.PrefetchScalarGridSpec(
            num_scalar_prefetch=1,
            grid=(1,),
            in_specs=[full(a.shape) for a in arrays],
            out_specs=[full(a) for a in shapes],
        ),
        out_shape=[jax.ShapeDtypeStruct(a, BF) for a in shapes],
        compiler_params=params(),
        name="pack",
    )(pos, *arrays)


def sources(pos):
    z, y, c, x = pos[0], pos[1], pos[2], pos[3]
    found = []
    for other in range(2):
        core = c ^ 1 if other else c
        swap = core == 0
        for first in range(2):
            for second in range(2):
                dx = jnp.where(swap, first, second)
                dy = jnp.where(swap, second, first)
                buffer = other * 4 + second * 2 + first
                for k in range(LINE):
                    shard = ((z - k) & (LINE - 1)) * 4 + (y ^ dy) * 2 + core
                    found.append((buffer, k, shard, x ^ dx))
    return found


def fetch(pos, buffers, target, rows, column, width, sem, stride=None, start=0):
    stride = width if stride is None else stride
    return [
        pltpu.make_async_copy(
            buffers[buffer].at[k, :, pl.ds(column, width)],
            target.at[
                pl.ds(pl.multiple_of(shard * rows, 16), rows),
                pl.ds(pl.multiple_of(start + x * stride, 128), width),
            ],
            sem,
        )
        for buffer, k, shard, x in sources(pos)
    ]


def fetch_in(pos, buffers, target, sem):
    copies = []
    for t in range(THIRDS):
        copies += fetch(pos, buffers, target, 48, t * CW, CW, sem, None, 2 * CW * t)
    return copies


def fetch_tiny(pos, buffers, target, column, sem):
    return [
        pltpu.make_async_copy(
            buffers[buffer].at[k, pl.ds(0, 16), pl.ds(column, TINY)], target.at[x, shard], sem
        )
        for buffer, k, shard, x in sources(pos)
    ]


def run_all(copies):
    for copy in copies:
        copy.start()
    for copy in copies:
        copy.wait()


def unpack_vectors(tiny, targets):
    shards = tiny.shape[1]
    for half in range(2):
        for place, top, size in FIELDS[half]:
            total = shards * size
            tiled = jnp.zeros((shards, total), F32)
            for i, at, n in rows_of(size):
                lane = lax.broadcasted_iota(jnp.int32, (TINY, total), 0)
                spot = lax.broadcasted_iota(jnp.int32, (TINY, total), 1) % size
                spot = jnp.where((lane + at == spot) & (lane < n), 1.0, 0.0).astype(BF)
                tiled = tiled + mm(tiny[half, :, top + i, :], spot)
            owner = lax.broadcasted_iota(jnp.int32, (shards, total), 0)
            place_of = lax.broadcasted_iota(jnp.int32, (shards, total), 1) // size
            targets[place][...] = jnp.sum(jnp.where(place_of == owner, tiled, 0.0), axis=0, keepdims=True)


def place_tile(pos, held, keep, send, rows, line):
    z, y, c, x = pos[0], pos[1], pos[2], pos[3]
    for relative, out in enumerate((keep, send)):
        core = c ^ relative
        swap = core == 0
        for first in range(2):
            for second in range(2):
                dx = jnp.where(swap, first, second)
                dy = jnp.where(swap, second, first)
                for slot, chip in line:
                    shard = chip * 4 + (y ^ dy) * 2 + core
                    start = pl.multiple_of(shard * rows, 16)
                    out[first, second, slot] = held[x ^ dx, pl.ds(start, rows), :]


def whole_line(pos):
    return [(k, (pos[0] + k) & (LINE - 1)) for k in range(LINE)]


def hold(held, tile):
    width = tile.shape[1] // 2
    held[0] = tile[:, :width].astype(BF)
    held[1] = tile[:, width:].astype(BF)


def grad_down_kernel(pos, act, low, keep, send, held):
    hold(held, dg(act[...], low[...], TN))
    place_tile(pos, held, keep, send, held.shape[1] // 4, [(0, 0)])


def joined(refs):
    return jnp.concatenate([r[...] for r in refs], axis=1)


def grad_up_kernel(pos, low, pre_left, pre_right, first_low, *refs):
    att, (keep, send, held) = refs[:-3], refs[-3:]
    j = pl.program_id(0)

    @pl.when(j == 0)
    def _():
        hold(held, dg(joined(att), first_low[...], TN))

    @pl.when(j > 0)
    def _():
        held[0] = dg(low[...], pre_left[...], TN).astype(BF)
        held[1] = dg(low[...], pre_right[...], TN).astype(BF)

    place_tile(pos, held, keep, send, 48, whole_line(pos))


def tiny_rows(vectors, fields):
    block = jnp.zeros((16 * 48, TINY), F32)
    row = lax.broadcasted_iota(jnp.int32, (16 * 48, 16), 0)
    shard = lax.broadcasted_iota(jnp.int32, (16 * 48, 16), 1)
    for vector, (_, top, size) in zip(vectors, fields):
        length = vector.shape[1]
        owner = lax.broadcasted_iota(jnp.int32, (16, length), 0)
        place = lax.broadcasted_iota(jnp.int32, (16, length), 1)
        own = jnp.where(place // size == owner, jnp.broadcast_to(vector, (16, length)), 0.0).astype(BF)
        place = lax.broadcasted_iota(jnp.int32, (length, TINY), 0) % size
        lane = lax.broadcasted_iota(jnp.int32, (length, TINY), 1)
        for i, at, n in rows_of(size):
            spot = jnp.where((lane + at == place) & (lane < n), 1.0, 0.0).astype(BF)
            lift = jnp.where(row == shard * 48 + top + i, 1.0, 0.0).astype(BF)
            block = block + mm(lift, mm(own, spot).astype(BF))
    return block.astype(BF)


def grad_in_kernel(pos, x, *refs):
    parts, (keep, send, held) = refs[:-3], refs[-3:]
    for i, ref in enumerate(parts):

        @pl.when(pl.program_id(0) == i)
        def _(ref=ref):
            hold(held, dg(x[...], ref[...], TN))

    place_tile(pos, held, keep, send, 48, whole_line(pos))


def grad_last_kernel(pos, x, part, bq, bv, upb, outb, g1, s1, downb, g2, s2, keep, send, held):
    hold(held, dg(x[...], part[...], TN))
    take = lambda ref: ref.at[:, :, :, :, pl.ds(0, CW)]
    place_tile(pos, held, take(keep), take(send), 48, whole_line(pos))
    groups = ((jnp.concatenate([bq[...], bv[...]], axis=1), upb[...]), [r[...] for r in (outb, g1, s1, downb, g2, s2)])
    for half in range(2):
        held[half, :, :TINY] = tiny_rows(groups[half], FIELDS[half])
    take = lambda ref: ref.at[:, :, :, :, pl.ds(CW, TINY)]
    place_tile(pos, held.at[:, :, pl.ds(0, TINY)], take(keep), take(send), 48, whole_line(pos))


def grad_call(kernel, name, pos, arrays, in_specs, grid, block, shape, index, us):
    held = (2, 16 * 48, CW)
    return pl.pallas_call(
        kernel,
        grid_spec=pltpu.PrefetchScalarGridSpec(
            num_scalar_prefetch=1,
            grid=(grid,),
            in_specs=in_specs,
            out_specs=[pl.BlockSpec(block, index)] * 2,
            scratch_shapes=[pltpu.VMEM(held, BF)],
        ),
        out_shape=[jax.ShapeDtypeStruct(shape, BF)] * 2,
        compiler_params=params(),
        cost_estimate=cost(us),
        name=name,
    )(pos, *arrays)


def whole(array):
    return pl.BlockSpec(array.shape, lambda j, p: (0,) * array.ndim)


def grad_down(pos, act, low):
    tokens, hidden = act.shape
    rows = hidden // 16
    specs = [pl.BlockSpec((tokens, hidden // LINE), lambda j, p: (0, (j + p[0]) & (LINE - 1))), whole(low)]
    return grad_call(
        grad_down_kernel, "grad_down", pos, (act, low), specs, LINE,
        (2, 2, 1, rows, CW), (2, 2, LINE, rows, CW), lambda j, p: (0, 0, j, 0, 0), 9,
    )


def grad_up(pos, low, pre, att, first_low):
    tokens, hidden = pre.shape
    ups = hidden // 2 // CW
    specs = [
        whole(low),
        pl.BlockSpec((tokens, CW), lambda j, p: (0, jnp.maximum(j - 1, 0))),
        pl.BlockSpec((tokens, CW), lambda j, p: (0, ups + jnp.maximum(j - 1, 0))),
        whole(first_low),
    ] + [whole(a) for a in att]
    return grad_call(
        grad_up_kernel, "grad_up", pos, (low, pre, pre, first_low, *att), specs, 1 + ups,
        (2, 2, LINE, 48, CW), (2, 2, LINE, 48, CW * (1 + ups)), lambda j, p: (0, 0, 0, 0, j), 10,
    )


def grad_in(pos, x, parts):
    return grad_call(
        grad_in_kernel, "grad_in", pos, (x, *parts), [whole(a) for a in (x, *parts)], len(parts),
        (2, 2, LINE, 48, CW), (2, 2, LINE, 48, CW * len(parts)), lambda j, p: (0, 0, 0, 0, j), 5,
    )


def grad_last(pos, x, part, vectors):
    arrays = (x, part, *vectors)
    shape = (2, 2, LINE, 48, CW + TINY)
    return grad_call(
        grad_last_kernel, "grad_last", pos, arrays, [whole(a) for a in arrays], 1,
        shape, shape, lambda j, p: (0, 0, 0, 0, 0), 4,
    )


def halves(pos, mine, got):
    swap = pos[3] == 0
    return jnp.where(swap, mine, got).astype(F32), jnp.where(swap, got, mine).astype(F32)


def finish_down_kernel(pos, mine, got, down):
    for x, half in enumerate(halves(pos, mine[...], got[...])):
        down[:, CW * x : CW * (x + 1)] = half


def finish_up_kernel(pos, mine, got, out, up):
    width = up.shape[1] // 2
    for x, half in enumerate(halves(pos, mine[...], got[...])):
        out[:, CW * x : CW * (x + 1)] = half[:, :CW]
        up[:, width * x : width * (x + 1)] = half[:, CW:]


def finish_in_kernel(pos, mine, got, mine_last, got_last, weight, *vectors):
    third = weight.shape[1] // 3
    more = halves(pos, mine[...], got[...])
    for x, last in enumerate(halves(pos, mine_last[...], got_last[...])):
        for t in range(THIRDS):
            for part in range(3):
                start = part * third + (2 * t + x) * 128
                if t < THIRDS - 1:
                    piece = more[x][:, t * CW + part * 128 : t * CW + (part + 1) * 128]
                else:
                    piece = last[:, part * 128 : (part + 1) * 128]
                weight[:, start : start + 128] = piece
        for place, top, size in FIELDS[x]:
            for i, at, n in rows_of(size):
                vectors[place][:, at : at + n] = last[top + i : top + i + 1, CW : CW + n]


def finish(kernel, name, pos, sums, shapes):
    full = lambda shape: pl.BlockSpec(shape, lambda i, p: (0, 0))
    return pl.pallas_call(
        kernel,
        grid_spec=pltpu.PrefetchScalarGridSpec(
            num_scalar_prefetch=1,
            grid=(1,),
            in_specs=[full(a.shape) for a in sums],
            out_specs=[full(shape) for shape in shapes],
        ),
        out_shape=[jax.ShapeDtypeStruct(shape, F32) for shape in shapes],
        compiler_params=params(),
        name=name,
    )(pos, *sums)


def pair_bias(bias):
    model = bias.shape[1] // 2
    parts = []
    for pair in range(model // 128):
        at = pair * 128
        parts += [bias[:, at : at + 128], jnp.zeros((1, 128), F32), bias[:, model + at : model + at + 128]]
    return jnp.concatenate(parts, axis=1)


def qkv_rows(x, weight, bias, outs):
    y = mm(x[...], weight[...])
    scale = 1.0 / math.sqrt(x.shape[1] // HEADS)
    for t, out in enumerate(outs):
        width = out.shape[1]
        for at in range(0, width, 128):
            here = y[:, t * width + at : t * width + at + 128]
            place = t * width + at
            if at // 128 % 3 != 1:
                here = here + bias[:, place : place + 128]
            here = here.astype(BF)
            out[:, at : at + 128] = here * jnp.asarray(scale, BF) if at // 128 % 3 == 0 else here


def qkv_fetch_kernel(pos, x, *refs):
    buffers, outs, refs = refs[:8], refs[8 : 8 + THIRDS], refs[8 + THIRDS :]
    vectors, (weight, tiny, bias, sem, sem_tiny) = refs[:8], refs[8:]

    @pl.when(pl.program_id(0) == 0)
    def _():
        copies = fetch_in(pos, buffers, weight, sem)
        small = fetch_tiny(pos, buffers, tiny, THIRDS * CW, sem_tiny)
        for copy in small + copies:
            copy.start()
        for copy in small:
            copy.wait()
        unpack_vectors(tiny, vectors)
        bias[...] = pair_bias(vectors[0][...])
        for copy in copies:
            copy.wait()

    qkv_rows(x, weight, bias, outs)


def qkv_fetch(pos, x, buffers, shards, block=256):
    tokens, model = x.shape
    vec = lambda n: (pl.BlockSpec((1, n), lambda i, p: (0, 0)), jax.ShapeDtypeStruct((1, n), F32))
    vecs = [vec(model * n) for n in (2, 1, 1, 1, 4, 1, 1, 1)]
    return pl.pallas_call(
        qkv_fetch_kernel,
        grid_spec=pltpu.PrefetchScalarGridSpec(
            num_scalar_prefetch=1,
            grid=(tokens // block,),
            in_specs=[pl.BlockSpec((block, model), lambda i, p: (i, 0))]
            + [pl.BlockSpec(memory_space=pl.ANY)] * 8,
            out_specs=[pl.BlockSpec((block, 2 * CW), lambda i, p: (i, 0))] * THIRDS + [v[0] for v in vecs],
            scratch_shapes=[
                pltpu.VMEM((model, 3 * model), BF),
                pltpu.VMEM((2, shards, 16, TINY), BF),
                pltpu.VMEM((1, 3 * model), F32),
                pltpu.SemaphoreType.DMA,
                pltpu.SemaphoreType.DMA,
            ],
        ),
        out_shape=[jax.ShapeDtypeStruct((tokens, 2 * CW), BF)] * THIRDS + [v[1] for v in vecs],
        compiler_params=params(),
        cost_estimate=cost(10),
        name="qkv_fetch",
    )(pos, x, *buffers)


def qkv_plain_kernel(x, weight, bias, *outs):
    qkv_rows(x, weight, bias, outs)


def qkv(x, weight, bias, block=256):
    tokens, model = x.shape
    full = lambda a: pl.BlockSpec(a.shape, lambda i: (0, 0))
    return pl.pallas_call(
        qkv_plain_kernel,
        grid=(tokens // block,),
        in_specs=[pl.BlockSpec((block, model), lambda i: (i, 0)), full(weight), full(bias)],
        out_specs=[pl.BlockSpec((block, 2 * CW), lambda i: (i, 0))] * THIRDS,
        out_shape=[jax.ShapeDtypeStruct((tokens, 2 * CW), BF)] * THIRDS,
        compiler_params=params(),
    )(x, weight, bias)


def aug(q,k,h,bias,lane):
    own=(lane>=64) if h else (lane<64)
    j0=0 if h else 64
    z=jnp.zeros_like(q)
    one=jnp.where(lane==j0,jnp.ones_like(q),z)
    qa=jnp.where(own,q,one)
    ka=jnp.where(own,k,jnp.where(lane==j0,bias,z))
    return qa,ka,own
def attn_fwd_kernel(cnt,q_ref,k_ref,v_ref,o_ref,l_ref):
    p=pl.program_id(0)
    q=q_ref[...];k=k_ref[...];v=v_ref[...]
    S=q.shape[0]
    lane=lax.broadcasted_iota(jnp.int32,q.shape,1)
    row=lax.broadcasted_iota(jnp.int32,q.shape,0)
    bias=jnp.where(row<cnt[p],0.0,-1e30).astype(BF)
    vt=v.T
    outs=[]
    for h in range(2):
        qa,ka,own=aug(q,k,h,bias,lane)
        s=dg(ka,qa,NT)
        m=jnp.max(s,axis=0,keepdims=True)
        e=jnp.exp(s-m)
        l=jnp.sum(e,axis=0,keepdims=True)
        ot=mm(vt[64*h:64*h+64],e.astype(BF))
        outs.append(ot*(1.0/l))
        l_ref[0,0,h:h+1,:]=m+jnp.log(l)
    o_ref[...]=jnp.concatenate(outs,axis=0).T.astype(BF)
def attn_fwd(rows, counts, pages):
    tokens, width = rows.shape
    length, pairs = tokens // pages, width // CW
    block = lambda o: pl.BlockSpec((length, 128), lambda p, h, c: (p, 3 * h + o))
    return pl.pallas_call(
        attn_fwd_kernel,
        grid_spec=pltpu.PrefetchScalarGridSpec(
            num_scalar_prefetch=1,
            grid=(pages, pairs),
            in_specs=[block(0), block(1), block(2)],
            out_specs=[
                pl.BlockSpec((length, 128), lambda p, h, c: (p, h)),
                pl.BlockSpec((1, 1, 2, length), lambda p, h, c: (p, h, 0, 0)),
            ],
        ),
        out_shape=[
            jax.ShapeDtypeStruct((tokens, pairs * 128), BF),
            jax.ShapeDtypeStruct((pages, pairs, 2, length), F32),
        ],
        compiler_params=params(),
        cost_estimate=cost(3.5 * pairs),
        name="attn_fwd",
    )(counts, rows, rows, rows)


def attn_bwd_kernel(cnt,q_ref,k_ref,v_ref,g_ref,o_ref,l_ref,d_ref,bq_ref,bv_ref):
    p=pl.program_id(1)
    q=q_ref[...];k=k_ref[...];v=v_ref[...];g=g_ref[...]
    lane=lax.broadcasted_iota(jnp.int32,q.shape,1)
    row=lax.broadcasted_iota(jnp.int32,q.shape,0)
    bias=jnp.where(row<cnt[p],0.0,-1e30).astype(BF)
    prod=g.astype(F32)*o_ref[...].astype(F32)
    hi=prod.astype(BF); lo=(prod-hi.astype(F32)).astype(BF)
    r8=lax.broadcasted_iota(jnp.int32,(16,128),0); l8=lax.broadcasted_iota(jnp.int32,(16,128),1)
    sel=jnp.where(r8==l8//64,1.0,0.0).astype(BF)
    delta=dg(sel,hi,NT)+dg(sel,lo,NT)
    kt=k.T
    dv=[];dk=[];dqt=[]
    for h in range(2):
        qa,ka,own=aug(q,k,h,bias,lane)
        s=dg(ka,qa,NT)
        pr=jnp.exp(s-l_ref[0,0,h:h+1,:])
        va=jnp.where(own,v,jnp.zeros_like(v))
        dp=dg(va,g,NT)
        ds=(pr*(dp-delta[h:h+1])).astype(BF)
        dv.append(mm(pr.astype(BF),g)); dk.append(mm(ds,q))
        dqt.append(mm(kt[64*h:64*h+64],ds))
    first=lane<64
    dvv=jnp.where(first,dv[0],dv[1])
    dq=jnp.concatenate(dqt,axis=0).T*0.125
    d_ref[:,:128]=dq.astype(BF); d_ref[:,256:]=dvv.astype(BF)
    d_ref[:,128:256]=jnp.where(first,dk[0],dk[1]).astype(BF)
    sq=jnp.sum(dq,axis=0,keepdims=True); sv=jnp.sum(dvv,axis=0,keepdims=True)
    @pl.when(p==0)
    def _():
        bq_ref[...]=sq; bv_ref[...]=sv
    @pl.when(p>0)
    def _():
        bq_ref[...]+=sq; bv_ref[...]+=sv
def attn_bwd(rows, counts, grad, out, totals, pages, at):
    tokens, width = rows.shape
    length, pairs = tokens // pages, width // CW
    block = lambda o: pl.BlockSpec((length, 128), lambda h, p, c: (p, 3 * h + o))
    line = pl.BlockSpec((1, 128), lambda h, p, c: (0, h))
    return pl.pallas_call(
        attn_bwd_kernel,
        grid_spec=pltpu.PrefetchScalarGridSpec(
            num_scalar_prefetch=1,
            grid=(pairs, pages),
            in_specs=[
                block(0),
                block(1),
                block(2),
                pl.BlockSpec((length, 128), lambda h, p, c: (p, h + at)),
                pl.BlockSpec((length, 128), lambda h, p, c: (p, h)),
                pl.BlockSpec((1, 1, 2, length), lambda h, p, c: (p, h, 0, 0)),
            ],
            out_specs=[pl.BlockSpec((length, CW), lambda h, p, c: (p, h))] + [line] * 2,
        ),
        out_shape=[jax.ShapeDtypeStruct((tokens, width), BF)]
        + [jax.ShapeDtypeStruct((1, pairs * 128), F32)] * 2,
        compiler_params=params(),
        cost_estimate=cost(4.5 * pairs),
        name="attn_bwd",
    )(counts, rows, rows, rows, grad, out, totals)


def norm(t):
    m=jnp.mean(t,axis=-1,keepdims=True); c=t-m
    v=jnp.mean(c*c,axis=-1,keepdims=True); inv=lax.rsqrt(v+1e-12)
    return c*inv,inv
def norm_back(e,hat,inv):
    return inv*(e-jnp.mean(e,axis=-1,keepdims=True)-hat*jnp.mean(e*hat,axis=-1,keepdims=True))
def col(t): return jnp.sum(t,axis=0,keepdims=True)
C=1536
def main_fetch_kernel(pos, *refs):
    att, (x, cot), refs = refs[:-47], refs[-47:-45], refs[-45:]
    two, three, rest = refs[:8], refs[8:16], refs[16:]
    vecs, outs, scratch = rest[:7], rest[7:22], rest[22:]
    slope, ow, uw, dw, *sems = scratch

    copies = (
        fetch(pos, two, ow, 48, 0, CW, sems[0]),
        fetch(pos, two, uw, 48, CW, uw.shape[1] // 2, sems[1]),
        fetch(pos, three, dw, dw.shape[0] // 16, 0, CW, sems[2]),
    )
    at_start = pl.program_id(0) == 0

    @pl.when(at_start)
    def _():
        for group in copies:
            for copy in group:
                copy.start()

    def ready(place):
        @pl.when(at_start)
        def _():
            for copy in copies[place]:
                copy.wait()

    main_kernel(att, x, cot, ow, uw, dw, *vecs, *outs, slope, ready)


def main_plain_kernel(*refs):
    main_kernel(refs[:-28], *refs[-28:])


def main_kernel(att,x,cot,ow,uw,dw,ob,g1,s1,ub,db,g2,s2,
                lo_ref,act_ref,sl_ref,nl_ref,pl_ref,fl_ref,gf_ref,ga_ref,
                vg2,vs2,vdb,vub,vg1,vs1,vob,slope,ready=lambda place: None):
    i=pl.program_id(0)
    FF=uw.shape[1]
    ready(0)
    fs=x[...].astype(F32)+mm(joined(att),ow[...])+ob[...]
    fh,fi=norm(fs)
    normed=fh*g1[...]+s1[...]
    nl=normed.astype(BF); nl_ref[...]=nl
    acc=normed+db[...]
    ready(1)
    for j in range(0,FF,C):
        pre=mm(nl,uw[:,j:j+C])+ub[:,j:j+C]
        phi=0.5*(1.0+lax.erf(pre*(1.0/math.sqrt(2.0))))
        a=(pre*phi).astype(BF)
        act_ref[:,j:j+C]=a
        slope[:,j:j+C]=phi+pre*jnp.exp(-0.5*pre*pre)*(1.0/math.sqrt(2.0*math.pi))
        if j==0: ready(2)
        acc=acc+mm(a,dw[j:j+C,:])
    sh,si=norm(acc)
    lo_ref[...]=(sh*g2[...]+s2[...]).astype(BF)
    gr=cot[...].astype(F32)
    gs=norm_back(gr*g2[...],sh,si)
    sl=gs.astype(BF); sl_ref[...]=sl
    gn=gs
    ubs=[]
    for j in range(0,FF,C):
        gp=dg(sl,dw[j:j+C,:],NT)*slope[:,j:j+C]
        ubs.append(col(gp))
        gpl=gp.astype(BF); pl_ref[:,j:j+C]=gpl
        gn=gn+dg(gpl,uw[:,j:j+C],NT)
    gf=norm_back(gn*g1[...],fh,fi)
    fl=gf.astype(BF); fl_ref[...]=fl; gf_ref[...]=gf
    ga_ref[...]=dg(fl,ow[...],NT).astype(BF)
    vals=[(vg2,col(gr*sh)),(vs2,col(gr)),(vdb,col(gs)),(vub,jnp.concatenate(ubs,1)),(vg1,col(gn*fh)),(vs1,col(gn)),(vob,col(gf))]
    @pl.when(i==0)
    def _():
        for r,v in vals: r[...]=v
    @pl.when(i>0)
    def _():
        for r,v in vals: r[...]+=v
def main(att, x, cot, weights, vecs, pos=None, R=256):
    T, D = x.shape
    FF = vecs[3].shape[1]
    rb = lambda n: pl.BlockSpec((R, n), lambda i, *p: (i, 0))
    full = lambda a: pl.BlockSpec(a.shape, lambda i, *p: (0, 0))
    sds = lambda n, t=BF: jax.ShapeDtypeStruct((T, n), t)
    vec = lambda n: (pl.BlockSpec((1, n), lambda i, *p: (0, 0)), jax.ShapeDtypeStruct((1, n), F32))
    vs = [vec(n) for n in (D, D, D, FF, D, D, D)]
    fetched = pos is not None
    scratch = [pltpu.VMEM((R, FF), F32)]
    if fetched:
        scratch += [pltpu.VMEM((D, D), BF), pltpu.VMEM((D, FF), BF), pltpu.VMEM((FF, D), BF)] + [pltpu.SemaphoreType.DMA] * 3
    return pl.pallas_call(
        main_fetch_kernel if fetched else main_plain_kernel,
        grid_spec=pltpu.PrefetchScalarGridSpec(
            num_scalar_prefetch=1 if fetched else 0,
            grid=(T // R,),
            in_specs=[rb(a.shape[1]) for a in (*att, x, cot)]
            + [pl.BlockSpec(memory_space=pl.ANY) if fetched else full(w) for w in weights]
            + [full(v) for v in vecs],
            out_specs=[rb(D), rb(FF), rb(D), rb(D), rb(FF), rb(D), rb(D), rb(D)] + [v[0] for v in vs],
            scratch_shapes=scratch,
        ),
        out_shape=[sds(D), sds(FF), sds(D), sds(D), sds(FF), sds(D), sds(D, F32), sds(D)] + [v[1] for v in vs],
        compiler_params=params(),
        cost_estimate=cost(45),
        name="main",
    )(*([pos] if fetched else []), *att, x, cot, *weights, *vecs)


def tn_kernel(a,b,o): o[...]=dg(a[...],b[...],TN).astype(BF)
def tn(a,b,bm,bn):
    T,M=a.shape;N=b.shape[1]
    return pl.pallas_call(tn_kernel,grid=(M//bm,N//bn),
      in_specs=[pl.BlockSpec((T,bm),lambda i,j:(0,i)),pl.BlockSpec((T,bn),lambda i,j:(0,j))],
      out_specs=pl.BlockSpec((bm,bn),lambda i,j:(i,j)),out_shape=jax.ShapeDtypeStruct((M,N),BF),compiler_params=params())(a,b)
def ig_kernel(gf, parts, w, o):
    o[...] = (gf[...] + dg(joined(parts), w[...], NT)).astype(BF)


def ig_plain_kernel(gf, *refs):
    ig_kernel(gf, refs[:-2], refs[-2], refs[-1])


def ig_fetch_kernel(pos, gf, *refs):
    parts, buffers, (o, weight, sem) = refs[:-11], refs[-11:-3], refs[-3:]

    @pl.when(pl.program_id(0) == 0)
    def _():
        run_all(fetch_in(pos, buffers, weight, sem))

    ig_kernel(gf, parts, weight, o)


def ig(parts, gf, weights, pos=None, R=256):
    T, D = gf.shape
    rb = lambda n: pl.BlockSpec((R, n), lambda i, *p: (i, 0))
    fetched = pos is not None
    return pl.pallas_call(
        ig_fetch_kernel if fetched else ig_plain_kernel,
        grid_spec=pltpu.PrefetchScalarGridSpec(
            num_scalar_prefetch=1 if fetched else 0,
            grid=(T // R,),
            in_specs=[rb(a.shape[1]) for a in (gf, *parts)]
            + [pl.BlockSpec(memory_space=pl.ANY) if fetched else pl.BlockSpec(w.shape, lambda i, *p: (0, 0)) for w in weights],
            out_specs=rb(D),
            scratch_shapes=[pltpu.VMEM((D, 3 * D), BF), pltpu.SemaphoreType.DMA] if fetched else [],
        ),
        out_shape=jax.ShapeDtypeStruct((T, D), BF),
        compiler_params=params(),
        cost_estimate=cost(10),
        name="ig",
    )(*([pos] if fetched else []), gf, *parts, *weights)


def local(
    hidden_states,
    page_counts,
    cotangent,
    attn_in_weight,
    attn_in_bias,
    attn_out_weight,
    attn_out_bias,
    first_gain,
    first_shift,
    up_weight,
    up_bias,
    down_weight,
    down_bias,
    second_gain,
    second_shift,
):
    pages, length, model = hidden_states.shape
    hidden = up_weight.shape[1]
    x = hidden_states.reshape(-1, model)
    grad_rows = cotangent.reshape(-1, model)
    weights = (attn_in_weight, attn_out_weight, up_weight, down_weight)
    vectors = (
        attn_in_bias,
        attn_out_bias,
        first_gain,
        first_shift,
        up_bias,
        down_bias,
        second_gain,
        second_shift,
    )
    lined = lax.axis_size("fsdp") == 4 * LINE and lax.axis_size("rep") == 2
    pairs = HEADS // 2 // THIRDS
    forward = [None] * THIRDS
    backward = [None] * THIRDS

    def ahead(t, rows):
        forward[t] = attn_fwd(rows, page_counts, pages)

    def back(t, rows):
        backward[t] = attn_bwd(rows, page_counts, grad_att, *forward[t], pages, pairs * t)

    if lined:
        index = lax.axis_index("fsdp")
        pos = jnp.stack([index // 4, index // 2 % 2, index % 2, lax.axis_index("rep")]).astype(jnp.int32)
        one, two, three = pack(pos, weights, vectors)
        line_one = jnp.stack(along_line(one))
        second_one = move(line_one, to_second)
        first_one = move(line_one, to_first)
        parts_two = along_line(after(two, line_one))
        parts_three = along_line(after(three, line_one))
        both_one = move(after(second_one, *parts_two[1:]), to_first)
        in_w = over_core((line_one, first_one, second_one, both_one))
        line_two = jnp.stack(parts_two)
        second_two = move(line_two, to_second)
        first_two = move(line_two, to_first)
        outs = qkv_fetch(pos, x, after(in_w, line_two), 16)
        rows, full = outs[:THIRDS], outs[THIRDS:]
        line_three = jnp.stack(after(parts_three, rows))
        second_three = move(line_three, to_second)
        first_three = move(line_three, to_first)
        ahead(0, after(rows[0], line_three))
        both_two = move(after(second_two, forward[0]), to_first)
        ahead(1, after(rows[1], forward[0], second_two))
        both_three = move(after(second_three, forward[1]), to_first)
        ready = (line_two, first_two, second_two, line_three, first_three, second_three)
        ready = over_core(after(ready, forward[1]))
        ahead(2, after(rows[2], forward[1], second_three, first_three))
        last = over_core(after((both_two, both_three), forward[2]))
        later = (*ready[0:3], last[0], *ready[6:9], last[2], *ready[3:6], last[1], *ready[9:12], last[3])
    else:
        pos = None
        gathered = lambda a: lax.all_gather(a, "fsdp", axis=0, tiled=True)
        in_w = gathered(attn_in_weight).reshape(model, 3, -1, 128)
        in_w = (in_w.transpose(0, 2, 1, 3).reshape(model, 3 * model),)
        full = [gathered(v).astype(F32).reshape(1, -1) for v in vectors]
        later = tuple(gathered(w) for w in weights[1:])
        rows = qkv(x, in_w[0], pair_bias(full[0]))
        for t in range(THIRDS):
            ahead(t, rows[t])
    attended = [f[0] for f in forward]
    (
        output, act, second_low, normed_low, pre_low, first_low, grad_first, grad_att,
        vg2, vs2, vdb, vub, vg1, vs1, vob,
    ) = main(attended, x, grad_rows, later, full[1:], pos)
    if lined:
        keep_d, send_d = grad_down(pos, act, second_low)
        core_d = move(send_d, to_core)
        keep_u, send_u = grad_up(pos, *after((normed_low, pre_low), keep_d), attended, first_low)
        go_d, stay_d = add_core(keep_d, core_d)
        core_u = move(send_u, to_core)
        first_d = move(go_d, to_first)
        back(0, after(rows[0], go_d, stay_d, keep_u))
        go_u, stay_u = add_core(*after((keep_u, core_u), backward[0]))
        first_u = move(go_u, to_first)
        back(1, after(rows[1], go_u, stay_u))
        go_d, stay_d = add_core(*after((stay_d, first_d), backward[1]))
        second_d = move(go_d, to_second)
        keep_i, send_i = grad_in(pos, x, after((backward[0][0], backward[1][0]), go_d, stay_d))
        core_i = move(send_i, to_core)
        back(2, after(rows[2], keep_i))
        parts = tuple(b[0] for b in backward)
        vbq = jnp.concatenate([b[1] for b in backward], axis=1)
        vbv = jnp.concatenate([b[2] for b in backward], axis=1)
        go_i, stay_i = add_core(*after((keep_i, core_i), backward[2]))
        first_i = move(go_i, to_first)
        keep_l, send_l = grad_last(
            pos, x, after(parts[2], go_i, stay_i), (vbq, vbv, vub, vob, vg1, vs1, vdb, vg2, vs2)
        )
        core_l = move(send_l, to_core)
        go_u, stay_u = add_core(*after((stay_u, first_u), keep_l))
        second_u = move(go_u, to_second)
        low_d = add_last(*after((stay_d, second_d), go_u))
        line_d = move_line(low_d)
        go_l, stay_l = add_core(keep_l, after(core_l, low_d))
        first_l = move(go_l, to_first)
        go_i, stay_i = add_core(*after((stay_i, first_i), go_l, stay_l))
        second_i = move(go_i, to_second)
        input_grad = ig(parts, after(grad_first, go_i, stay_i), in_w, pos)
        low_u = add_last(*after((stay_u, second_u), input_grad))
        line_u = move_line(low_u)
        go_l, stay_l = add_core(*after((stay_l, first_l), low_u))
        second_l = move(go_l, to_second)
        low_i = add_last(*after((stay_i, second_i), go_l))
        line_i = move_line(low_i)
        mine_d = add_line(low_d, after(line_d, low_i))
        low_l = add_last(*after((stay_l, second_l), mine_d))
        line_l = move_line(low_l)
        got_d = move(mine_d, to_x)
        mine_u = add_line(low_u, after(line_u, low_l))
        got_u = move(mine_u, to_x)
        mine_i = add_line(low_i, after(line_i, mine_u))
        got_i = move(mine_i, to_x)
        (t_down,) = finish(
            finish_down_kernel, "finish_down", pos, (mine_d, after(got_d, mine_i)), [down_weight.shape]
        )
        mine_l = add_line(low_l, after(line_l, t_down))
        got_l = move(mine_l, to_x)
        t_out, t_up = finish(
            finish_up_kernel, "finish_up", pos, (mine_u, after(got_u, mine_l)),
            [attn_out_weight.shape, up_weight.shape],
        )
        shapes = [attn_in_weight.shape] + [(1, v.shape[0]) for v in vectors]
        t_in, *small = finish(finish_in_kernel, "finish_in", pos, (mine_i, got_i, mine_l, got_l), shapes)
        small = [b.reshape(-1) for b in small]
    else:
        for t in range(THIRDS):
            back(t, rows[t])
        parts = tuple(b[0] for b in backward)
        vbq = jnp.concatenate([b[1] for b in backward], axis=1)
        vbv = jnp.concatenate([b[2] for b in backward], axis=1)
        input_grad = ig(parts, grad_first, in_w)

        def total(a):
            share = lax.psum_scatter(a.astype(BF), "fsdp", scatter_dimension=0, tiled=True)
            return lax.psum(share, "rep").astype(F32)

        att = jnp.concatenate(attended, axis=1)
        t_down = total(tn(act, second_low, 768, 768))
        t_up = total(tn(normed_low, pre_low, 768, 768))
        t_out = total(tn(att, first_low, 768, 768))
        t_in = jnp.concatenate([tn(x, d, 768, 768) for d in parts], axis=1)
        t_in = total(t_in.reshape(model, -1, 3, 128).transpose(0, 2, 1, 3).reshape(model, 3 * model))
        small = [
            total(v.reshape(-1))
            for v in (jnp.concatenate([vbq, vbv], axis=1), vob, vg1, vs1, vub, vdb, vg2, vs2)
        ]
    b_in, b_out, b_g1, b_s1, b_up, b_down, b_g2, b_s2 = small
    return (
        output.reshape(hidden_states.shape),
        input_grad.reshape(hidden_states.shape),
        t_in, b_in, t_out, b_out, b_g1, b_s1, t_up, b_up, t_down, b_down, b_g2, b_s2,
    )


def solution(mesh):
    return jax.shard_map(
        local,
        mesh=mesh,
        in_specs=(
            P(("fsdp", "rep"), None, None),
            P(("fsdp", "rep")),
            P(("fsdp", "rep"), None, None),
            P("fsdp", None),
            P("fsdp"),
            P("fsdp", None),
            P("fsdp"),
            P("fsdp"),
            P("fsdp"),
            P("fsdp", None),
            P("fsdp"),
            P("fsdp", None),
            P("fsdp"),
            P("fsdp"),
            P("fsdp"),
        ),
        out_specs=(
            P(("fsdp", "rep"), None, None),
            P(("fsdp", "rep"), None, None),
            P("fsdp", None),
            P("fsdp"),
            P("fsdp", None),
            P("fsdp"),
            P("fsdp"),
            P("fsdp"),
            P("fsdp", None),
            P("fsdp"),
            P("fsdp", None),
            P("fsdp"),
            P("fsdp"),
            P("fsdp"),
        ),
        check_vma=False,
    )
```

```python
import math

import jax
import jax.numpy as jnp
from jax import lax
from jax.experimental import pallas as pl
from jax.experimental.pallas import tpu as pltpu
from jax.sharding import PartitionSpec as P

HEADS = 12
BF = jnp.bfloat16
F32 = jnp.float32
NT = (((1,), (1,)), ((), ()))
TN = (((0,), (0,)), ((), ()))
CW = 384
THIRDS = 3
LINE = 4
TINY = 128
AXES = ("fsdp", "rep")


def dg(a, b, dims):
    return lax.dot_general(a, b, dims, preferred_element_type=F32)


def mm(a, b):
    return jnp.dot(a, b, preferred_element_type=F32)


def params():
    return pltpu.CompilerParams(vmem_limit_bytes=60 * 1024 * 1024)


def cost(us):
    return pl.CostEstimate(flops=int(us * 1.15e9), bytes_accessed=int(us * 1e6), transcendentals=0)


def flat_index(z, y, c, x):
    return (z * 4 + y * 2 + c) * 2 + x


def permutation(target):
    pairs = []
    for z in range(LINE):
        for y in range(2):
            for c in range(2):
                for x in range(2):
                    pairs.append((flat_index(z, y, c, x), flat_index(*target(z, y, c, x))))
    return pairs


def to_core(z, y, c, x):
    return (z, y, 1 - c, x)


def to_x(z, y, c, x):
    return (z, y, c, 1 - x)


def to_first(z, y, c, x):
    return (z, y, c, 1 - x) if c == 0 else (z, 1 - y, c, x)


def to_second(z, y, c, x):
    return (z, 1 - y, c, x) if c == 0 else (z, y, c, 1 - x)


def to_line(step):
    return lambda z, y, c, x: ((z + step) % LINE, y, c, x)


def move(value, target):
    return lax.ppermute(value, AXES, permutation(target))


def after(values, *earlier):
    return lax.optimization_barrier((values, earlier))[0]


def along_line(half):
    return [half] + [move(half, to_line(k)) for k in range(1, LINE)]


def over_core(parts):
    return tuple(parts) + tuple(move(part, to_core) for part in parts)


def add_core(keep, got):
    keep, got = keep.astype(F32), got.astype(F32)
    return (keep[1] + got[1]).astype(BF), (keep[0] + got[0]).astype(BF)


def add_kernel(keep, got, go, stay):
    total = keep[...].astype(F32) + got[...].astype(F32)
    stay[...] = total[0].astype(BF)
    go[...] = total[1].astype(BF)


def add_wide(keep, got):
    _, second, line, rows, width = keep.shape
    half = line // 2
    both = pl.BlockSpec((2, 1, half, rows, width), lambda i, j: (0, i, j, 0, 0))
    one = pl.BlockSpec((1, half, rows, width), lambda i, j: (i, j, 0, 0))
    return pl.pallas_call(
        add_kernel,
        grid=(second, 2),
        in_specs=[both, both],
        out_specs=[one, one],
        out_shape=[jax.ShapeDtypeStruct(keep.shape[1:], BF)] * 2,
        compiler_params=params(),
        cost_estimate=cost(4),
        name="add_wide",
    )(keep, got)


def add_last(stay, got):
    return (stay.astype(F32) + got.astype(F32)).astype(BF)


def add_line(low, parts):
    total = low[0].astype(F32)
    for part in parts:
        total = total + part.astype(F32)
    return total.astype(BF)


def move_line(low):
    return [move(low[k], to_line(k)) for k in range(1, LINE)]


FIELDS = (((0, 0, 96), (4, 1, 192)), tuple((n, i, 48) for i, n in enumerate((1, 2, 3, 5, 6, 7))))


def rows_of(width):
    return [(i, at, min(TINY, width - at)) for i, at in enumerate(range(0, width, TINY))]


def pack_kernel(pos, inw, outw, upw, downw, *refs):
    vectors, (one, two, three) = refs[:8], refs[8:]

    def fill(x):
        third = inw.shape[1] // 3
        for t in range(THIRDS):
            for part in range(3):
                start = part * third + (2 * t + x) * 128
                piece = inw[:, start : start + 128]
                one[:, t * CW + part * 128 : t * CW + (part + 1) * 128] = piece
        row = lax.broadcasted_iota(jnp.int32, (48, TINY), 0)
        block = jnp.zeros((48, TINY), F32)
        for place, top, size in FIELDS[x]:
            for i, at, n in rows_of(size):
                piece = vectors[place][:, at : at + n].astype(F32)
                if n < TINY:
                    piece = jnp.concatenate([piece, jnp.zeros((1, TINY - n), F32)], axis=1)
                block = jnp.where(row == top + i, jnp.broadcast_to(piece, (48, TINY)), block)
        one[:, THIRDS * CW :] = block.astype(BF)
        two[:, :CW] = outw[:, x * CW : (x + 1) * CW]
        width = upw.shape[1] // 2
        two[:, CW:] = upw[:, x * width : (x + 1) * width]
        three[...] = downw[:, x * CW : (x + 1) * CW]

    @pl.when(pos[3] == 0)
    def _():
        fill(0)

    @pl.when(pos[3] == 1)
    def _():
        fill(1)


def pack(pos, weights, vectors):
    shapes = [
        (48, weights[0].shape[1] // 2 + TINY),
        (48, weights[1].shape[1] // 2 + weights[2].shape[1] // 2),
        (weights[3].shape[0], CW),
    ]
    arrays = tuple(weights) + tuple(v.reshape(1, -1) for v in vectors)
    full = lambda a: pl.BlockSpec(a, lambda i, p: (0, 0))
    return pl.pallas_call(
        pack_kernel,
        grid_spec=pltpu.PrefetchScalarGridSpec(
            num_scalar_prefetch=1,
            grid=(1,),
            in_specs=[full(a.shape) for a in arrays],
            out_specs=[full(a) for a in shapes],
        ),
        out_shape=[jax.ShapeDtypeStruct(a, BF) for a in shapes],
        compiler_params=params(),
        name="pack",
    )(pos, *arrays)


def sources(pos):
    z, y, c, x = pos[0], pos[1], pos[2], pos[3]
    found = []
    for other in range(2):
        core = c ^ 1 if other else c
        swap = core == 0
        for first in range(2):
            for second in range(2):
                dx = jnp.where(swap, first, second)
                dy = jnp.where(swap, second, first)
                buffer = other * 4 + second * 2 + first
                for k in range(LINE):
                    shard = ((z - k) & (LINE - 1)) * 4 + (y ^ dy) * 2 + core
                    found.append((buffer, k, shard, x ^ dx))
    return found


def fetch(pos, buffers, target, rows, column, width, sem, stride=None, start=0):
    stride = width if stride is None else stride
    return [
        pltpu.make_async_copy(
            buffers[buffer].at[k, :, pl.ds(column, width)],
            target.at[
                pl.ds(pl.multiple_of(shard * rows, 16), rows),
                pl.ds(pl.multiple_of(start + x * stride, 128), width),
            ],
            sem,
        )
        for buffer, k, shard, x in sources(pos)
    ]


def fetch_in(pos, buffers, target, sem):
    copies = []
    for t in range(THIRDS):
        copies += fetch(pos, buffers, target, 48, t * CW, CW, sem, None, 2 * CW * t)
    return copies


def fetch_tiny(pos, buffers, target, column, sem):
    return [
        pltpu.make_async_copy(
            buffers[buffer].at[k, pl.ds(0, 16), pl.ds(column, TINY)], target.at[x, shard], sem
        )
        for buffer, k, shard, x in sources(pos)
    ]


def run_all(copies):
    for copy in copies:
        copy.start()
    for copy in copies:
        copy.wait()


def spots(length, size, axis):
    shape = (length, TINY) if axis == 0 else (TINY, length)
    entry = lax.broadcasted_iota(jnp.int32, shape, axis).astype(F32)
    lane = lax.broadcasted_iota(jnp.int32, shape, 1 - axis).astype(F32)
    inner = entry - jnp.floor((entry + 0.5) * (1.0 / size)) * size
    return [
        jnp.where((lane + at == inner) & (lane < n), 1.0, 0.0).astype(BF) for _, at, n in rows_of(size)
    ]


def owned(shards, length):
    size = length // shards
    start = lax.broadcasted_iota(jnp.int32, (shards, length), 0) * size
    entry = lax.broadcasted_iota(jnp.int32, (shards, length), 1)
    return (entry >= start) & (entry < start + size)


def unpack_vectors(tiny, targets):
    shards = tiny.shape[1]
    made = {}
    for half in range(2):
        for place, top, size in FIELDS[half]:
            total = shards * size
            if size not in made:
                made[size] = spots(total, size, 1), owned(shards, total)
            each, mask = made[size]
            tiled = sum(mm(tiny[half, :, top + i, :], spot) for i, spot in enumerate(each))
            targets[place][...] = jnp.sum(jnp.where(mask, tiled, 0.0), axis=0, keepdims=True)


def place_tile(pos, held, keep, send, rows, line):
    z, y, c, x = pos[0], pos[1], pos[2], pos[3]
    for relative, out in enumerate((keep, send)):
        core = c ^ relative
        swap = core == 0
        for first in range(2):
            for second in range(2):
                dx = jnp.where(swap, first, second)
                dy = jnp.where(swap, second, first)
                for slot, chip in line:
                    shard = chip * 4 + (y ^ dy) * 2 + core
                    start = pl.multiple_of(shard * rows, 16)
                    out[first, second, slot] = held[x ^ dx, pl.ds(start, rows), :]


def whole_line(pos):
    return [(k, (pos[0] + k) & (LINE - 1)) for k in range(LINE)]


def hold(held, tile):
    width = tile.shape[1] // 2
    held[0] = tile[:, :width].astype(BF)
    held[1] = tile[:, width:].astype(BF)


def joined(refs):
    return jnp.concatenate([r[...] for r in refs], axis=1)


def tiny_rows(vectors, fields):
    rows = []
    made = {}
    for vector, (_, _, size) in zip(vectors, fields):
        length = vector.shape[1]
        if size not in made:
            made[size] = spots(length, size, 0), owned(16, length)
        each, mask = made[size]
        own = jnp.where(mask, jnp.broadcast_to(vector, mask.shape), 0.0).astype(BF)
        rows += [mm(own, spot) for spot in each]
    count = len(rows)
    rows = jnp.concatenate(rows + [jnp.zeros((16 * (8 - count), TINY), F32)], axis=0).astype(BF)
    to = lax.broadcasted_iota(jnp.int32, (16 * 48, 128), 0)
    of = lax.broadcasted_iota(jnp.int32, (16 * 48, 128), 1)
    lift = jnp.where(to == (of & 15) * 48 + (of >> 4), 1.0, 0.0).astype(BF)
    return mm(lift, rows).astype(BF)


def grad_in_kernel(pos, x, *refs):
    parts, (keep, send, held) = refs[:-3], refs[-3:]
    for i, ref in enumerate(parts):

        @pl.when(pl.program_id(0) == i)
        def _(ref=ref):
            hold(held, dg(x[...], ref[...], TN))

    place_tile(pos, held, keep, send, 48, whole_line(pos))


def grad_last_kernel(pos, x, part, *refs):
    bq, bv, refs = refs[:THIRDS], refs[THIRDS : 2 * THIRDS], refs[2 * THIRDS :]
    upb, outb, g1, s1, downb, g2, s2, keep, send, held = refs
    hold(held, dg(x[...], part[...], TN))
    take = lambda ref: ref.at[:, :, :, :, pl.ds(0, CW)]
    place_tile(pos, held, take(keep), take(send), 48, whole_line(pos))
    groups = ((joined((*bq, *bv)), upb[...]), [r[...] for r in (outb, g1, s1, downb, g2, s2)])
    for half in range(2):
        held[half, :, :TINY] = tiny_rows(groups[half], FIELDS[half])
    take = lambda ref: ref.at[:, :, :, :, pl.ds(CW, TINY)]
    place_tile(pos, held.at[:, :, pl.ds(0, TINY)], take(keep), take(send), 48, whole_line(pos))


def grad_call(kernel, name, pos, arrays, in_specs, grid, block, shape, index, us):
    held = (2, 16 * 48, CW)
    return pl.pallas_call(
        kernel,
        grid_spec=pltpu.PrefetchScalarGridSpec(
            num_scalar_prefetch=1,
            grid=(grid,),
            in_specs=in_specs,
            out_specs=[pl.BlockSpec(block, index)] * 2,
            scratch_shapes=[pltpu.VMEM(held, BF)],
        ),
        out_shape=[jax.ShapeDtypeStruct(shape, BF)] * 2,
        compiler_params=params(),
        cost_estimate=cost(us),
        name=name,
    )(pos, *arrays)


def whole(array):
    return pl.BlockSpec(array.shape, lambda j, p: (0,) * array.ndim)


def grad_in(pos, x, parts):
    return grad_call(
        grad_in_kernel, "grad_in", pos, (x, *parts), [whole(a) for a in (x, *parts)], len(parts),
        (2, 2, LINE, 48, CW), (2, 2, LINE, 48, CW * len(parts)), lambda j, p: (0, 0, 0, 0, j), 5,
    )


def grad_last(pos, x, part, vectors):
    arrays = (x, part, *vectors)
    shape = (2, 2, LINE, 48, CW + TINY)
    return grad_call(
        grad_last_kernel, "grad_last", pos, arrays, [whole(a) for a in arrays], 1,
        shape, shape, lambda j, p: (0, 0, 0, 0, 0), 4,
    )


def halves(pos, mine, got):
    swap = pos[3] == 0
    return jnp.where(swap, mine, got).astype(F32), jnp.where(swap, got, mine).astype(F32)


def finish_down_kernel(pos, mine, got, down):
    for x, half in enumerate(halves(pos, mine[...], got[...])):
        down[:, CW * x : CW * (x + 1)] = half


def finish_kernel(pos, mine_u, got_u, mine, got, mine_last, got_last, out, up, weight, *vectors):
    width = up.shape[1] // 2
    third = weight.shape[1] // 3
    for x, half in enumerate(halves(pos, mine_u[...], got_u[...])):
        out[:, CW * x : CW * (x + 1)] = half[:, :CW]
        up[:, width * x : width * (x + 1)] = half[:, CW:]
    more = halves(pos, mine[...], got[...])
    for x, last in enumerate(halves(pos, mine_last[...], got_last[...])):
        for t in range(THIRDS):
            for part in range(3):
                start = part * third + (2 * t + x) * 128
                if t < THIRDS - 1:
                    piece = more[x][:, t * CW + part * 128 : t * CW + (part + 1) * 128]
                else:
                    piece = last[:, part * 128 : (part + 1) * 128]
                weight[:, start : start + 128] = piece
        for place, top, size in FIELDS[x]:
            for i, at, n in rows_of(size):
                vectors[place][:, at : at + n] = last[top + i : top + i + 1, CW : CW + n]


def finish(kernel, name, pos, sums, shapes):
    full = lambda shape: pl.BlockSpec(shape, lambda i, p: (0, 0))
    return pl.pallas_call(
        kernel,
        grid_spec=pltpu.PrefetchScalarGridSpec(
            num_scalar_prefetch=1,
            grid=(1,),
            in_specs=[full(a.shape) for a in sums],
            out_specs=[full(shape) for shape in shapes],
        ),
        out_shape=[jax.ShapeDtypeStruct(shape, F32) for shape in shapes],
        compiler_params=params(),
        name=name,
    )(pos, *sums)


def pair_bias(bias):
    model = bias.shape[1] // 2
    parts = []
    for pair in range(model // 128):
        at = pair * 128
        parts += [bias[:, at : at + 128], jnp.zeros((1, 128), F32), bias[:, model + at : model + at + 128]]
    return jnp.concatenate(parts, axis=1)


def qkv_rows(x, weight, bias, outs):
    y = mm(x[...], weight[...])
    scale = 1.0 / math.sqrt(x.shape[1] // HEADS)
    for t, out in enumerate(outs):
        width = out.shape[1]
        for at in range(0, width, 128):
            here = y[:, t * width + at : t * width + at + 128]
            place = t * width + at
            if at // 128 % 3 != 1:
                here = here + bias[:, place : place + 128]
            here = here.astype(BF)
            out[:, at : at + 128] = here * jnp.asarray(scale, BF) if at // 128 % 3 == 0 else here


def qkv_fetch_kernel(pos, x, *refs):
    buffers, outs, refs = refs[:8], refs[8 : 8 + THIRDS], refs[8 + THIRDS :]
    vectors, (weight, tiny, bias, sem, sem_tiny) = refs[:8], refs[8:]

    @pl.when(pl.program_id(0) == 0)
    def _():
        copies = fetch_in(pos, buffers, weight, sem)
        small = fetch_tiny(pos, buffers, tiny, THIRDS * CW, sem_tiny)
        for copy in small + copies:
            copy.start()
        for copy in small:
            copy.wait()
        unpack_vectors(tiny, vectors)
        bias[...] = pair_bias(vectors[0][...])
        for copy in copies:
            copy.wait()

    qkv_rows(x, weight, bias, outs)


def qkv_fetch(pos, x, buffers, shards, block=256):
    tokens, model = x.shape
    vec = lambda n: (pl.BlockSpec((1, n), lambda i, p: (0, 0)), jax.ShapeDtypeStruct((1, n), F32))
    vecs = [vec(model * n) for n in (2, 1, 1, 1, 4, 1, 1, 1)]
    return pl.pallas_call(
        qkv_fetch_kernel,
        grid_spec=pltpu.PrefetchScalarGridSpec(
            num_scalar_prefetch=1,
            grid=(tokens // block,),
            in_specs=[pl.BlockSpec((block, model), lambda i, p: (i, 0))]
            + [pl.BlockSpec(memory_space=pl.ANY)] * 8,
            out_specs=[pl.BlockSpec((block, 2 * CW), lambda i, p: (i, 0))] * THIRDS + [v[0] for v in vecs],
            scratch_shapes=[
                pltpu.VMEM((model, 3 * model), BF),
                pltpu.VMEM((2, shards, 16, TINY), BF),
                pltpu.VMEM((1, 3 * model), F32),
                pltpu.SemaphoreType.DMA,
                pltpu.SemaphoreType.DMA,
            ],
        ),
        out_shape=[jax.ShapeDtypeStruct((tokens, 2 * CW), BF)] * THIRDS + [v[1] for v in vecs],
        compiler_params=params(),
        cost_estimate=cost(10),
        name="qkv_fetch",
    )(pos, x, *buffers)


def qkv_plain_kernel(x, weight, bias, *outs):
    qkv_rows(x, weight, bias, outs)


def qkv(x, weight, bias, block=256):
    tokens, model = x.shape
    full = lambda a: pl.BlockSpec(a.shape, lambda i: (0, 0))
    return pl.pallas_call(
        qkv_plain_kernel,
        grid=(tokens // block,),
        in_specs=[pl.BlockSpec((block, model), lambda i: (i, 0)), full(weight), full(bias)],
        out_specs=[pl.BlockSpec((block, 2 * CW), lambda i: (i, 0))] * THIRDS,
        out_shape=[jax.ShapeDtypeStruct((tokens, 2 * CW), BF)] * THIRDS,
        compiler_params=params(),
    )(x, weight, bias)


def aug(q,k,h,bias,lane):
    own=(lane>=64) if h else (lane<64)
    j0=0 if h else 64
    z=jnp.zeros_like(q)
    one=jnp.where(lane==j0,jnp.ones_like(q),z)
    qa=jnp.where(own,q,one)
    ka=jnp.where(own,k,jnp.where(lane==j0,bias,z))
    return qa,ka,own
def attn_fwd_kernel(cnt,q_ref,k_ref,v_ref,o_ref,l_ref):
    p=pl.program_id(0)
    q=q_ref[...];k=k_ref[...];v=v_ref[...]
    S=q.shape[0]
    lane=lax.broadcasted_iota(jnp.int32,q.shape,1)
    row=lax.broadcasted_iota(jnp.int32,q.shape,0)
    bias=jnp.where(row<cnt[p],0.0,-1e30).astype(BF)
    vt=v.T
    outs=[]
    for h in range(2):
        qa,ka,own=aug(q,k,h,bias,lane)
        s=dg(ka,qa,NT)
        m=jnp.max(s,axis=0,keepdims=True)
        e=jnp.exp(s-m)
        l=jnp.sum(e,axis=0,keepdims=True)
        ot=mm(vt[64*h:64*h+64],e.astype(BF))
        outs.append(ot*(1.0/l))
        l_ref[0,0,h:h+1,:]=m+jnp.log(l)
    o_ref[...]=jnp.concatenate(outs,axis=0).T.astype(BF)
def attn_fwd(rows, counts, pages):
    tokens, width = rows.shape
    length, pairs = tokens // pages, width // CW
    block = lambda o: pl.BlockSpec((length, 128), lambda p, h, c: (p, 3 * h + o))
    return pl.pallas_call(
        attn_fwd_kernel,
        grid_spec=pltpu.PrefetchScalarGridSpec(
            num_scalar_prefetch=1,
            grid=(pages, pairs),
            in_specs=[block(0), block(1), block(2)],
            out_specs=[
                pl.BlockSpec((length, 128), lambda p, h, c: (p, h)),
                pl.BlockSpec((1, 1, 2, length), lambda p, h, c: (p, h, 0, 0)),
            ],
        ),
        out_shape=[
            jax.ShapeDtypeStruct((tokens, pairs * 128), BF),
            jax.ShapeDtypeStruct((pages, pairs, 2, length), F32),
        ],
        compiler_params=params(),
        cost_estimate=cost(3.5 * pairs),
        name="attn_fwd",
    )(counts, rows, rows, rows)


def attn_bwd_kernel(cnt,q_ref,k_ref,v_ref,g_ref,o_ref,l_ref,d_ref,bq_ref,bv_ref):
    p=pl.program_id(1)
    q=q_ref[...];k=k_ref[...];v=v_ref[...];g=g_ref[...]
    lane=lax.broadcasted_iota(jnp.int32,q.shape,1)
    row=lax.broadcasted_iota(jnp.int32,q.shape,0)
    bias=jnp.where(row<cnt[p],0.0,-1e30).astype(BF)
    prod=g.astype(F32)*o_ref[...].astype(F32)
    hi=prod.astype(BF); lo=(prod-hi.astype(F32)).astype(BF)
    r8=lax.broadcasted_iota(jnp.int32,(16,128),0); l8=lax.broadcasted_iota(jnp.int32,(16,128),1)
    sel=jnp.where(r8==l8//64,1.0,0.0).astype(BF)
    delta=dg(sel,hi,NT)+dg(sel,lo,NT)
    kt=k.T
    dv=[];dk=[];dqt=[]
    for h in range(2):
        qa,ka,own=aug(q,k,h,bias,lane)
        s=dg(ka,qa,NT)
        pr=jnp.exp(s-l_ref[0,0,h:h+1,:])
        va=jnp.where(own,v,jnp.zeros_like(v))
        dp=dg(va,g,NT)
        ds=(pr*(dp-delta[h:h+1])).astype(BF)
        dv.append(mm(pr.astype(BF),g)); dk.append(mm(ds,q))
        dqt.append(mm(kt[64*h:64*h+64],ds))
    first=lane<64
    dvv=jnp.where(first,dv[0],dv[1])
    dq=jnp.concatenate(dqt,axis=0).T*0.125
    d_ref[:,:128]=dq.astype(BF); d_ref[:,256:]=dvv.astype(BF)
    d_ref[:,128:256]=jnp.where(first,dk[0],dk[1]).astype(BF)
    sq=jnp.sum(dq,axis=0,keepdims=True); sv=jnp.sum(dvv,axis=0,keepdims=True)
    @pl.when(p==0)
    def _():
        bq_ref[...]=sq; bv_ref[...]=sv
    @pl.when(p>0)
    def _():
        bq_ref[...]+=sq; bv_ref[...]+=sv
def attn_bwd(rows, counts, grad, out, totals, pages, at):
    tokens, width = rows.shape
    length, pairs = tokens // pages, width // CW
    block = lambda o: pl.BlockSpec((length, 128), lambda h, p, c: (p, 3 * h + o))
    line = pl.BlockSpec((1, 128), lambda h, p, c: (0, h))
    return pl.pallas_call(
        attn_bwd_kernel,
        grid_spec=pltpu.PrefetchScalarGridSpec(
            num_scalar_prefetch=1,
            grid=(pairs, pages),
            in_specs=[
                block(0),
                block(1),
                block(2),
                pl.BlockSpec((length, 128), lambda h, p, c: (p, h + at)),
                pl.BlockSpec((length, 128), lambda h, p, c: (p, h)),
                pl.BlockSpec((1, 1, 2, length), lambda h, p, c: (p, h, 0, 0)),
            ],
            out_specs=[pl.BlockSpec((length, CW), lambda h, p, c: (p, h))] + [line] * 2,
        ),
        out_shape=[jax.ShapeDtypeStruct((tokens, width), BF)]
        + [jax.ShapeDtypeStruct((1, pairs * 128), F32)] * 2,
        compiler_params=params(),
        cost_estimate=cost(4.5 * pairs),
        name="attn_bwd",
    )(counts, rows, rows, rows, grad, out, totals)


def norm(t):
    m=jnp.mean(t,axis=-1,keepdims=True); c=t-m
    v=jnp.mean(c*c,axis=-1,keepdims=True); inv=lax.rsqrt(v+1e-12)
    return c*inv,inv
def norm_back(e,hat,inv):
    return inv*(e-jnp.mean(e,axis=-1,keepdims=True)-hat*jnp.mean(e*hat,axis=-1,keepdims=True))
def col(t): return jnp.sum(t,axis=0,keepdims=True)
C=1536
def main_fetch_kernel(pos, *refs):
    att, (x, cot), refs = refs[:-49], refs[-49:-47], refs[-47:]
    two, three, refs = refs[:8], refs[8:16], refs[16:]
    vecs, (out, gf, ga), sums, refs = refs[:7], refs[7:10], refs[10:17], refs[17:]
    keep_d, send_d, keep_u, send_u, refs = *refs[:4], refs[4:]
    slope, ow, uw, dw, big, wide, held, *sems = refs
    act, pre = big.at[0], big.at[1]
    low, back, first, attended = (wide.at[n] for n in range(4))
    step = pl.program_id(0)
    rows = x.shape[0]
    blocks = act.shape[0] // rows
    copies = (
        fetch(pos, two, ow, 48, 0, CW, sems[0]),
        fetch(pos, two, uw, 48, CW, uw.shape[1] // 2, sems[1]),
        fetch(pos, three, dw, dw.shape[0] // 16, 0, CW, sems[2]),
    )

    @pl.when(step == 0)
    def _():
        for group in copies:
            for copy in group:
                copy.start()

    def ready(place):
        @pl.when(step == 0)
        def _():
            for copy in copies[place]:
                copy.wait()

    @pl.when(step < blocks)
    def _():
        here = pl.ds(pl.multiple_of(step * rows, 16), rows)
        attended[here, :] = joined(att)
        main_kernel(
            att, x, cot, ow, uw, dw, *vecs, out,
            act.at[here, :], back.at[here, :], low.at[here, :], pre.at[here, :], first.at[here, :],
            gf, ga, *sums, slope, ready,
        )

    @pl.when((step >= blocks) & (step < blocks + LINE))
    def _():
        chip = (pos[0] + step - blocks) & (LINE - 1)
        columns = act.shape[1] // LINE
        here = pl.ds(pl.multiple_of(chip * columns, 128), columns)
        hold(held, dg(act[:, here], back[...], TN))
        place_tile(pos, held, keep_d, send_d, held.shape[1] // 4, [(0, 0)])

    @pl.when(step == blocks + LINE)
    def _():
        hold(held, dg(attended[...], first[...], TN))
        place_tile(pos, held, keep_u, send_u, 48, whole_line(pos))

    @pl.when(step > blocks + LINE)
    def _():
        at = pl.multiple_of((step - blocks - LINE - 1) * CW, 128)
        right = pl.multiple_of(at + pre.shape[1] // 2, 128)
        columns = jnp.concatenate([pre[:, pl.ds(at, CW)], pre[:, pl.ds(right, CW)]], axis=1)
        hold(held, dg(low[...], columns, TN))
        place_tile(pos, held, keep_u, send_u, 48, whole_line(pos))


def main_fetch(pos, att, x, cot, weights, vecs, rows=256):
    T, D = x.shape
    FF = vecs[3].shape[1]
    blocks, ups = T // rows, FF // 2 // CW
    rb = lambda n: pl.BlockSpec((rows, n), lambda i, p: (jnp.minimum(i, blocks - 1), 0))
    full = lambda a: pl.BlockSpec(a.shape, lambda i, p: (0, 0))
    vec = lambda n: (pl.BlockSpec((1, n), lambda i, p: (0, 0)), jax.ShapeDtypeStruct((1, n), F32))
    vs = [vec(n) for n in (D, D, D, FF, D, D, D)]
    down = pl.BlockSpec(
        (2, 2, 1, FF // 16, CW), lambda i, p: (0, 0, jnp.clip(i - blocks, 0, LINE - 1), 0, 0)
    )
    up = pl.BlockSpec(
        (2, 2, LINE, 48, CW), lambda i, p: (0, 0, 0, 0, jnp.clip(i - blocks - LINE, 0, ups))
    )
    shapes = [(2, 2, LINE, FF // 16, CW)] * 2 + [(2, 2, LINE, 48, CW * (1 + ups))] * 2
    return pl.pallas_call(
        main_fetch_kernel,
        grid_spec=pltpu.PrefetchScalarGridSpec(
            num_scalar_prefetch=1,
            grid=(blocks + LINE + 1 + ups,),
            in_specs=[rb(a.shape[1]) for a in (*att, x, cot)]
            + [pl.BlockSpec(memory_space=pl.ANY)] * len(weights)
            + [full(v) for v in vecs],
            out_specs=[rb(D)] * 3 + [v[0] for v in vs] + [down, down, up, up],
            scratch_shapes=[
                pltpu.VMEM((rows, FF), F32),
                pltpu.VMEM((D, D), BF),
                pltpu.VMEM((D, FF), BF),
                pltpu.VMEM((FF, D), BF),
                pltpu.VMEM((2, T, FF), BF),
                pltpu.VMEM((4, T, D), BF),
                pltpu.VMEM((2, 16 * 48, CW), BF),
            ]
            + [pltpu.SemaphoreType.DMA] * 3,
        ),
        out_shape=[jax.ShapeDtypeStruct((T, D), t) for t in (BF, F32, BF)]
        + [v[1] for v in vs]
        + [jax.ShapeDtypeStruct(a, BF) for a in shapes],
        compiler_params=params(),
        cost_estimate=cost(58),
        name="main",
    )(pos, *att, x, cot, *weights, *vecs)


def main_plain_kernel(*refs):
    main_kernel(refs[:-28], *refs[-28:])


def main_kernel(att,x,cot,ow,uw,dw,ob,g1,s1,ub,db,g2,s2,
                lo_ref,act_ref,sl_ref,nl_ref,pl_ref,fl_ref,gf_ref,ga_ref,
                vg2,vs2,vdb,vub,vg1,vs1,vob,slope,ready=lambda place: None):
    i=pl.program_id(0)
    FF=uw.shape[1]
    ready(0)
    fs=x[...].astype(F32)+mm(joined(att),ow[...])+ob[...]
    fh,fi=norm(fs)
    normed=fh*g1[...]+s1[...]
    nl=normed.astype(BF); nl_ref[...]=nl
    acc=normed+db[...]
    ready(1)
    for j in range(0,FF,C):
        pre=mm(nl,uw[:,j:j+C])+ub[:,j:j+C]
        phi=0.5*(1.0+lax.erf(pre*(1.0/math.sqrt(2.0))))
        a=(pre*phi).astype(BF)
        act_ref[:,j:j+C]=a
        slope[:,j:j+C]=phi+pre*jnp.exp(-0.5*pre*pre)*(1.0/math.sqrt(2.0*math.pi))
        if j==0: ready(2)
        acc=acc+mm(a,dw[j:j+C,:])
    sh,si=norm(acc)
    lo_ref[...]=(sh*g2[...]+s2[...]).astype(BF)
    gr=cot[...].astype(F32)
    gs=norm_back(gr*g2[...],sh,si)
    sl=gs.astype(BF); sl_ref[...]=sl
    gn=gs
    ubs=[]
    for j in range(0,FF,C):
        gp=dg(sl,dw[j:j+C,:],NT)*slope[:,j:j+C]
        ubs.append(col(gp))
        gpl=gp.astype(BF); pl_ref[:,j:j+C]=gpl
        gn=gn+dg(gpl,uw[:,j:j+C],NT)
    gf=norm_back(gn*g1[...],fh,fi)
    fl=gf.astype(BF); fl_ref[...]=fl; gf_ref[...]=gf
    ga_ref[...]=dg(fl,ow[...],NT).astype(BF)
    vals=[(vg2,col(gr*sh)),(vs2,col(gr)),(vdb,col(gs)),(vub,jnp.concatenate(ubs,1)),(vg1,col(gn*fh)),(vs1,col(gn)),(vob,col(gf))]
    @pl.when(i==0)
    def _():
        for r,v in vals: r[...]=v
    @pl.when(i>0)
    def _():
        for r,v in vals: r[...]+=v
def main(att, x, cot, weights, vecs, R=256):
    T, D = x.shape
    FF = vecs[3].shape[1]
    rb = lambda n: pl.BlockSpec((R, n), lambda i: (i, 0))
    full = lambda a: pl.BlockSpec(a.shape, lambda i: (0, 0))
    sds = lambda n, t=BF: jax.ShapeDtypeStruct((T, n), t)
    vec = lambda n: (pl.BlockSpec((1, n), lambda i: (0, 0)), jax.ShapeDtypeStruct((1, n), F32))
    vs = [vec(n) for n in (D, D, D, FF, D, D, D)]
    return pl.pallas_call(
        main_plain_kernel,
        grid=(T // R,),
        in_specs=[rb(a.shape[1]) for a in (*att, x, cot)] + [full(w) for w in weights] + [full(v) for v in vecs],
        out_specs=[rb(D), rb(FF), rb(D), rb(D), rb(FF), rb(D), rb(D), rb(D)] + [v[0] for v in vs],
        out_shape=[sds(D), sds(FF), sds(D), sds(D), sds(FF), sds(D), sds(D, F32), sds(D)] + [v[1] for v in vs],
        scratch_shapes=[pltpu.VMEM((R, FF), F32)],
        compiler_params=params(),
        name="main",
    )(*att, x, cot, *weights, *vecs)


def tn_kernel(a,b,o): o[...]=dg(a[...],b[...],TN).astype(BF)
def tn(a,b,bm,bn):
    T,M=a.shape;N=b.shape[1]
    return pl.pallas_call(tn_kernel,grid=(M//bm,N//bn),
      in_specs=[pl.BlockSpec((T,bm),lambda i,j:(0,i)),pl.BlockSpec((T,bn),lambda i,j:(0,j))],
      out_specs=pl.BlockSpec((bm,bn),lambda i,j:(i,j)),out_shape=jax.ShapeDtypeStruct((M,N),BF),compiler_params=params())(a,b)
def ig_kernel(gf, parts, w, o):
    o[...] = (gf[...] + dg(joined(parts), w[...], NT)).astype(BF)


def ig_plain_kernel(gf, *refs):
    ig_kernel(gf, refs[:-2], refs[-2], refs[-1])


def ig_fetch_kernel(pos, gf, *refs):
    parts, buffers, (o, weight, sem) = refs[:-11], refs[-11:-3], refs[-3:]

    @pl.when(pl.program_id(0) == 0)
    def _():
        run_all(fetch_in(pos, buffers, weight, sem))

    ig_kernel(gf, parts, weight, o)


def ig(parts, gf, weights, pos=None, R=256):
    T, D = gf.shape
    rb = lambda n: pl.BlockSpec((R, n), lambda i, *p: (i, 0))
    fetched = pos is not None
    return pl.pallas_call(
        ig_fetch_kernel if fetched else ig_plain_kernel,
        grid_spec=pltpu.PrefetchScalarGridSpec(
            num_scalar_prefetch=1 if fetched else 0,
            grid=(T // R,),
            in_specs=[rb(a.shape[1]) for a in (gf, *parts)]
            + [pl.BlockSpec(memory_space=pl.ANY) if fetched else pl.BlockSpec(w.shape, lambda i, *p: (0, 0)) for w in weights],
            out_specs=rb(D),
            scratch_shapes=[pltpu.VMEM((D, 3 * D), BF), pltpu.SemaphoreType.DMA] if fetched else [],
        ),
        out_shape=jax.ShapeDtypeStruct((T, D), BF),
        compiler_params=params(),
        cost_estimate=cost(10),
        name="ig",
    )(*([pos] if fetched else []), gf, *parts, *weights)


def local(
    hidden_states,
    page_counts,
    cotangent,
    attn_in_weight,
    attn_in_bias,
    attn_out_weight,
    attn_out_bias,
    first_gain,
    first_shift,
    up_weight,
    up_bias,
    down_weight,
    down_bias,
    second_gain,
    second_shift,
):
    pages, length, model = hidden_states.shape
    hidden = up_weight.shape[1]
    x = hidden_states.reshape(-1, model)
    grad_rows = cotangent.reshape(-1, model)
    weights = (attn_in_weight, attn_out_weight, up_weight, down_weight)
    vectors = (
        attn_in_bias,
        attn_out_bias,
        first_gain,
        first_shift,
        up_bias,
        down_bias,
        second_gain,
        second_shift,
    )
    lined = lax.axis_size("fsdp") == 4 * LINE and lax.axis_size("rep") == 2
    pairs = HEADS // 2 // THIRDS
    forward = [None] * THIRDS
    backward = [None] * THIRDS

    def ahead(t, rows):
        forward[t] = attn_fwd(rows, page_counts, pages)

    def back(t, rows):
        backward[t] = attn_bwd(rows, page_counts, grad_att, *forward[t], pages, pairs * t)

    if lined:
        index = lax.axis_index("fsdp")
        pos = jnp.stack([index // 4, index // 2 % 2, index % 2, lax.axis_index("rep")]).astype(jnp.int32)
        one, two, three = pack(pos, weights, vectors)
        line_one = jnp.stack(along_line(one))
        second_one = move(line_one, to_second)
        first_one = move(line_one, to_first)
        parts_two = along_line(after(two, line_one))
        parts_three = along_line(after(three, line_one))
        both_one = move(after(second_one, *parts_two[1:]), to_first)
        in_w = over_core((line_one, first_one, second_one, both_one))
        line_two = jnp.stack(parts_two)
        second_two = move(line_two, to_second)
        first_two = move(line_two, to_first)
        outs = qkv_fetch(pos, x, after(in_w, line_two), 16)
        rows, full = outs[:THIRDS], outs[THIRDS:]
        line_three = jnp.stack(after(parts_three, rows))
        second_three = move(line_three, to_second)
        first_three = move(line_three, to_first)
        ahead(0, after(rows[0], line_three))
        both_two = move(after(second_two, forward[0]), to_first)
        ahead(1, after(rows[1], forward[0], second_two))
        both_three = move(after(second_three, forward[1]), to_first)
        ready = (line_two, first_two, second_two, line_three, first_three, second_three)
        ready = over_core(after(ready, forward[1]))
        ahead(2, after(rows[2], forward[1], second_three, first_three))
        last = over_core(after((both_two, both_three), forward[2]))
        later = (*ready[0:3], last[0], *ready[6:9], last[2], *ready[3:6], last[1], *ready[9:12], last[3])
    else:
        pos = None
        gathered = lambda a: lax.all_gather(a, "fsdp", axis=0, tiled=True)
        in_w = gathered(attn_in_weight).reshape(model, 3, -1, 128)
        in_w = (in_w.transpose(0, 2, 1, 3).reshape(model, 3 * model),)
        full = [gathered(v).astype(F32).reshape(1, -1) for v in vectors]
        later = tuple(gathered(w) for w in weights[1:])
        rows = qkv(x, in_w[0], pair_bias(full[0]))
        for t in range(THIRDS):
            ahead(t, rows[t])
    attended = [f[0] for f in forward]
    if lined:
        (
            output, grad_first, grad_att, vg2, vs2, vdb, vub, vg1, vs1, vob,
            keep_d, send_d, keep_u, send_u,
        ) = main_fetch(pos, attended, x, grad_rows, later, full[1:])
        core_d = move(send_d, to_core)
        core_u = move(send_u, to_core)
        back(0, rows[0])
        go_d, stay_d = add_wide(*after((keep_d, core_d), backward[0]))
        first_d = move(go_d, to_first)
        go_u, stay_u = add_wide(*after((keep_u, core_u), go_d))
        first_u = move(go_u, to_first)
        back(1, after(rows[1], go_u, stay_u))
        go_d, stay_d = add_core(*after((stay_d, first_d), backward[1]))
        second_d = move(go_d, to_second)
        keep_i, send_i = grad_in(pos, x, after((backward[0][0], backward[1][0]), go_d, stay_d))
        core_i = move(send_i, to_core)
        back(2, after(rows[2], keep_i))
        low_d = add_last(*after((stay_d, second_d), backward[2]))
        line_d = move_line(low_d)
        go_u, stay_u = add_core(*after((stay_u, first_u), low_d))
        second_u = move(go_u, to_second)
        parts = tuple(b[0] for b in backward)
        vbq = [b[1] for b in backward]
        vbv = [b[2] for b in backward]
        go_i, stay_i = add_wide(*after((keep_i, core_i), go_u, stay_u))
        first_i = move(go_i, to_first)
        keep_l, send_l = grad_last(
            pos, x, after(parts[2], go_i, stay_i), (*vbq, *vbv, vub, vob, vg1, vs1, vdb, vg2, vs2)
        )
        core_l = move(send_l, to_core)
        mine_d = add_line(low_d, after(line_d, keep_l))
        low_u = add_last(*after((stay_u, second_u), mine_d))
        line_u = move_line(low_u)
        go_l, stay_l = add_core(keep_l, after(core_l, low_u))
        first_l = move(go_l, to_first)
        go_i, stay_i = add_core(*after((stay_i, first_i), go_l, stay_l))
        second_i = move(go_i, to_second)
        input_grad = ig(parts, after(grad_first, go_i, stay_i), in_w, pos)
        mine_u = add_line(low_u, after(line_u, input_grad))
        low_i = add_last(*after((stay_i, second_i), mine_u))
        line_i = move_line(low_i)
        go_l, stay_l = add_core(*after((stay_l, first_l), low_i))
        second_l = move(go_l, to_second)
        got_d = move(after(mine_d, go_l), to_x)
        low_l = add_last(*after((stay_l, second_l), go_l))
        mine_i = add_line(low_i, after(line_i, low_l))
        line_l = move_line(after(low_l, mine_i))
        got_u = move(after(mine_u, mine_i), to_x)
        got_i = move(mine_i, to_x)
        (t_down,) = finish(
            finish_down_kernel, "finish_down", pos, (mine_d, after(got_d, low_l)), [down_weight.shape]
        )
        mine_l = add_line(low_l, after(line_l, t_down))
        got_l = move(mine_l, to_x)
        shapes = [attn_out_weight.shape, up_weight.shape, attn_in_weight.shape]
        shapes += [(1, v.shape[0]) for v in vectors]
        t_out, t_up, t_in, *small = finish(
            finish_kernel, "finish", pos, (mine_u, got_u, mine_i, got_i, mine_l, got_l), shapes
        )
        small = [b.reshape(-1) for b in small]
    else:
        (
            output, act, second_low, normed_low, pre_low, first_low, grad_first, grad_att,
            vg2, vs2, vdb, vub, vg1, vs1, vob,
        ) = main(attended, x, grad_rows, later, full[1:])
        for t in range(THIRDS):
            back(t, rows[t])
        parts = tuple(b[0] for b in backward)
        vbq = jnp.concatenate([b[1] for b in backward], axis=1)
        vbv = jnp.concatenate([b[2] for b in backward], axis=1)
        input_grad = ig(parts, grad_first, in_w)

        def total(a):
            share = lax.psum_scatter(a.astype(BF), "fsdp", scatter_dimension=0, tiled=True)
            return lax.psum(share, "rep").astype(F32)

        att = jnp.concatenate(attended, axis=1)
        t_down = total(tn(act, second_low, 768, 768))
        t_up = total(tn(normed_low, pre_low, 768, 768))
        t_out = total(tn(att, first_low, 768, 768))
        t_in = jnp.concatenate([tn(x, d, 768, 768) for d in parts], axis=1)
        t_in = total(t_in.reshape(model, -1, 3, 128).transpose(0, 2, 1, 3).reshape(model, 3 * model))
        small = [
            total(v.reshape(-1))
            for v in (jnp.concatenate([vbq, vbv], axis=1), vob, vg1, vs1, vub, vdb, vg2, vs2)
        ]
    b_in, b_out, b_g1, b_s1, b_up, b_down, b_g2, b_s2 = small
    return (
        output.reshape(hidden_states.shape),
        input_grad.reshape(hidden_states.shape),
        t_in, b_in, t_out, b_out, b_g1, b_s1, t_up, b_up, t_down, b_down, b_g2, b_s2,
    )


def solution(mesh):
    return jax.shard_map(
        local,
        mesh=mesh,
        in_specs=(
            P(("fsdp", "rep"), None, None),
            P(("fsdp", "rep")),
            P(("fsdp", "rep"), None, None),
            P("fsdp", None),
            P("fsdp"),
            P("fsdp", None),
            P("fsdp"),
            P("fsdp"),
            P("fsdp"),
            P("fsdp", None),
            P("fsdp"),
            P("fsdp", None),
            P("fsdp"),
            P("fsdp"),
            P("fsdp"),
        ),
        out_specs=(
            P(("fsdp", "rep"), None, None),
            P(("fsdp", "rep"), None, None),
            P("fsdp", None),
            P("fsdp"),
            P("fsdp", None),
            P("fsdp"),
            P("fsdp"),
            P("fsdp"),
            P("fsdp", None),
            P("fsdp"),
            P("fsdp", None),
            P("fsdp"),
            P("fsdp"),
            P("fsdp"),
        ),
        check_vma=False,
    )
```

```python
import math

import jax
import jax.numpy as jnp
from jax import lax
from jax.experimental import pallas as pl
from jax.experimental.pallas import tpu as pltpu
from jax.sharding import PartitionSpec as P

HEADS = 12
BF = jnp.bfloat16
F32 = jnp.float32
NT = (((1,), (1,)), ((), ()))
TN = (((0,), (0,)), ((), ()))
CW = 384
THIRDS = 3
LINE = 4
TINY = 128
AXES = ("fsdp", "rep")


def dg(a, b, dims):
    return lax.dot_general(a, b, dims, preferred_element_type=F32)


def mm(a, b):
    return jnp.dot(a, b, preferred_element_type=F32)


def params():
    return pltpu.CompilerParams(vmem_limit_bytes=60 * 1024 * 1024)


def cost(us):
    return pl.CostEstimate(flops=int(us * 1.15e9), bytes_accessed=int(us * 1e6), transcendentals=0)


def flat_index(z, y, c, x):
    return (z * 4 + y * 2 + c) * 2 + x


def permutation(target):
    pairs = []
    for z in range(LINE):
        for y in range(2):
            for c in range(2):
                for x in range(2):
                    pairs.append((flat_index(z, y, c, x), flat_index(*target(z, y, c, x))))
    return pairs


def to_core(z, y, c, x):
    return (z, y, 1 - c, x)


def to_x(z, y, c, x):
    return (z, y, c, 1 - x)


def to_first(z, y, c, x):
    return (z, y, c, 1 - x) if c == 0 else (z, 1 - y, c, x)


def to_second(z, y, c, x):
    return (z, 1 - y, c, x) if c == 0 else (z, y, c, 1 - x)


def to_line(step):
    return lambda z, y, c, x: ((z + step) % LINE, y, c, x)


def move(value, target):
    return lax.ppermute(value, AXES, permutation(target))


def after(values, *earlier):
    return lax.optimization_barrier((values, earlier))[0]


def along_line(half):
    return [half] + [move(half, to_line(k)) for k in range(1, LINE)]


def in_order(parts):
    here = lax.axis_index("fsdp") // 4
    return jnp.stack([lax.select_n((here - chip) & (LINE - 1), *parts) for chip in range(LINE)])


def over_core(parts):
    return tuple(parts) + tuple(move(part, to_core) for part in parts)


def add_core(keep, got):
    keep, got = keep.astype(F32), got.astype(F32)
    return (keep[1] + got[1]).astype(BF), (keep[0] + got[0]).astype(BF)


def add_kernel(keep, got, go, stay):
    total = keep[...].astype(F32) + got[...].astype(F32)
    stay[...] = total[0].astype(BF)
    go[...] = total[1].astype(BF)


def add_wide(keep, got):
    _, second, line, rows, width = keep.shape
    half = line // 2
    both = pl.BlockSpec((2, 1, half, rows, width), lambda i, j: (0, i, j, 0, 0))
    one = pl.BlockSpec((1, half, rows, width), lambda i, j: (i, j, 0, 0))
    return pl.pallas_call(
        add_kernel,
        grid=(second, 2),
        in_specs=[both, both],
        out_specs=[one, one],
        out_shape=[jax.ShapeDtypeStruct(keep.shape[1:], BF)] * 2,
        compiler_params=params(),
        cost_estimate=cost(4),
        name="add_wide",
    )(keep, got)


def add_last(stay, got):
    return (stay.astype(F32) + got.astype(F32)).astype(BF)


def add_line(low, parts):
    total = low[0].astype(F32)
    for part in parts:
        total = total + part.astype(F32)
    return total.astype(BF)


def move_line(low):
    return [move(low[k], to_line(k)) for k in range(1, LINE)]


FIELDS = (((0, 0, 96), (4, 1, 192)), tuple((n, i, 48) for i, n in enumerate((1, 2, 3, 5, 6, 7))))


def rows_of(width):
    return [(i, at, min(TINY, width - at)) for i, at in enumerate(range(0, width, TINY))]


def pack_kernel(pos, inw, outw, upw, downw, *refs):
    vectors, (one, two, three) = refs[:8], refs[8:]

    def fill(x):
        third = inw.shape[1] // 3
        for t in range(THIRDS):
            for part in range(3):
                start = part * third + (2 * t + x) * 128
                piece = inw[:, start : start + 128]
                one[:, t * CW + part * 128 : t * CW + (part + 1) * 128] = piece
        row = lax.broadcasted_iota(jnp.int32, (48, TINY), 0)
        block = jnp.zeros((48, TINY), F32)
        for place, top, size in FIELDS[x]:
            for i, at, n in rows_of(size):
                piece = vectors[place][:, at : at + n].astype(F32)
                if n < TINY:
                    piece = jnp.concatenate([piece, jnp.zeros((1, TINY - n), F32)], axis=1)
                block = jnp.where(row == top + i, jnp.broadcast_to(piece, (48, TINY)), block)
        one[:, THIRDS * CW :] = block.astype(BF)
        two[:, :CW] = outw[:, x * CW : (x + 1) * CW]
        width = upw.shape[1] // 2
        two[:, CW:] = upw[:, x * width : (x + 1) * width]
        three[...] = downw[:, x * CW : (x + 1) * CW]

    @pl.when(pos[3] == 0)
    def _():
        fill(0)

    @pl.when(pos[3] == 1)
    def _():
        fill(1)


def pack(pos, weights, vectors):
    shapes = [
        (48, weights[0].shape[1] // 2 + TINY),
        (48, weights[1].shape[1] // 2 + weights[2].shape[1] // 2),
        (weights[3].shape[0], CW),
    ]
    arrays = tuple(weights) + tuple(v.reshape(1, -1) for v in vectors)
    full = lambda a: pl.BlockSpec(a, lambda i, p: (0, 0))
    return pl.pallas_call(
        pack_kernel,
        grid_spec=pltpu.PrefetchScalarGridSpec(
            num_scalar_prefetch=1,
            grid=(1,),
            in_specs=[full(a.shape) for a in arrays],
            out_specs=[full(a) for a in shapes],
        ),
        out_shape=[jax.ShapeDtypeStruct(a, BF) for a in shapes],
        compiler_params=params(),
        name="pack",
    )(pos, *arrays)


def sources(pos):
    y, c, x = pos[1], pos[2], pos[3]
    found = []
    for other in range(2):
        core = c ^ 1 if other else c
        swap = core == 0
        for first in range(2):
            for second in range(2):
                dx = jnp.where(swap, first, second)
                dy = jnp.where(swap, second, first)
                found.append((other * 4 + second * 2 + first, (y ^ dy) * 2 + core, x ^ dx))
    return found


def fetch(pos, buffers, target, rows, column, width, sem, stride=None, start=0):
    stride = width if stride is None else stride
    return [
        pltpu.make_async_copy(
            buffers[buffer].at[:, :, pl.ds(column, width)],
            target.at[
                :,
                pl.ds(pl.multiple_of(place * rows, 16), rows),
                pl.ds(pl.multiple_of(start + x * stride, 128), width),
            ],
            sem,
        )
        for buffer, place, x in sources(pos)
    ]


def fetch_in(pos, buffers, target, sem):
    copies = []
    for t in range(THIRDS):
        copies += fetch(pos, buffers, target, 48, t * CW, CW, sem, None, 2 * CW * t)
    return copies


def fetch_tiny(pos, buffers, target, column, sem):
    return [
        pltpu.make_async_copy(
            buffers[buffer].at[:, pl.ds(0, 16), pl.ds(column, TINY)], target.at[x, :, place], sem
        )
        for buffer, place, x in sources(pos)
    ]


def flat(ref, start=0, width=None):
    width = ref.shape[-1] if width is None else width
    return ref[:, :, start : start + width].reshape(-1, width) if len(ref.shape) == 3 else ref[:, start : start + width]


def run_all(copies):
    for copy in copies:
        copy.start()
    for copy in copies:
        copy.wait()


def spots(length, size, axis):
    shape = (length, TINY) if axis == 0 else (TINY, length)
    entry = lax.broadcasted_iota(jnp.int32, shape, axis).astype(F32)
    lane = lax.broadcasted_iota(jnp.int32, shape, 1 - axis).astype(F32)
    inner = entry - jnp.floor((entry + 0.5) * (1.0 / size)) * size
    return [
        jnp.where((lane + at == inner) & (lane < n), 1.0, 0.0).astype(BF) for _, at, n in rows_of(size)
    ]


def owned(shards, length):
    size = length // shards
    start = lax.broadcasted_iota(jnp.int32, (shards, length), 0) * size
    entry = lax.broadcasted_iota(jnp.int32, (shards, length), 1)
    return (entry >= start) & (entry < start + size)


def unpack_vectors(tiny, targets):
    shards = tiny.shape[1] * tiny.shape[2]
    made = {}
    for half in range(2):
        for place, top, size in FIELDS[half]:
            total = shards * size
            if size not in made:
                made[size] = spots(total, size, 1), owned(shards, total)
            each, mask = made[size]
            tiled = sum(mm(tiny[half, :, :, top + i, :].reshape(shards, TINY), spot) for i, spot in enumerate(each))
            targets[place][...] = jnp.sum(jnp.where(mask, tiled, 0.0), axis=0, keepdims=True)


def place_tile(pos, held, keep, send, rows, line):
    z, y, c, x = pos[0], pos[1], pos[2], pos[3]
    for relative, out in enumerate((keep, send)):
        core = c ^ relative
        swap = core == 0
        for first in range(2):
            for second in range(2):
                dx = jnp.where(swap, first, second)
                dy = jnp.where(swap, second, first)
                for slot, chip in line:
                    shard = chip * 4 + (y ^ dy) * 2 + core
                    start = pl.multiple_of(shard * rows, 16)
                    out[first, second, slot] = held[x ^ dx, pl.ds(start, rows), :]


def whole_line(pos):
    return [(k, (pos[0] + k) & (LINE - 1)) for k in range(LINE)]


def hold(held, tile):
    width = tile.shape[1] // 2
    held[0] = tile[:, :width].astype(BF)
    held[1] = tile[:, width:].astype(BF)


def joined(refs):
    return jnp.concatenate([r[...] for r in refs], axis=1)


def tiny_rows(vectors, fields):
    rows = []
    made = {}
    for vector, (_, _, size) in zip(vectors, fields):
        length = vector.shape[1]
        if size not in made:
            made[size] = spots(length, size, 0), owned(16, length)
        each, mask = made[size]
        own = jnp.where(mask, jnp.broadcast_to(vector, mask.shape), 0.0).astype(BF)
        rows += [mm(own, spot) for spot in each]
    count = len(rows)
    rows = jnp.concatenate(rows + [jnp.zeros((16 * (8 - count), TINY), F32)], axis=0).astype(BF)
    to = lax.broadcasted_iota(jnp.int32, (16 * 48, 128), 0)
    of = lax.broadcasted_iota(jnp.int32, (16 * 48, 128), 1)
    lift = jnp.where(to == (of & 15) * 48 + (of >> 4), 1.0, 0.0).astype(BF)
    return mm(lift, rows).astype(BF)


def grad_in_kernel(pos, x, *refs):
    parts, (keep, send, held) = refs[:-3], refs[-3:]
    for i, ref in enumerate(parts):

        @pl.when(pl.program_id(0) == i)
        def _(ref=ref):
            hold(held, dg(x[...], ref[...], TN))

    place_tile(pos, held, keep, send, 48, whole_line(pos))


def grad_last_kernel(pos, x, part, *refs):
    bq, bv, refs = refs[:THIRDS], refs[THIRDS : 2 * THIRDS], refs[2 * THIRDS :]
    upb, outb, g1, s1, downb, g2, s2, keep, send, held = refs
    hold(held, dg(x[...], part[...], TN))
    take = lambda ref: ref.at[:, :, :, :, pl.ds(0, CW)]
    place_tile(pos, held, take(keep), take(send), 48, whole_line(pos))
    groups = ((joined((*bq, *bv)), upb[...]), [r[...] for r in (outb, g1, s1, downb, g2, s2)])
    for half in range(2):
        held[half, :, :TINY] = tiny_rows(groups[half], FIELDS[half])
    take = lambda ref: ref.at[:, :, :, :, pl.ds(CW, TINY)]
    place_tile(pos, held.at[:, :, pl.ds(0, TINY)], take(keep), take(send), 48, whole_line(pos))


def grad_call(kernel, name, pos, arrays, in_specs, grid, block, shape, index, us):
    held = (2, 16 * 48, CW)
    return pl.pallas_call(
        kernel,
        grid_spec=pltpu.PrefetchScalarGridSpec(
            num_scalar_prefetch=1,
            grid=(grid,),
            in_specs=in_specs,
            out_specs=[pl.BlockSpec(block, index)] * 2,
            scratch_shapes=[pltpu.VMEM(held, BF)],
        ),
        out_shape=[jax.ShapeDtypeStruct(shape, BF)] * 2,
        compiler_params=params(),
        cost_estimate=cost(us),
        name=name,
    )(pos, *arrays)


def whole(array):
    return pl.BlockSpec(array.shape, lambda j, p: (0,) * array.ndim)


def grad_in(pos, x, parts):
    return grad_call(
        grad_in_kernel, "grad_in", pos, (x, *parts), [whole(a) for a in (x, *parts)], len(parts),
        (2, 2, LINE, 48, CW), (2, 2, LINE, 48, CW * len(parts)), lambda j, p: (0, 0, 0, 0, j), 5,
    )


def grad_last(pos, x, part, vectors):
    arrays = (x, part, *vectors)
    shape = (2, 2, LINE, 48, CW + TINY)
    return grad_call(
        grad_last_kernel, "grad_last", pos, arrays, [whole(a) for a in arrays], 1,
        shape, shape, lambda j, p: (0, 0, 0, 0, 0), 4,
    )


def halves(pos, mine, got):
    swap = pos[3] == 0
    return jnp.where(swap, mine, got).astype(F32), jnp.where(swap, got, mine).astype(F32)


def finish_down_kernel(pos, mine, got, down):
    for x, half in enumerate(halves(pos, mine[...], got[...])):
        down[:, CW * x : CW * (x + 1)] = half


def finish_kernel(pos, mine_u, got_u, mine, got, mine_last, got_last, out, up, weight, *vectors):
    width = up.shape[1] // 2
    third = weight.shape[1] // 3
    for x, half in enumerate(halves(pos, mine_u[...], got_u[...])):
        out[:, CW * x : CW * (x + 1)] = half[:, :CW]
        up[:, width * x : width * (x + 1)] = half[:, CW:]
    more = halves(pos, mine[...], got[...])
    for x, last in enumerate(halves(pos, mine_last[...], got_last[...])):
        for t in range(THIRDS):
            for part in range(3):
                start = part * third + (2 * t + x) * 128
                if t < THIRDS - 1:
                    piece = more[x][:, t * CW + part * 128 : t * CW + (part + 1) * 128]
                else:
                    piece = last[:, part * 128 : (part + 1) * 128]
                weight[:, start : start + 128] = piece
        for place, top, size in FIELDS[x]:
            for i, at, n in rows_of(size):
                vectors[place][:, at : at + n] = last[top + i : top + i + 1, CW : CW + n]


def finish(kernel, name, pos, sums, shapes):
    full = lambda shape: pl.BlockSpec(shape, lambda i, p: (0, 0))
    return pl.pallas_call(
        kernel,
        grid_spec=pltpu.PrefetchScalarGridSpec(
            num_scalar_prefetch=1,
            grid=(1,),
            in_specs=[full(a.shape) for a in sums],
            out_specs=[full(shape) for shape in shapes],
        ),
        out_shape=[jax.ShapeDtypeStruct(shape, F32) for shape in shapes],
        compiler_params=params(),
        name=name,
    )(pos, *sums)


def pair_bias(bias):
    model = bias.shape[1] // 2
    parts = []
    for pair in range(model // 128):
        at = pair * 128
        parts += [bias[:, at : at + 128], jnp.zeros((1, 128), F32), bias[:, model + at : model + at + 128]]
    return jnp.concatenate(parts, axis=1)


def qkv_rows(x, weight, bias, outs):
    y = mm(x[...], flat(weight))
    scale = 1.0 / math.sqrt(x.shape[1] // HEADS)
    for t, out in enumerate(outs):
        width = out.shape[1]
        for at in range(0, width, 128):
            here = y[:, t * width + at : t * width + at + 128]
            place = t * width + at
            if at // 128 % 3 != 1:
                here = here + bias[:, place : place + 128]
            here = here.astype(BF)
            out[:, at : at + 128] = here * jnp.asarray(scale, BF) if at // 128 % 3 == 0 else here


def qkv_fetch_kernel(pos, x, *refs):
    buffers, outs, refs = refs[:8], refs[8 : 8 + THIRDS], refs[8 + THIRDS :]
    vectors, (weight, tiny, bias, sem, sem_tiny) = refs[:8], refs[8:]

    @pl.when(pl.program_id(0) == 0)
    def _():
        copies = fetch_in(pos, buffers, weight, sem)
        small = fetch_tiny(pos, buffers, tiny, THIRDS * CW, sem_tiny)
        for copy in small + copies:
            copy.start()
        for copy in small:
            copy.wait()
        unpack_vectors(tiny, vectors)
        bias[...] = pair_bias(vectors[0][...])
        for copy in copies:
            copy.wait()

    qkv_rows(x, weight, bias, outs)


def qkv_fetch(pos, x, buffers, shards, block=256):
    tokens, model = x.shape
    vec = lambda n: (pl.BlockSpec((1, n), lambda i, p: (0, 0)), jax.ShapeDtypeStruct((1, n), F32))
    vecs = [vec(model * n) for n in (2, 1, 1, 1, 4, 1, 1, 1)]
    return pl.pallas_call(
        qkv_fetch_kernel,
        grid_spec=pltpu.PrefetchScalarGridSpec(
            num_scalar_prefetch=1,
            grid=(tokens // block,),
            in_specs=[pl.BlockSpec((block, model), lambda i, p: (i, 0))]
            + [pl.BlockSpec(memory_space=pl.ANY)] * 8,
            out_specs=[pl.BlockSpec((block, 2 * CW), lambda i, p: (i, 0))] * THIRDS + [v[0] for v in vecs],
            scratch_shapes=[
                pltpu.VMEM((LINE, model // LINE, 3 * model), BF),
                pltpu.VMEM((2, LINE, shards // LINE, 16, TINY), BF),
                pltpu.VMEM((1, 3 * model), F32),
                pltpu.SemaphoreType.DMA,
                pltpu.SemaphoreType.DMA,
            ],
        ),
        out_shape=[jax.ShapeDtypeStruct((tokens, 2 * CW), BF)] * THIRDS + [v[1] for v in vecs],
        compiler_params=params(),
        cost_estimate=cost(10),
        name="qkv_fetch",
    )(pos, x, *buffers)


def qkv_plain_kernel(x, weight, bias, *outs):
    qkv_rows(x, weight, bias, outs)


def qkv(x, weight, bias, block=256):
    tokens, model = x.shape
    full = lambda a: pl.BlockSpec(a.shape, lambda i: (0, 0))
    return pl.pallas_call(
        qkv_plain_kernel,
        grid=(tokens // block,),
        in_specs=[pl.BlockSpec((block, model), lambda i: (i, 0)), full(weight), full(bias)],
        out_specs=[pl.BlockSpec((block, 2 * CW), lambda i: (i, 0))] * THIRDS,
        out_shape=[jax.ShapeDtypeStruct((tokens, 2 * CW), BF)] * THIRDS,
        compiler_params=params(),
    )(x, weight, bias)


def aug(q,k,h,bias,lane):
    own=(lane>=64) if h else (lane<64)
    j0=0 if h else 64
    z=jnp.zeros_like(q)
    one=jnp.where(lane==j0,jnp.ones_like(q),z)
    qa=jnp.where(own,q,one)
    ka=jnp.where(own,k,jnp.where(lane==j0,bias,z))
    return qa,ka,own
def attn_fwd_kernel(cnt,q_ref,k_ref,v_ref,o_ref,l_ref):
    p=pl.program_id(0)
    q=q_ref[...];k=k_ref[...];v=v_ref[...]
    S=q.shape[0]
    lane=lax.broadcasted_iota(jnp.int32,q.shape,1)
    row=lax.broadcasted_iota(jnp.int32,q.shape,0)
    bias=jnp.where(row<cnt[p],0.0,-1e30).astype(BF)
    vt=v.T
    outs=[]
    for h in range(2):
        qa,ka,own=aug(q,k,h,bias,lane)
        s=dg(ka,qa,NT)
        m=jnp.max(s,axis=0,keepdims=True)
        e=jnp.exp(s-m)
        l=jnp.sum(e,axis=0,keepdims=True)
        ot=mm(vt[64*h:64*h+64],e.astype(BF))
        outs.append(ot*(1.0/l))
        l_ref[0,0,h:h+1,:]=m+jnp.log(l)
    o_ref[...]=jnp.concatenate(outs,axis=0).T.astype(BF)
def attn_fwd(rows, counts, pages):
    tokens, width = rows.shape
    length, pairs = tokens // pages, width // CW
    block = lambda o: pl.BlockSpec((length, 128), lambda p, h, c: (p, 3 * h + o))
    return pl.pallas_call(
        attn_fwd_kernel,
        grid_spec=pltpu.PrefetchScalarGridSpec(
            num_scalar_prefetch=1,
            grid=(pages, pairs),
            in_specs=[block(0), block(1), block(2)],
            out_specs=[
                pl.BlockSpec((length, 128), lambda p, h, c: (p, h)),
                pl.BlockSpec((1, 1, 2, length), lambda p, h, c: (p, h, 0, 0)),
            ],
        ),
        out_shape=[
            jax.ShapeDtypeStruct((tokens, pairs * 128), BF),
            jax.ShapeDtypeStruct((pages, pairs, 2, length), F32),
        ],
        compiler_params=params(),
        cost_estimate=cost(3.5 * pairs),
        name="attn_fwd",
    )(counts, rows, rows, rows)


def attn_bwd_kernel(cnt,q_ref,k_ref,v_ref,g_ref,o_ref,l_ref,d_ref,bq_ref,bv_ref):
    p=pl.program_id(1)
    q=q_ref[...];k=k_ref[...];v=v_ref[...];g=g_ref[...]
    lane=lax.broadcasted_iota(jnp.int32,q.shape,1)
    row=lax.broadcasted_iota(jnp.int32,q.shape,0)
    bias=jnp.where(row<cnt[p],0.0,-1e30).astype(BF)
    prod=g.astype(F32)*o_ref[...].astype(F32)
    hi=prod.astype(BF); lo=(prod-hi.astype(F32)).astype(BF)
    r8=lax.broadcasted_iota(jnp.int32,(16,128),0); l8=lax.broadcasted_iota(jnp.int32,(16,128),1)
    sel=jnp.where(r8==l8//64,1.0,0.0).astype(BF)
    delta=dg(sel,hi,NT)+dg(sel,lo,NT)
    kt=k.T
    dv=[];dk=[];dqt=[]
    for h in range(2):
        qa,ka,own=aug(q,k,h,bias,lane)
        s=dg(ka,qa,NT)
        pr=jnp.exp(s-l_ref[0,0,h:h+1,:])
        va=jnp.where(own,v,jnp.zeros_like(v))
        dp=dg(va,g,NT)
        ds=(pr*(dp-delta[h:h+1])).astype(BF)
        dv.append(mm(pr.astype(BF),g)); dk.append(mm(ds,q))
        dqt.append(mm(kt[64*h:64*h+64],ds))
    first=lane<64
    dvv=jnp.where(first,dv[0],dv[1])
    dq=jnp.concatenate(dqt,axis=0).T*0.125
    d_ref[:,:128]=dq.astype(BF); d_ref[:,256:]=dvv.astype(BF)
    d_ref[:,128:256]=jnp.where(first,dk[0],dk[1]).astype(BF)
    sq=jnp.sum(dq,axis=0,keepdims=True); sv=jnp.sum(dvv,axis=0,keepdims=True)
    @pl.when(p==0)
    def _():
        bq_ref[...]=sq; bv_ref[...]=sv
    @pl.when(p>0)
    def _():
        bq_ref[...]+=sq; bv_ref[...]+=sv
def attn_bwd(rows, counts, grad, out, totals, pages, at):
    tokens, width = rows.shape
    length, pairs = tokens // pages, width // CW
    block = lambda o: pl.BlockSpec((length, 128), lambda h, p, c: (p, 3 * h + o))
    line = pl.BlockSpec((1, 128), lambda h, p, c: (0, h))
    return pl.pallas_call(
        attn_bwd_kernel,
        grid_spec=pltpu.PrefetchScalarGridSpec(
            num_scalar_prefetch=1,
            grid=(pairs, pages),
            in_specs=[
                block(0),
                block(1),
                block(2),
                pl.BlockSpec((length, 128), lambda h, p, c: (p, h + at)),
                pl.BlockSpec((length, 128), lambda h, p, c: (p, h)),
                pl.BlockSpec((1, 1, 2, length), lambda h, p, c: (p, h, 0, 0)),
            ],
            out_specs=[pl.BlockSpec((length, CW), lambda h, p, c: (p, h))] + [line] * 2,
        ),
        out_shape=[jax.ShapeDtypeStruct((tokens, width), BF)]
        + [jax.ShapeDtypeStruct((1, pairs * 128), F32)] * 2,
        compiler_params=params(),
        cost_estimate=cost(4.5 * pairs),
        name="attn_bwd",
    )(counts, rows, rows, rows, grad, out, totals)


def norm(t):
    m=jnp.mean(t,axis=-1,keepdims=True); c=t-m
    v=jnp.mean(c*c,axis=-1,keepdims=True); inv=lax.rsqrt(v+1e-12)
    return c*inv,inv
def norm_back(e,hat,inv):
    return inv*(e-jnp.mean(e,axis=-1,keepdims=True)-hat*jnp.mean(e*hat,axis=-1,keepdims=True))
def col(t): return jnp.sum(t,axis=0,keepdims=True)
C=768
def rows_at(ref, start, count):
    if len(ref.shape) == 2:
        return ref[start : start + count, :]
    each = ref.shape[1]
    return ref[start // each, start % each : start % each + count, :]


def main_fetch_kernel(pos, *refs):
    att, (x, cot), refs = refs[:-49], refs[-49:-47], refs[-47:]
    two, three, refs = refs[:8], refs[8:16], refs[16:]
    vecs, (out, gf, ga), sums, refs = refs[:7], refs[7:10], refs[10:17], refs[17:]
    keep_d, send_d, keep_u, send_u, refs = *refs[:4], refs[4:]
    slope, ow, uw, dw, big, wide, held, *sems = refs
    act, pre = big.at[0], big.at[1]
    low, back, first, attended = (wide.at[n] for n in range(4))
    step = pl.program_id(0)
    rows = x.shape[0]
    blocks = act.shape[0] // rows
    copies = (
        fetch(pos, two, ow, 48, 0, CW, sems[0]),
        fetch(pos, two, uw, 48, CW, uw.shape[2] // 2, sems[1]),
        fetch(pos, three, dw, dw.shape[1] // 4, 0, CW, sems[2]),
    )

    @pl.when(step == 0)
    def _():
        for group in copies:
            for copy in group:
                copy.start()

    def ready(place):
        @pl.when(step == 0)
        def _():
            for copy in copies[place]:
                copy.wait()

    @pl.when(step < blocks)
    def _():
        here = pl.ds(pl.multiple_of(step * rows, 16), rows)
        attended[here, :] = joined(att)
        main_kernel(
            att, x, cot, ow, uw, dw, *vecs, out,
            act.at[here, :], back.at[here, :], low.at[here, :], pre.at[here, :], first.at[here, :],
            gf, ga, *sums, slope, ready,
        )

    @pl.when((step >= blocks) & (step < blocks + LINE))
    def _():
        chip = (pos[0] + step - blocks) & (LINE - 1)
        columns = act.shape[1] // LINE
        here = pl.ds(pl.multiple_of(chip * columns, 128), columns)
        hold(held, dg(act[:, here], back[...], TN))
        place_tile(pos, held, keep_d, send_d, held.shape[1] // 4, [(0, 0)])

    @pl.when(step == blocks + LINE)
    def _():
        hold(held, dg(attended[...], first[...], TN))
        place_tile(pos, held, keep_u, send_u, 48, whole_line(pos))

    @pl.when(step > blocks + LINE)
    def _():
        at = pl.multiple_of((step - blocks - LINE - 1) * CW, 128)
        right = pl.multiple_of(at + pre.shape[1] // 2, 128)
        columns = jnp.concatenate([pre[:, pl.ds(at, CW)], pre[:, pl.ds(right, CW)]], axis=1)
        hold(held, dg(low[...], columns, TN))
        place_tile(pos, held, keep_u, send_u, 48, whole_line(pos))


def main_fetch(pos, att, x, cot, weights, vecs, rows=512):
    T, D = x.shape
    FF = vecs[3].shape[1]
    blocks, ups = T // rows, FF // 2 // CW
    rb = lambda n: pl.BlockSpec((rows, n), lambda i, p: (jnp.minimum(i, blocks - 1), 0))
    full = lambda a: pl.BlockSpec(a.shape, lambda i, p: (0, 0))
    vec = lambda n: (pl.BlockSpec((1, n), lambda i, p: (0, 0)), jax.ShapeDtypeStruct((1, n), F32))
    vs = [vec(n) for n in (D, D, D, FF, D, D, D)]
    down = pl.BlockSpec(
        (2, 2, 1, FF // 16, CW), lambda i, p: (0, 0, jnp.clip(i - blocks, 0, LINE - 1), 0, 0)
    )
    up = pl.BlockSpec(
        (2, 2, LINE, 48, CW), lambda i, p: (0, 0, 0, 0, jnp.clip(i - blocks - LINE, 0, ups))
    )
    shapes = [(2, 2, LINE, FF // 16, CW)] * 2 + [(2, 2, LINE, 48, CW * (1 + ups))] * 2
    return pl.pallas_call(
        main_fetch_kernel,
        grid_spec=pltpu.PrefetchScalarGridSpec(
            num_scalar_prefetch=1,
            grid=(blocks + LINE + 1 + ups,),
            in_specs=[rb(a.shape[1]) for a in (*att, x, cot)]
            + [pl.BlockSpec(memory_space=pl.ANY)] * len(weights)
            + [full(v) for v in vecs],
            out_specs=[rb(D)] * 3 + [v[0] for v in vs] + [down, down, up, up],
            scratch_shapes=[
                pltpu.VMEM((rows, FF), BF),
                pltpu.VMEM((LINE, D // LINE, D), BF),
                pltpu.VMEM((LINE, D // LINE, FF), BF),
                pltpu.VMEM((LINE, FF // LINE, D), BF),
                pltpu.VMEM((2, T, FF), BF),
                pltpu.VMEM((4, T, D), BF),
                pltpu.VMEM((2, 16 * 48, CW), BF),
            ]
            + [pltpu.SemaphoreType.DMA] * 3,
        ),
        out_shape=[jax.ShapeDtypeStruct((T, D), t) for t in (BF, F32, BF)]
        + [v[1] for v in vs]
        + [jax.ShapeDtypeStruct(a, BF) for a in shapes],
        compiler_params=params(),
        cost_estimate=cost(58),
        name="main",
    )(pos, *att, x, cot, *weights, *vecs)


def main_plain_kernel(*refs):
    main_kernel(refs[:-28], *refs[-28:])


def main_kernel(att,x,cot,ow,uw,dw,ob,g1,s1,ub,db,g2,s2,
                lo_ref,act_ref,sl_ref,nl_ref,pl_ref,fl_ref,gf_ref,ga_ref,
                vg2,vs2,vdb,vub,vg1,vs1,vob,slope,ready=lambda place: None):
    i=pl.program_id(0)
    FF=uw.shape[-1]
    ready(0)
    fs=x[...].astype(F32)+mm(joined(att),flat(ow))+ob[...]
    fh,fi=norm(fs)
    normed=fh*g1[...]+s1[...]
    nl=normed.astype(BF); nl_ref[...]=nl
    acc=normed+db[...]
    ready(1)
    for j in range(0,FF,C):
        pre=mm(nl,flat(uw,j,C))+ub[:,j:j+C]
        phi=0.5*(1.0+lax.erf(pre*(1.0/math.sqrt(2.0))))
        a=(pre*phi).astype(BF)
        act_ref[:,j:j+C]=a
        slope[:,j:j+C]=(phi+pre*jnp.exp(-0.5*pre*pre)*(1.0/math.sqrt(2.0*math.pi))).astype(slope.dtype)
        if j==0: ready(2)
        acc=acc+mm(a,rows_at(dw,j,C))
    sh,si=norm(acc)
    lo_ref[...]=(sh*g2[...]+s2[...]).astype(BF)
    gr=cot[...].astype(F32)
    gs=norm_back(gr*g2[...],sh,si)
    sl=gs.astype(BF); sl_ref[...]=sl
    gn=gs
    ubs=[]
    for j in range(0,FF,C):
        gp=dg(sl,rows_at(dw,j,C),NT)*slope[:,j:j+C]
        ubs.append(col(gp))
        gpl=gp.astype(BF); pl_ref[:,j:j+C]=gpl
        gn=gn+dg(gpl,flat(uw,j,C),NT)
    gf=norm_back(gn*g1[...],fh,fi)
    fl=gf.astype(BF); fl_ref[...]=fl; gf_ref[...]=gf
    ga_ref[...]=dg(fl,flat(ow),NT).astype(BF)
    vals=[(vg2,col(gr*sh)),(vs2,col(gr)),(vdb,col(gs)),(vub,jnp.concatenate(ubs,1)),(vg1,col(gn*fh)),(vs1,col(gn)),(vob,col(gf))]
    @pl.when(i==0)
    def _():
        for r,v in vals: r[...]=v
    @pl.when(i>0)
    def _():
        for r,v in vals: r[...]+=v
def main(att, x, cot, weights, vecs, R=256):
    T, D = x.shape
    FF = vecs[3].shape[1]
    rb = lambda n: pl.BlockSpec((R, n), lambda i: (i, 0))
    full = lambda a: pl.BlockSpec(a.shape, lambda i: (0, 0))
    sds = lambda n, t=BF: jax.ShapeDtypeStruct((T, n), t)
    vec = lambda n: (pl.BlockSpec((1, n), lambda i: (0, 0)), jax.ShapeDtypeStruct((1, n), F32))
    vs = [vec(n) for n in (D, D, D, FF, D, D, D)]
    return pl.pallas_call(
        main_plain_kernel,
        grid=(T // R,),
        in_specs=[rb(a.shape[1]) for a in (*att, x, cot)] + [full(w) for w in weights] + [full(v) for v in vecs],
        out_specs=[rb(D), rb(FF), rb(D), rb(D), rb(FF), rb(D), rb(D), rb(D)] + [v[0] for v in vs],
        out_shape=[sds(D), sds(FF), sds(D), sds(D), sds(FF), sds(D), sds(D, F32), sds(D)] + [v[1] for v in vs],
        scratch_shapes=[pltpu.VMEM((R, FF), F32)],
        compiler_params=params(),
        name="main",
    )(*att, x, cot, *weights, *vecs)


def tn_kernel(a,b,o): o[...]=dg(a[...],b[...],TN).astype(BF)
def tn(a,b,bm,bn):
    T,M=a.shape;N=b.shape[1]
    return pl.pallas_call(tn_kernel,grid=(M//bm,N//bn),
      in_specs=[pl.BlockSpec((T,bm),lambda i,j:(0,i)),pl.BlockSpec((T,bn),lambda i,j:(0,j))],
      out_specs=pl.BlockSpec((bm,bn),lambda i,j:(i,j)),out_shape=jax.ShapeDtypeStruct((M,N),BF),compiler_params=params())(a,b)
def ig_kernel(gf, parts, w, o):
    o[...] = (gf[...] + dg(joined(parts), flat(w), NT)).astype(BF)


def ig_plain_kernel(gf, *refs):
    ig_kernel(gf, refs[:-2], refs[-2], refs[-1])


def ig_fetch_kernel(pos, gf, *refs):
    parts, buffers, (o, weight, sem) = refs[:-11], refs[-11:-3], refs[-3:]

    @pl.when(pl.program_id(0) == 0)
    def _():
        run_all(fetch_in(pos, buffers, weight, sem))

    ig_kernel(gf, parts, weight, o)


def ig(parts, gf, weights, pos=None, R=256):
    T, D = gf.shape
    rb = lambda n: pl.BlockSpec((R, n), lambda i, *p: (i, 0))
    fetched = pos is not None
    return pl.pallas_call(
        ig_fetch_kernel if fetched else ig_plain_kernel,
        grid_spec=pltpu.PrefetchScalarGridSpec(
            num_scalar_prefetch=1 if fetched else 0,
            grid=(T // R,),
            in_specs=[rb(a.shape[1]) for a in (gf, *parts)]
            + [pl.BlockSpec(memory_space=pl.ANY) if fetched else pl.BlockSpec(w.shape, lambda i, *p: (0, 0)) for w in weights],
            out_specs=rb(D),
            scratch_shapes=[pltpu.VMEM((LINE, D // LINE, 3 * D), BF), pltpu.SemaphoreType.DMA] if fetched else [],
        ),
        out_shape=jax.ShapeDtypeStruct((T, D), BF),
        compiler_params=params(),
        cost_estimate=cost(10),
        name="ig",
    )(*([pos] if fetched else []), gf, *parts, *weights)


def local(
    hidden_states,
    page_counts,
    cotangent,
    attn_in_weight,
    attn_in_bias,
    attn_out_weight,
    attn_out_bias,
    first_gain,
    first_shift,
    up_weight,
    up_bias,
    down_weight,
    down_bias,
    second_gain,
    second_shift,
):
    pages, length, model = hidden_states.shape
    hidden = up_weight.shape[1]
    x = hidden_states.reshape(-1, model)
    grad_rows = cotangent.reshape(-1, model)
    weights = (attn_in_weight, attn_out_weight, up_weight, down_weight)
    vectors = (
        attn_in_bias,
        attn_out_bias,
        first_gain,
        first_shift,
        up_bias,
        down_bias,
        second_gain,
        second_shift,
    )
    lined = lax.axis_size("fsdp") == 4 * LINE and lax.axis_size("rep") == 2
    pairs = HEADS // 2 // THIRDS
    forward = [None] * THIRDS
    backward = [None] * THIRDS

    def ahead(t, rows):
        forward[t] = attn_fwd(rows, page_counts, pages)

    def back(t, rows):
        backward[t] = attn_bwd(rows, page_counts, grad_att, *forward[t], pages, pairs * t)

    if lined:
        index = lax.axis_index("fsdp")
        pos = jnp.stack([index // 4, index // 2 % 2, index % 2, lax.axis_index("rep")]).astype(jnp.int32)
        one, two, three = pack(pos, weights, vectors)
        line_one = in_order(along_line(one))
        second_one = move(line_one, to_second)
        first_one = move(line_one, to_first)
        parts_two = along_line(after(two, line_one))
        parts_three = along_line(after(three, line_one))
        both_one = move(after(second_one, *parts_two[1:]), to_first)
        in_w = over_core((line_one, first_one, second_one, both_one))
        line_two = in_order(parts_two)
        second_two = move(line_two, to_second)
        first_two = move(line_two, to_first)
        outs = qkv_fetch(pos, x, after(in_w, line_two), 16)
        rows, full = outs[:THIRDS], outs[THIRDS:]
        line_three = in_order(after(parts_three, rows))
        second_three = move(line_three, to_second)
        first_three = move(line_three, to_first)
        ahead(0, after(rows[0], line_three))
        both_two = move(after(second_two, forward[0]), to_first)
        ahead(1, after(rows[1], forward[0], second_two))
        both_three = move(after(second_three, forward[1]), to_first)
        ready = (line_two, first_two, second_two, line_three, first_three, second_three)
        ready = over_core(after(ready, forward[1]))
        ahead(2, after(rows[2], forward[1], second_three, first_three))
        last = over_core(after((both_two, both_three), forward[2]))
        later = (*ready[0:3], last[0], *ready[6:9], last[2], *ready[3:6], last[1], *ready[9:12], last[3])
    else:
        pos = None
        gathered = lambda a: lax.all_gather(a, "fsdp", axis=0, tiled=True)
        in_w = gathered(attn_in_weight).reshape(model, 3, -1, 128)
        in_w = (in_w.transpose(0, 2, 1, 3).reshape(model, 3 * model),)
        full = [gathered(v).astype(F32).reshape(1, -1) for v in vectors]
        later = tuple(gathered(w) for w in weights[1:])
        rows = qkv(x, in_w[0], pair_bias(full[0]))
        for t in range(THIRDS):
            ahead(t, rows[t])
    attended = [f[0] for f in forward]
    if lined:
        (
            output, grad_first, grad_att, vg2, vs2, vdb, vub, vg1, vs1, vob,
            keep_d, send_d, keep_u, send_u,
        ) = main_fetch(pos, attended, x, grad_rows, later, full[1:])
        core_d = move(send_d, to_core)
        core_u = move(send_u, to_core)
        back(0, rows[0])
        go_d, stay_d = add_wide(*after((keep_d, core_d), backward[0]))
        first_d = move(go_d, to_first)
        go_u, stay_u = add_wide(*after((keep_u, core_u), go_d))
        first_u = move(go_u, to_first)
        back(1, after(rows[1], go_u, stay_u))
        go_d, stay_d = add_core(*after((stay_d, first_d), backward[1]))
        second_d = move(go_d, to_second)
        keep_i, send_i = grad_in(pos, x, after((backward[0][0], backward[1][0]), go_d, stay_d))
        core_i = move(send_i, to_core)
        back(2, after(rows[2], keep_i))
        low_d = add_last(*after((stay_d, second_d), backward[2]))
        line_d = move_line(low_d)
        go_u, stay_u = add_core(*after((stay_u, first_u), low_d))
        second_u = move(go_u, to_second)
        parts = tuple(b[0] for b in backward)
        vbq = [b[1] for b in backward]
        vbv = [b[2] for b in backward]
        go_i, stay_i = add_wide(*after((keep_i, core_i), go_u, stay_u))
        first_i = move(go_i, to_first)
        keep_l, send_l = grad_last(
            pos, x, after(parts[2], go_i, stay_i), (*vbq, *vbv, vub, vob, vg1, vs1, vdb, vg2, vs2)
        )
        core_l = move(send_l, to_core)
        mine_d = add_line(low_d, after(line_d, keep_l))
        low_u = add_last(*after((stay_u, second_u), mine_d))
        line_u = move_line(low_u)
        go_l, stay_l = add_core(keep_l, after(core_l, low_u))
        first_l = move(go_l, to_first)
        go_i, stay_i = add_core(*after((stay_i, first_i), go_l, stay_l))
        second_i = move(go_i, to_second)
        input_grad = ig(parts, after(grad_first, go_i, stay_i), in_w, pos)
        mine_u = add_line(low_u, after(line_u, input_grad))
        low_i = add_last(*after((stay_i, second_i), mine_u))
        line_i = move_line(low_i)
        go_l, stay_l = add_core(*after((stay_l, first_l), low_i))
        second_l = move(go_l, to_second)
        got_d = move(after(mine_d, go_l), to_x)
        low_l = add_last(*after((stay_l, second_l), go_l))
        mine_i = add_line(low_i, after(line_i, low_l))
        line_l = move_line(after(low_l, mine_i))
        got_u = move(after(mine_u, mine_i), to_x)
        got_i = move(mine_i, to_x)
        (t_down,) = finish(
            finish_down_kernel, "finish_down", pos, (mine_d, after(got_d, low_l)), [down_weight.shape]
        )
        mine_l = add_line(low_l, after(line_l, t_down))
        got_l = move(mine_l, to_x)
        shapes = [attn_out_weight.shape, up_weight.shape, attn_in_weight.shape]
        shapes += [(1, v.shape[0]) for v in vectors]
        t_out, t_up, t_in, *small = finish(
            finish_kernel, "finish", pos, (mine_u, got_u, mine_i, got_i, mine_l, got_l), shapes
        )
        small = [b.reshape(-1) for b in small]
    else:
        (
            output, act, second_low, normed_low, pre_low, first_low, grad_first, grad_att,
            vg2, vs2, vdb, vub, vg1, vs1, vob,
        ) = main(attended, x, grad_rows, later, full[1:])
        for t in range(THIRDS):
            back(t, rows[t])
        parts = tuple(b[0] for b in backward)
        vbq = jnp.concatenate([b[1] for b in backward], axis=1)
        vbv = jnp.concatenate([b[2] for b in backward], axis=1)
        input_grad = ig(parts, grad_first, in_w)

        def total(a):
            share = lax.psum_scatter(a.astype(BF), "fsdp", scatter_dimension=0, tiled=True)
            return lax.psum(share, "rep").astype(F32)

        att = jnp.concatenate(attended, axis=1)
        t_down = total(tn(act, second_low, 768, 768))
        t_up = total(tn(normed_low, pre_low, 768, 768))
        t_out = total(tn(att, first_low, 768, 768))
        t_in = jnp.concatenate([tn(x, d, 768, 768) for d in parts], axis=1)
        t_in = total(t_in.reshape(model, -1, 3, 128).transpose(0, 2, 1, 3).reshape(model, 3 * model))
        small = [
            total(v.reshape(-1))
            for v in (jnp.concatenate([vbq, vbv], axis=1), vob, vg1, vs1, vub, vdb, vg2, vs2)
        ]
    b_in, b_out, b_g1, b_s1, b_up, b_down, b_g2, b_s2 = small
    return (
        output.reshape(hidden_states.shape),
        input_grad.reshape(hidden_states.shape),
        t_in, b_in, t_out, b_out, b_g1, b_s1, t_up, b_up, t_down, b_down, b_g2, b_s2,
    )


def solution(mesh):
    return jax.shard_map(
        local,
        mesh=mesh,
        in_specs=(
            P(("fsdp", "rep"), None, None),
            P(("fsdp", "rep")),
            P(("fsdp", "rep"), None, None),
            P("fsdp", None),
            P("fsdp"),
            P("fsdp", None),
            P("fsdp"),
            P("fsdp"),
            P("fsdp"),
            P("fsdp", None),
            P("fsdp"),
            P("fsdp", None),
            P("fsdp"),
            P("fsdp"),
            P("fsdp"),
        ),
        out_specs=(
            P(("fsdp", "rep"), None, None),
            P(("fsdp", "rep"), None, None),
            P("fsdp", None),
            P("fsdp"),
            P("fsdp", None),
            P("fsdp"),
            P("fsdp"),
            P("fsdp"),
            P("fsdp", None),
            P("fsdp"),
            P("fsdp", None),
            P("fsdp"),
            P("fsdp"),
            P("fsdp"),
        ),
        check_vma=False,
    )
```

```python
import math

import jax
import jax.numpy as jnp
from jax import lax
from jax.experimental import pallas as pl
from jax.experimental.pallas import tpu as pltpu
from jax.sharding import PartitionSpec as P

HEADS = 12
BF = jnp.bfloat16
F32 = jnp.float32
NT = (((1,), (1,)), ((), ()))
TN = (((0,), (0,)), ((), ()))
CW = 384
THIRDS = 3
LINE = 4
TINY = 128
AXES = ("fsdp", "rep")


def dg(a, b, dims):
    return lax.dot_general(a, b, dims, preferred_element_type=F32)


def mm(a, b):
    return jnp.dot(a, b, preferred_element_type=F32)


def params():
    return pltpu.CompilerParams(vmem_limit_bytes=60 * 1024 * 1024)


def cost(us):
    return pl.CostEstimate(flops=int(us * 1.15e9), bytes_accessed=int(us * 1e6), transcendentals=0)


def flat_index(z, y, c, x):
    return (z * 4 + y * 2 + c) * 2 + x


def permutation(target):
    pairs = []
    for z in range(LINE):
        for y in range(2):
            for c in range(2):
                for x in range(2):
                    pairs.append((flat_index(z, y, c, x), flat_index(*target(z, y, c, x))))
    return pairs


def to_core(z, y, c, x):
    return (z, y, 1 - c, x)


def to_x(z, y, c, x):
    return (z, y, c, 1 - x)


def to_first(z, y, c, x):
    return (z, y, c, 1 - x) if c == 0 else (z, 1 - y, c, x)


def to_second(z, y, c, x):
    return (z, 1 - y, c, x) if c == 0 else (z, y, c, 1 - x)


def to_line(step):
    return lambda z, y, c, x: ((z + step) % LINE, y, c, x)


def move(value, target):
    return lax.ppermute(value, AXES, permutation(target))


def after(values, *earlier):
    return lax.optimization_barrier((values, earlier))[0]


def along_line(half):
    return [half] + [move(half, to_line(k)) for k in range(1, LINE)]


def in_order(parts):
    here = lax.axis_index("fsdp") // 4
    return jnp.stack([lax.select_n((here - chip) & (LINE - 1), *parts) for chip in range(LINE)])


def over_core(parts):
    return tuple(parts) + tuple(move(part, to_core) for part in parts)


def add_core(keep, got):
    keep, got = keep.astype(F32), got.astype(F32)
    return (keep[1] + got[1]).astype(BF), (keep[0] + got[0]).astype(BF)


def add_kernel(keep, got, go, stay):
    total = keep[...].astype(F32) + got[...].astype(F32)
    stay[...] = total[0].astype(BF)
    go[...] = total[1].astype(BF)


def add_wide(keep, got):
    _, second, line, rows, width = keep.shape
    both = pl.BlockSpec((2, 1, line, rows, width), lambda i: (0, i, 0, 0, 0))
    one = pl.BlockSpec((1, line, rows, width), lambda i: (i, 0, 0, 0))
    return pl.pallas_call(
        add_kernel,
        grid=(second,),
        in_specs=[both, both],
        out_specs=[one, one],
        out_shape=[jax.ShapeDtypeStruct(keep.shape[1:], BF)] * 2,
        compiler_params=params(),
        cost_estimate=cost(4),
        name="add_wide",
    )(keep, got)


def add_last(stay, got):
    return (stay.astype(F32) + got.astype(F32)).astype(BF)


def add_line(low, parts):
    total = low[0].astype(F32)
    for part in parts:
        total = total + part.astype(F32)
    return total.astype(BF)


def move_line(low):
    return [move(low[k], to_line(k)) for k in range(1, LINE)]


FIELDS = (((0, 0, 96), (4, 1, 192)), tuple((n, i, 48) for i, n in enumerate((1, 2, 3, 5, 6, 7))))


def rows_of(width):
    return [(i, at, min(TINY, width - at)) for i, at in enumerate(range(0, width, TINY))]


def pack_kernel(pos, inw, outw, upw, downw, *refs):
    vectors, (one, two, three) = refs[:8], refs[8:]

    def fill(x):
        third = inw.shape[1] // 3
        for t in range(THIRDS):
            for part in range(3):
                start = part * third + (2 * t + x) * 128
                piece = inw[:, start : start + 128]
                one[:, t * CW + part * 128 : t * CW + (part + 1) * 128] = piece
        row = lax.broadcasted_iota(jnp.int32, (48, TINY), 0)
        block = jnp.zeros((48, TINY), F32)
        for place, top, size in FIELDS[x]:
            for i, at, n in rows_of(size):
                piece = vectors[place][at : at + n].astype(F32).reshape(1, n)
                if n < TINY:
                    piece = jnp.concatenate([piece, jnp.zeros((1, TINY - n), F32)], axis=1)
                block = jnp.where(row == top + i, jnp.broadcast_to(piece, (48, TINY)), block)
        one[:, THIRDS * CW :] = block.astype(BF)
        two[:, :CW] = outw[:, x * CW : (x + 1) * CW]
        width = upw.shape[1] // 2
        two[:, CW:] = upw[:, x * width : (x + 1) * width]
        three[...] = downw[:, x * CW : (x + 1) * CW]

    @pl.when(pos[3] == 0)
    def _():
        fill(0)

    @pl.when(pos[3] == 1)
    def _():
        fill(1)


def pack(pos, weights, vectors):
    shapes = [
        (48, weights[0].shape[1] // 2 + TINY),
        (48, weights[1].shape[1] // 2 + weights[2].shape[1] // 2),
        (weights[3].shape[0], CW),
    ]
    arrays = tuple(weights) + tuple(vectors)
    full = lambda a: pl.BlockSpec(a, lambda i, p: (0,) * len(a))
    return pl.pallas_call(
        pack_kernel,
        grid_spec=pltpu.PrefetchScalarGridSpec(
            num_scalar_prefetch=1,
            grid=(1,),
            in_specs=[full(a.shape) for a in arrays],
            out_specs=[full(a) for a in shapes],
        ),
        out_shape=[jax.ShapeDtypeStruct(a, BF) for a in shapes],
        compiler_params=params(),
        name="pack",
    )(pos, *arrays)


def sources(pos):
    y, c, x = pos[1], pos[2], pos[3]
    found = []
    for other in range(2):
        core = c ^ 1 if other else c
        swap = core == 0
        for first in range(2):
            for second in range(2):
                dx = jnp.where(swap, first, second)
                dy = jnp.where(swap, second, first)
                found.append((other * 4 + second * 2 + first, (y ^ dy) * 2 + core, x ^ dx))
    return found


def fetch(pos, buffers, target, rows, column, width, sem, stride=None, start=0):
    stride = width if stride is None else stride
    return [
        pltpu.make_async_copy(
            buffers[buffer].at[:, :, pl.ds(column, width)],
            target.at[
                :,
                pl.ds(pl.multiple_of(place * rows, 16), rows),
                pl.ds(pl.multiple_of(start + x * stride, 128), width),
            ],
            sem,
        )
        for buffer, place, x in sources(pos)
    ]


def fetch_in(pos, buffers, target, sem):
    copies = []
    for t in range(THIRDS):
        copies += fetch(pos, buffers, target, 48, t * CW, CW, sem, None, 2 * CW * t)
    return copies


def fetch_tiny(pos, buffers, target, column, sem):
    return [
        pltpu.make_async_copy(
            buffers[buffer].at[:, pl.ds(0, 16), pl.ds(column, TINY)], target.at[x, :, place], sem
        )
        for buffer, place, x in sources(pos)
    ]


def flat(ref, start=0, width=None):
    width = ref.shape[-1] if width is None else width
    return ref[:, :, start : start + width].reshape(-1, width) if len(ref.shape) == 3 else ref[:, start : start + width]


def run_all(copies):
    for copy in copies:
        copy.start()
    for copy in copies:
        copy.wait()


def spots(length, size, axis):
    shape = (length, TINY) if axis == 0 else (TINY, length)
    entry = lax.broadcasted_iota(jnp.int32, shape, axis).astype(F32)
    lane = lax.broadcasted_iota(jnp.int32, shape, 1 - axis).astype(F32)
    inner = entry - jnp.floor((entry + 0.5) * (1.0 / size)) * size
    return [
        jnp.where((lane + at == inner) & (lane < n), 1.0, 0.0).astype(BF) for _, at, n in rows_of(size)
    ]


def owned(shards, length):
    size = length // shards
    start = lax.broadcasted_iota(jnp.int32, (shards, length), 0) * size
    entry = lax.broadcasted_iota(jnp.int32, (shards, length), 1)
    return (entry >= start) & (entry < start + size)


def unpack_vectors(tiny, targets):
    shards = tiny.shape[1] * tiny.shape[2]
    made = {}
    for half in range(2):
        for place, top, size in FIELDS[half]:
            total = shards * size
            if size not in made:
                made[size] = spots(total, size, 1), owned(shards, total)
            each, mask = made[size]
            tiled = sum(mm(tiny[half, :, :, top + i, :].reshape(shards, TINY), spot) for i, spot in enumerate(each))
            targets[place][...] = jnp.sum(jnp.where(mask, tiled, 0.0), axis=0, keepdims=True)


def place_tile(pos, held, keep, send, rows, line):
    z, y, c, x = pos[0], pos[1], pos[2], pos[3]
    for relative, out in enumerate((keep, send)):
        core = c ^ relative
        swap = core == 0
        for first in range(2):
            for second in range(2):
                dx = jnp.where(swap, first, second)
                dy = jnp.where(swap, second, first)
                for slot, chip in line:
                    shard = chip * 4 + (y ^ dy) * 2 + core
                    start = pl.multiple_of(shard * rows, 16)
                    out[first, second, slot] = held[x ^ dx, pl.ds(start, rows), :]


def whole_line(pos):
    return [(k, (pos[0] + k) & (LINE - 1)) for k in range(LINE)]


def hold(held, tile):
    width = tile.shape[1] // 2
    held[0] = tile[:, :width].astype(BF)
    held[1] = tile[:, width:].astype(BF)


def joined(refs):
    return jnp.concatenate([r[...] for r in refs], axis=1)


def tiny_rows(vectors, fields):
    rows = []
    made = {}
    for vector, (_, _, size) in zip(vectors, fields):
        length = vector.shape[1]
        if size not in made:
            made[size] = spots(length, size, 0), owned(16, length)
        each, mask = made[size]
        own = jnp.where(mask, jnp.broadcast_to(vector, mask.shape), 0.0).astype(BF)
        rows += [mm(own, spot) for spot in each]
    count = len(rows)
    rows = jnp.concatenate(rows + [jnp.zeros((16 * (8 - count), TINY), F32)], axis=0).astype(BF)
    to = lax.broadcasted_iota(jnp.int32, (16 * 48, 128), 0)
    of = lax.broadcasted_iota(jnp.int32, (16 * 48, 128), 1)
    lift = jnp.where(to == (of & 15) * 48 + (of >> 4), 1.0, 0.0).astype(BF)
    return mm(lift, rows).astype(BF)


def grad_in_kernel(pos, x, *refs):
    parts, (keep, send, held) = refs[:-3], refs[-3:]
    for i, ref in enumerate(parts):

        @pl.when(pl.program_id(0) == i)
        def _(ref=ref):
            hold(held, dg(x[...], ref[...], TN))

    place_tile(pos, held, keep, send, 48, whole_line(pos))


def grad_last_kernel(pos, x, part, *refs):
    bq, bv, refs = refs[:THIRDS], refs[THIRDS : 2 * THIRDS], refs[2 * THIRDS :]
    upb, outb, g1, s1, downb, g2, s2, keep, send, held = refs
    hold(held, dg(x[...], part[...], TN))
    take = lambda ref: ref.at[:, :, :, :, pl.ds(0, CW)]
    place_tile(pos, held, take(keep), take(send), 48, whole_line(pos))
    groups = ((joined((*bq, *bv)), upb[...]), [r[...] for r in (outb, g1, s1, downb, g2, s2)])
    for half in range(2):
        held[half, :, :TINY] = tiny_rows(groups[half], FIELDS[half])
    take = lambda ref: ref.at[:, :, :, :, pl.ds(CW, TINY)]
    place_tile(pos, held.at[:, :, pl.ds(0, TINY)], take(keep), take(send), 48, whole_line(pos))


def grad_call(kernel, name, pos, arrays, in_specs, grid, block, shape, index, us):
    held = (2, 16 * 48, CW)
    return pl.pallas_call(
        kernel,
        grid_spec=pltpu.PrefetchScalarGridSpec(
            num_scalar_prefetch=1,
            grid=(grid,),
            in_specs=in_specs,
            out_specs=[pl.BlockSpec(block, index)] * 2,
            scratch_shapes=[pltpu.VMEM(held, BF)],
        ),
        out_shape=[jax.ShapeDtypeStruct(shape, BF)] * 2,
        compiler_params=params(),
        cost_estimate=cost(us),
        name=name,
    )(pos, *arrays)


def whole(array):
    return pl.BlockSpec(array.shape, lambda j, p: (0,) * array.ndim)


def grad_in(pos, x, parts):
    return grad_call(
        grad_in_kernel, "grad_in", pos, (x, *parts), [whole(a) for a in (x, *parts)], len(parts),
        (2, 2, LINE, 48, CW), (2, 2, LINE, 48, CW * len(parts)), lambda j, p: (0, 0, 0, 0, j), 5,
    )


def grad_last(pos, x, part, vectors):
    arrays = (x, part, *vectors)
    shape = (2, 2, LINE, 48, CW + TINY)
    return grad_call(
        grad_last_kernel, "grad_last", pos, arrays, [whole(a) for a in arrays], 1,
        shape, shape, lambda j, p: (0, 0, 0, 0, 0), 4,
    )


def halves(pos, mine, got):
    swap = pos[3] == 0
    return jnp.where(swap, mine, got).astype(F32), jnp.where(swap, got, mine).astype(F32)


def finish_down_kernel(pos, mine, got, down):
    for x, half in enumerate(halves(pos, mine[...], got[...])):
        down[:, CW * x : CW * (x + 1)] = half


def finish_kernel(pos, mine_u, got_u, mine, got, mine_last, got_last, out, up, weight, *vectors):
    width = up.shape[1] // 2
    third = weight.shape[1] // 3
    for x, half in enumerate(halves(pos, mine_u[...], got_u[...])):
        out[:, CW * x : CW * (x + 1)] = half[:, :CW]
        up[:, width * x : width * (x + 1)] = half[:, CW:]
    more = halves(pos, mine[...], got[...])
    for x, last in enumerate(halves(pos, mine_last[...], got_last[...])):
        for t in range(THIRDS):
            for part in range(3):
                start = part * third + (2 * t + x) * 128
                if t < THIRDS - 1:
                    piece = more[x][:, t * CW + part * 128 : t * CW + (part + 1) * 128]
                else:
                    piece = last[:, part * 128 : (part + 1) * 128]
                weight[:, start : start + 128] = piece
        for place, top, size in FIELDS[x]:
            for i, at, n in rows_of(size):
                vectors[place][:, at : at + n] = last[top + i : top + i + 1, CW : CW + n]


def finish(kernel, name, pos, sums, shapes):
    full = lambda shape: pl.BlockSpec(shape, lambda i, p: (0, 0))
    return pl.pallas_call(
        kernel,
        grid_spec=pltpu.PrefetchScalarGridSpec(
            num_scalar_prefetch=1,
            grid=(1,),
            in_specs=[pl.BlockSpec(memory_space=pltpu.VMEM)] * len(sums),
            out_specs=[full(shape) for shape in shapes],
        ),
        out_shape=[jax.ShapeDtypeStruct(shape, F32) for shape in shapes],
        compiler_params=params(),
        name=name,
    )(pos, *sums)


def pair_bias(bias):
    model = bias.shape[1] // 2
    parts = []
    for pair in range(model // 128):
        at = pair * 128
        parts += [bias[:, at : at + 128], jnp.zeros((1, 128), F32), bias[:, model + at : model + at + 128]]
    return jnp.concatenate(parts, axis=1)


def qkv_rows(x, weight, bias, outs):
    y = mm(x[...], flat(weight))
    scale = 1.0 / math.sqrt(x.shape[1] // HEADS)
    for t, out in enumerate(outs):
        width = out.shape[1]
        for at in range(0, width, 128):
            here = y[:, t * width + at : t * width + at + 128]
            place = t * width + at
            if at // 128 % 3 != 1:
                here = here + bias[:, place : place + 128]
            here = here.astype(BF)
            out[:, at : at + 128] = here * jnp.asarray(scale, BF) if at // 128 % 3 == 0 else here


def qkv_fetch_kernel(pos, x, *refs):
    buffers, outs, refs = refs[:8], refs[8 : 8 + THIRDS], refs[8 + THIRDS :]
    vectors, (weight, tiny, bias, sem, sem_tiny) = refs[:8], refs[8:]

    @pl.when(pl.program_id(0) == 0)
    def _():
        copies = fetch_in(pos, buffers, weight, sem)
        small = fetch_tiny(pos, buffers, tiny, THIRDS * CW, sem_tiny)
        for copy in small + copies:
            copy.start()
        for copy in small:
            copy.wait()
        unpack_vectors(tiny, vectors)
        bias[...] = pair_bias(vectors[0][...])
        for copy in copies:
            copy.wait()

    qkv_rows(x, weight, bias, outs)


def qkv_fetch(pos, x, buffers, shards, block=256):
    tokens, model = x.shape
    vec = lambda n: (pl.BlockSpec((1, n), lambda i, p: (0, 0)), jax.ShapeDtypeStruct((1, n), F32))
    vecs = [vec(model * n) for n in (2, 1, 1, 1, 4, 1, 1, 1)]
    return pl.pallas_call(
        qkv_fetch_kernel,
        grid_spec=pltpu.PrefetchScalarGridSpec(
            num_scalar_prefetch=1,
            grid=(tokens // block,),
            in_specs=[pl.BlockSpec((block, model), lambda i, p: (i, 0))]
            + [pl.BlockSpec(memory_space=pl.ANY)] * 8,
            out_specs=[pl.BlockSpec((block, 2 * CW), lambda i, p: (i, 0))] * THIRDS + [v[0] for v in vecs],
            scratch_shapes=[
                pltpu.VMEM((LINE, model // LINE, 3 * model), BF),
                pltpu.VMEM((2, LINE, shards // LINE, 16, TINY), BF),
                pltpu.VMEM((1, 3 * model), F32),
                pltpu.SemaphoreType.DMA,
                pltpu.SemaphoreType.DMA,
            ],
        ),
        out_shape=[jax.ShapeDtypeStruct((tokens, 2 * CW), BF)] * THIRDS + [v[1] for v in vecs],
        compiler_params=params(),
        cost_estimate=cost(10),
        name="qkv_fetch",
    )(pos, x, *buffers)


def qkv_plain_kernel(x, weight, bias, *outs):
    qkv_rows(x, weight, bias, outs)


def qkv(x, weight, bias, block=256):
    tokens, model = x.shape
    full = lambda a: pl.BlockSpec(a.shape, lambda i: (0, 0))
    return pl.pallas_call(
        qkv_plain_kernel,
        grid=(tokens // block,),
        in_specs=[pl.BlockSpec((block, model), lambda i: (i, 0)), full(weight), full(bias)],
        out_specs=[pl.BlockSpec((block, 2 * CW), lambda i: (i, 0))] * THIRDS,
        out_shape=[jax.ShapeDtypeStruct((tokens, 2 * CW), BF)] * THIRDS,
        compiler_params=params(),
    )(x, weight, bias)


def aug(q,k,h,bias,lane):
    own=(lane>=64) if h else (lane<64)
    j0=0 if h else 64
    z=jnp.zeros_like(q)
    one=jnp.where(lane==j0,jnp.ones_like(q),z)
    qa=jnp.where(own,q,one)
    ka=jnp.where(own,k,jnp.where(lane==j0,bias,z))
    return qa,ka,own
def attn_fwd_kernel(cnt,q_ref,k_ref,v_ref,o_ref,l_ref):
    p=pl.program_id(0)
    q=q_ref[...];k=k_ref[...];v=v_ref[...]
    S=q.shape[0]
    lane=lax.broadcasted_iota(jnp.int32,q.shape,1)
    row=lax.broadcasted_iota(jnp.int32,q.shape,0)
    bias=jnp.where(row<cnt[p],0.0,-1e30).astype(BF)
    vt=v.T
    outs=[]
    for h in range(2):
        qa,ka,own=aug(q,k,h,bias,lane)
        s=dg(ka,qa,NT)
        m=jnp.max(s,axis=0,keepdims=True)
        e=jnp.exp(s-m)
        l=jnp.sum(e,axis=0,keepdims=True)
        ot=mm(vt[64*h:64*h+64],e.astype(BF))
        outs.append(ot*(1.0/l))
        l_ref[0,0,h:h+1,:]=m+jnp.log(l)
    o_ref[...]=jnp.concatenate(outs,axis=0).T.astype(BF)
def attn_fwd(rows, counts, pages):
    tokens, width = rows.shape
    length, pairs = tokens // pages, width // CW
    block = lambda o: pl.BlockSpec((length, 128), lambda p, h, c: (p, 3 * h + o))
    return pl.pallas_call(
        attn_fwd_kernel,
        grid_spec=pltpu.PrefetchScalarGridSpec(
            num_scalar_prefetch=1,
            grid=(pages, pairs),
            in_specs=[block(0), block(1), block(2)],
            out_specs=[
                pl.BlockSpec((length, 128), lambda p, h, c: (p, h)),
                pl.BlockSpec((1, 1, 2, length), lambda p, h, c: (p, h, 0, 0)),
            ],
        ),
        out_shape=[
            jax.ShapeDtypeStruct((tokens, pairs * 128), BF),
            jax.ShapeDtypeStruct((pages, pairs, 2, length), F32),
        ],
        compiler_params=params(),
        cost_estimate=cost(3.5 * pairs),
        name="attn_fwd",
    )(counts, rows, rows, rows)


def attn_bwd_kernel(cnt,q_ref,k_ref,v_ref,g_ref,o_ref,l_ref,d_ref,bq_ref,bv_ref):
    p=pl.program_id(1)
    q=q_ref[...];k=k_ref[...];v=v_ref[...];g=g_ref[...]
    lane=lax.broadcasted_iota(jnp.int32,q.shape,1)
    row=lax.broadcasted_iota(jnp.int32,q.shape,0)
    bias=jnp.where(row<cnt[p],0.0,-1e30).astype(BF)
    prod=g.astype(F32)*o_ref[...].astype(F32)
    hi=prod.astype(BF); lo=(prod-hi.astype(F32)).astype(BF)
    r8=lax.broadcasted_iota(jnp.int32,(16,128),0); l8=lax.broadcasted_iota(jnp.int32,(16,128),1)
    sel=jnp.where(r8==l8//64,1.0,0.0).astype(BF)
    delta=dg(sel,hi,NT)+dg(sel,lo,NT)
    kt=k.T
    dv=[];dk=[];dqt=[]
    for h in range(2):
        qa,ka,own=aug(q,k,h,bias,lane)
        s=dg(ka,qa,NT)
        pr=jnp.exp(s-l_ref[0,0,h:h+1,:])
        va=jnp.where(own,v,jnp.zeros_like(v))
        dp=dg(va,g,NT)
        ds=(pr*(dp-delta[h:h+1])).astype(BF)
        dv.append(mm(pr.astype(BF),g)); dk.append(mm(ds,q))
        dqt.append(mm(kt[64*h:64*h+64],ds))
    first=lane<64
    dvv=jnp.where(first,dv[0],dv[1])
    dq=jnp.concatenate(dqt,axis=0).T*0.125
    d_ref[:,:128]=dq.astype(BF); d_ref[:,256:]=dvv.astype(BF)
    d_ref[:,128:256]=jnp.where(first,dk[0],dk[1]).astype(BF)
    sq=jnp.sum(dq,axis=0,keepdims=True); sv=jnp.sum(dvv,axis=0,keepdims=True)
    @pl.when(p==0)
    def _():
        bq_ref[...]=sq; bv_ref[...]=sv
    @pl.when(p>0)
    def _():
        bq_ref[...]+=sq; bv_ref[...]+=sv
def attn_bwd(rows, counts, grad, out, totals, pages, at):
    tokens, width = rows.shape
    length, pairs = tokens // pages, width // CW
    block = lambda o: pl.BlockSpec((length, 128), lambda h, p, c: (p, 3 * h + o))
    line = pl.BlockSpec((1, 128), lambda h, p, c: (0, h))
    return pl.pallas_call(
        attn_bwd_kernel,
        grid_spec=pltpu.PrefetchScalarGridSpec(
            num_scalar_prefetch=1,
            grid=(pairs, pages),
            in_specs=[
                block(0),
                block(1),
                block(2),
                pl.BlockSpec((length, 128), lambda h, p, c: (p, h + at)),
                pl.BlockSpec((length, 128), lambda h, p, c: (p, h)),
                pl.BlockSpec((1, 1, 2, length), lambda h, p, c: (p, h, 0, 0)),
            ],
            out_specs=[pl.BlockSpec((length, CW), lambda h, p, c: (p, h))] + [line] * 2,
        ),
        out_shape=[jax.ShapeDtypeStruct((tokens, width), BF)]
        + [jax.ShapeDtypeStruct((1, pairs * 128), F32)] * 2,
        compiler_params=params(),
        cost_estimate=cost(4.5 * pairs),
        name="attn_bwd",
    )(counts, rows, rows, rows, grad, out, totals)


def norm(t):
    m=jnp.mean(t,axis=-1,keepdims=True); c=t-m
    v=jnp.mean(c*c,axis=-1,keepdims=True); inv=lax.rsqrt(v+1e-12)
    return c*inv,inv
def norm_back(e,hat,inv):
    return inv*(e-jnp.mean(e,axis=-1,keepdims=True)-hat*jnp.mean(e*hat,axis=-1,keepdims=True))
def col(t): return jnp.sum(t,axis=0,keepdims=True)
C=768
def rows_at(ref, start, count):
    if len(ref.shape) == 2:
        return ref[start : start + count, :]
    each = ref.shape[1]
    return ref[start // each, start % each : start % each + count, :]


def main_fetch_kernel(pos, *refs):
    att, (x, cot), refs = refs[:-49], refs[-49:-47], refs[-47:]
    two, three, refs = refs[:8], refs[8:16], refs[16:]
    vecs, (out, gf, ga), sums, refs = refs[:7], refs[7:10], refs[10:17], refs[17:]
    keep_d, send_d, keep_u, send_u, refs = *refs[:4], refs[4:]
    slope, ow, uw, dw, big, wide, held, *sems = refs
    act, pre = big.at[0], big.at[1]
    low, back, first, attended = (wide.at[n] for n in range(4))
    step = pl.program_id(0)
    rows = x.shape[0]
    blocks = act.shape[0] // rows
    copies = (
        fetch(pos, two, ow, 48, 0, CW, sems[0]),
        fetch(pos, two, uw, 48, CW, uw.shape[2] // 2, sems[1]),
        fetch(pos, three, dw, dw.shape[1] // 4, 0, CW, sems[2]),
    )

    @pl.when(step == 0)
    def _():
        for group in copies:
            for copy in group:
                copy.start()

    def ready(place):
        @pl.when(step == 0)
        def _():
            for copy in copies[place]:
                copy.wait()

    @pl.when(step < blocks)
    def _():
        here = pl.ds(pl.multiple_of(step * rows, 16), rows)
        attended[here, :] = joined(att)
        main_kernel(
            att, x, cot, ow, uw, dw, *vecs, out,
            act.at[here, :], back.at[here, :], low.at[here, :], pre.at[here, :], first.at[here, :],
            gf, ga, *sums, slope, ready,
        )

    @pl.when((step >= blocks) & (step < blocks + LINE))
    def _():
        chip = (pos[0] + step - blocks) & (LINE - 1)
        columns = act.shape[1] // LINE
        here = pl.ds(pl.multiple_of(chip * columns, 128), columns)
        hold(held, dg(act[:, here], back[...], TN))
        place_tile(pos, held, keep_d, send_d, held.shape[1] // 4, [(0, 0)])

    @pl.when(step == blocks + LINE)
    def _():
        hold(held, dg(attended[...], first[...], TN))
        place_tile(pos, held, keep_u, send_u, 48, whole_line(pos))

    @pl.when(step > blocks + LINE)
    def _():
        at = pl.multiple_of((step - blocks - LINE - 1) * CW, 128)
        right = pl.multiple_of(at + pre.shape[1] // 2, 128)
        columns = jnp.concatenate([pre[:, pl.ds(at, CW)], pre[:, pl.ds(right, CW)]], axis=1)
        hold(held, dg(low[...], columns, TN))
        place_tile(pos, held, keep_u, send_u, 48, whole_line(pos))


def main_fetch(pos, att, x, cot, weights, vecs, rows=512):
    T, D = x.shape
    FF = vecs[3].shape[1]
    blocks, ups = T // rows, FF // 2 // CW
    rb = lambda n: pl.BlockSpec((rows, n), lambda i, p: (jnp.minimum(i, blocks - 1), 0))
    full = lambda a: pl.BlockSpec(a.shape, lambda i, p: (0, 0))
    vec = lambda n: (pl.BlockSpec((1, n), lambda i, p: (0, 0)), jax.ShapeDtypeStruct((1, n), F32))
    vs = [vec(n) for n in (D, D, D, FF, D, D, D)]
    down = pl.BlockSpec(
        (2, 2, 1, FF // 16, CW), lambda i, p: (0, 0, jnp.clip(i - blocks, 0, LINE - 1), 0, 0)
    )
    up = pl.BlockSpec(
        (2, 2, LINE, 48, CW), lambda i, p: (0, 0, 0, 0, jnp.clip(i - blocks - LINE, 0, ups))
    )
    shapes = [(2, 2, LINE, FF // 16, CW)] * 2 + [(2, 2, LINE, 48, CW * (1 + ups))] * 2
    return pl.pallas_call(
        main_fetch_kernel,
        grid_spec=pltpu.PrefetchScalarGridSpec(
            num_scalar_prefetch=1,
            grid=(blocks + LINE + 1 + ups,),
            in_specs=[rb(a.shape[1]) for a in (*att, x, cot)]
            + [pl.BlockSpec(memory_space=pl.ANY)] * len(weights)
            + [full(v) for v in vecs],
            out_specs=[rb(D)] * 3 + [v[0] for v in vs] + [down, down, up, up],
            scratch_shapes=[
                pltpu.VMEM((rows, FF), BF),
                pltpu.VMEM((LINE, D // LINE, D), BF),
                pltpu.VMEM((LINE, D // LINE, FF), BF),
                pltpu.VMEM((LINE, FF // LINE, D), BF),
                pltpu.VMEM((2, T, FF), BF),
                pltpu.VMEM((4, T, D), BF),
                pltpu.VMEM((2, 16 * 48, CW), BF),
            ]
            + [pltpu.SemaphoreType.DMA] * 3,
        ),
        out_shape=[jax.ShapeDtypeStruct((T, D), t) for t in (BF, F32, BF)]
        + [v[1] for v in vs]
        + [jax.ShapeDtypeStruct(a, BF) for a in shapes],
        compiler_params=params(),
        cost_estimate=cost(58),
        name="main",
    )(pos, *att, x, cot, *weights, *vecs)


def main_plain_kernel(*refs):
    main_kernel(refs[:-28], *refs[-28:])


def main_kernel(att,x,cot,ow,uw,dw,ob,g1,s1,ub,db,g2,s2,
                lo_ref,act_ref,sl_ref,nl_ref,pl_ref,fl_ref,gf_ref,ga_ref,
                vg2,vs2,vdb,vub,vg1,vs1,vob,slope,ready=lambda place: None):
    i=pl.program_id(0)
    FF=uw.shape[-1]
    ready(0)
    fs=x[...].astype(F32)+mm(joined(att),flat(ow))+ob[...]
    fh,fi=norm(fs)
    normed=fh*g1[...]+s1[...]
    nl=normed.astype(BF); nl_ref[...]=nl
    acc=normed+db[...]
    ready(1)
    for j in range(0,FF,C):
        pre=mm(nl,flat(uw,j,C))+ub[:,j:j+C]
        phi=0.5*(1.0+lax.erf(pre*(1.0/math.sqrt(2.0))))
        a=(pre*phi).astype(BF)
        act_ref[:,j:j+C]=a
        slope[:,j:j+C]=(phi+pre*jnp.exp(-0.5*pre*pre)*(1.0/math.sqrt(2.0*math.pi))).astype(slope.dtype)
        if j==0: ready(2)
        acc=acc+mm(a,rows_at(dw,j,C))
    sh,si=norm(acc)
    lo_ref[...]=(sh*g2[...]+s2[...]).astype(BF)
    gr=cot[...].astype(F32)
    gs=norm_back(gr*g2[...],sh,si)
    sl=gs.astype(BF); sl_ref[...]=sl
    gn=gs
    ubs=[]
    for j in range(0,FF,C):
        gp=dg(sl,rows_at(dw,j,C),NT)*slope[:,j:j+C]
        ubs.append(col(gp))
        gpl=gp.astype(BF); pl_ref[:,j:j+C]=gpl
        gn=gn+dg(gpl,flat(uw,j,C),NT)
    gf=norm_back(gn*g1[...],fh,fi)
    fl=gf.astype(BF); fl_ref[...]=fl; gf_ref[...]=gf
    ga_ref[...]=dg(fl,flat(ow),NT).astype(BF)
    vals=[(vg2,col(gr*sh)),(vs2,col(gr)),(vdb,col(gs)),(vub,jnp.concatenate(ubs,1)),(vg1,col(gn*fh)),(vs1,col(gn)),(vob,col(gf))]
    @pl.when(i==0)
    def _():
        for r,v in vals: r[...]=v
    @pl.when(i>0)
    def _():
        for r,v in vals: r[...]+=v
def main(att, x, cot, weights, vecs, R=256):
    T, D = x.shape
    FF = vecs[3].shape[1]
    rb = lambda n: pl.BlockSpec((R, n), lambda i: (i, 0))
    full = lambda a: pl.BlockSpec(a.shape, lambda i: (0, 0))
    sds = lambda n, t=BF: jax.ShapeDtypeStruct((T, n), t)
    vec = lambda n: (pl.BlockSpec((1, n), lambda i: (0, 0)), jax.ShapeDtypeStruct((1, n), F32))
    vs = [vec(n) for n in (D, D, D, FF, D, D, D)]
    return pl.pallas_call(
        main_plain_kernel,
        grid=(T // R,),
        in_specs=[rb(a.shape[1]) for a in (*att, x, cot)] + [full(w) for w in weights] + [full(v) for v in vecs],
        out_specs=[rb(D), rb(FF), rb(D), rb(D), rb(FF), rb(D), rb(D), rb(D)] + [v[0] for v in vs],
        out_shape=[sds(D), sds(FF), sds(D), sds(D), sds(FF), sds(D), sds(D, F32), sds(D)] + [v[1] for v in vs],
        scratch_shapes=[pltpu.VMEM((R, FF), F32)],
        compiler_params=params(),
        name="main",
    )(*att, x, cot, *weights, *vecs)


def tn_kernel(a,b,o): o[...]=dg(a[...],b[...],TN).astype(BF)
def tn(a,b,bm,bn):
    T,M=a.shape;N=b.shape[1]
    return pl.pallas_call(tn_kernel,grid=(M//bm,N//bn),
      in_specs=[pl.BlockSpec((T,bm),lambda i,j:(0,i)),pl.BlockSpec((T,bn),lambda i,j:(0,j))],
      out_specs=pl.BlockSpec((bm,bn),lambda i,j:(i,j)),out_shape=jax.ShapeDtypeStruct((M,N),BF),compiler_params=params())(a,b)
def ig_kernel(gf, parts, w, o):
    o[...] = (gf[...] + dg(joined(parts), flat(w), NT)).astype(BF)


def ig_plain_kernel(gf, *refs):
    ig_kernel(gf, refs[:-2], refs[-2], refs[-1])


def ig_fetch_kernel(pos, gf, *refs):
    parts, buffers, (o, weight, sem) = refs[:-11], refs[-11:-3], refs[-3:]

    @pl.when(pl.program_id(0) == 0)
    def _():
        run_all(fetch_in(pos, buffers, weight, sem))

    ig_kernel(gf, parts, weight, o)


def ig(parts, gf, weights, pos=None, R=256):
    T, D = gf.shape
    rb = lambda n: pl.BlockSpec((R, n), lambda i, *p: (i, 0))
    fetched = pos is not None
    return pl.pallas_call(
        ig_fetch_kernel if fetched else ig_plain_kernel,
        grid_spec=pltpu.PrefetchScalarGridSpec(
            num_scalar_prefetch=1 if fetched else 0,
            grid=(T // R,),
            in_specs=[rb(a.shape[1]) for a in (gf, *parts)]
            + [pl.BlockSpec(memory_space=pl.ANY) if fetched else pl.BlockSpec(w.shape, lambda i, *p: (0, 0)) for w in weights],
            out_specs=rb(D),
            scratch_shapes=[pltpu.VMEM((LINE, D // LINE, 3 * D), BF), pltpu.SemaphoreType.DMA] if fetched else [],
        ),
        out_shape=jax.ShapeDtypeStruct((T, D), BF),
        compiler_params=params(),
        cost_estimate=cost(10),
        name="ig",
    )(*([pos] if fetched else []), gf, *parts, *weights)


def local(
    hidden_states,
    page_counts,
    cotangent,
    attn_in_weight,
    attn_in_bias,
    attn_out_weight,
    attn_out_bias,
    first_gain,
    first_shift,
    up_weight,
    up_bias,
    down_weight,
    down_bias,
    second_gain,
    second_shift,
):
    pages, length, model = hidden_states.shape
    hidden = up_weight.shape[1]
    x = hidden_states.reshape(-1, model)
    grad_rows = cotangent.reshape(-1, model)
    weights = (attn_in_weight, attn_out_weight, up_weight, down_weight)
    vectors = (
        attn_in_bias,
        attn_out_bias,
        first_gain,
        first_shift,
        up_bias,
        down_bias,
        second_gain,
        second_shift,
    )
    lined = lax.axis_size("fsdp") == 4 * LINE and lax.axis_size("rep") == 2
    pairs = HEADS // 2 // THIRDS
    forward = [None] * THIRDS
    backward = [None] * THIRDS

    def ahead(t, rows):
        forward[t] = attn_fwd(rows, page_counts, pages)

    def back(t, rows):
        backward[t] = attn_bwd(rows, page_counts, grad_att, *forward[t], pages, pairs * t)

    if lined:
        index = lax.axis_index("fsdp")
        pos = jnp.stack([index // 4, index // 2 % 2, index % 2, lax.axis_index("rep")]).astype(jnp.int32)
        one, two, three = pack(pos, weights, vectors)
        line_one = in_order(along_line(one))
        second_one = move(line_one, to_second)
        first_one = move(line_one, to_first)
        parts_two = along_line(after(two, line_one))
        parts_three = along_line(after(three, line_one))
        both_one = move(after(second_one, *parts_two[1:]), to_first)
        in_w = over_core((line_one, first_one, second_one, both_one))
        line_two = in_order(parts_two)
        second_two = move(line_two, to_second)
        first_two = move(line_two, to_first)
        outs = qkv_fetch(pos, x, after(in_w, line_two), 16)
        rows, full = outs[:THIRDS], outs[THIRDS:]
        line_three = in_order(after(parts_three, rows))
        second_three = move(line_three, to_second)
        first_three = move(line_three, to_first)
        ahead(0, after(rows[0], line_three))
        both_two = move(after(second_two, forward[0]), to_first)
        ahead(1, after(rows[1], forward[0], second_two))
        both_three = move(after(second_three, forward[1]), to_first)
        early = [move(part, to_core) for part in after((line_two,), forward[0])]
        ready = (line_two, first_two, second_two, line_three, first_three, second_three)
        moved = [move(part, to_core) for part in after(ready[1:], forward[1])]
        ahead(2, after(rows[2], forward[1], second_three, first_three, *early))
        ready += (*early, *moved)
        last = over_core(after((both_two, both_three), forward[2]))
        later = (*ready[0:3], last[0], *ready[6:9], last[2], *ready[3:6], last[1], *ready[9:12], last[3])
    else:
        pos = None
        gathered = lambda a: lax.all_gather(a, "fsdp", axis=0, tiled=True)
        in_w = gathered(attn_in_weight).reshape(model, 3, -1, 128)
        in_w = (in_w.transpose(0, 2, 1, 3).reshape(model, 3 * model),)
        full = [gathered(v).astype(F32).reshape(1, -1) for v in vectors]
        later = tuple(gathered(w) for w in weights[1:])
        rows = qkv(x, in_w[0], pair_bias(full[0]))
        for t in range(THIRDS):
            ahead(t, rows[t])
    attended = [f[0] for f in forward]
    if lined:
        (
            output, grad_first, grad_att, vg2, vs2, vdb, vub, vg1, vs1, vob,
            keep_d, send_d, keep_u, send_u,
        ) = main_fetch(pos, attended, x, grad_rows, later, full[1:])
        core_d = move(send_d, to_core)
        core_u = move(send_u, to_core)
        back(0, rows[0])
        go_d, stay_d = add_wide(*after((keep_d, core_d), backward[0]))
        first_d = move(go_d, to_first)
        go_u, stay_u = add_wide(*after((keep_u, core_u), go_d))
        first_u = move(go_u, to_first)
        back(1, after(rows[1], go_u, stay_u))
        go_d, stay_d = add_core(*after((stay_d, first_d), backward[1]))
        second_d = move(go_d, to_second)
        keep_i, send_i = grad_in(pos, x, after((backward[0][0], backward[1][0]), go_d, stay_d))
        core_i = move(send_i, to_core)
        back(2, after(rows[2], keep_i))
        low_d = add_last(*after((stay_d, second_d), backward[2]))
        line_d = move_line(low_d)
        go_u, stay_u = add_core(*after((stay_u, first_u), low_d))
        second_u = move(go_u, to_second)
        parts = tuple(b[0] for b in backward)
        vbq = [b[1] for b in backward]
        vbv = [b[2] for b in backward]
        go_i, stay_i = add_wide(*after((keep_i, core_i), go_u, stay_u))
        first_i = move(go_i, to_first)
        keep_l, send_l = grad_last(
            pos, x, after(parts[2], go_i, stay_i), (*vbq, *vbv, vub, vob, vg1, vs1, vdb, vg2, vs2)
        )
        core_l = move(send_l, to_core)
        mine_d = add_line(low_d, after(line_d, keep_l))
        low_u = add_last(*after((stay_u, second_u), mine_d))
        line_u = move_line(low_u)
        go_l, stay_l = add_core(keep_l, after(core_l, low_u))
        first_l = move(go_l, to_first)
        go_i, stay_i = add_core(*after((stay_i, first_i), go_l, stay_l))
        second_i = move(go_i, to_second)
        input_grad = ig(parts, after(grad_first, go_i, stay_i), in_w, pos)
        mine_u = add_line(low_u, after(line_u, input_grad))
        low_i = add_last(*after((stay_i, second_i), mine_u))
        line_i = move_line(low_i)
        go_l, stay_l = add_core(*after((stay_l, first_l), low_i))
        second_l = move(go_l, to_second)
        got_d = move(after(mine_d, go_l), to_x)
        low_l = add_last(*after((stay_l, second_l), go_l))
        mine_i = add_line(low_i, after(line_i, low_l))
        line_l = move_line(after(low_l, mine_i))
        got_u = move(after(mine_u, mine_i), to_x)
        got_i = move(mine_i, to_x)
        (t_down,) = finish(
            finish_down_kernel, "finish_down", pos, (mine_d, after(got_d, low_l)), [down_weight.shape]
        )
        mine_l = add_line(low_l, after(line_l, t_down))
        got_l = move(mine_l, to_x)
        shapes = [attn_out_weight.shape, up_weight.shape, attn_in_weight.shape]
        shapes += [(1, v.shape[0]) for v in vectors]
        t_out, t_up, t_in, *small = finish(
            finish_kernel, "finish", pos, (mine_u, got_u, mine_i, got_i, mine_l, got_l), shapes
        )
        small = [b.reshape(-1) for b in small]
    else:
        (
            output, act, second_low, normed_low, pre_low, first_low, grad_first, grad_att,
            vg2, vs2, vdb, vub, vg1, vs1, vob,
        ) = main(attended, x, grad_rows, later, full[1:])
        for t in range(THIRDS):
            back(t, rows[t])
        parts = tuple(b[0] for b in backward)
        vbq = jnp.concatenate([b[1] for b in backward], axis=1)
        vbv = jnp.concatenate([b[2] for b in backward], axis=1)
        input_grad = ig(parts, grad_first, in_w)

        def total(a):
            share = lax.psum_scatter(a.astype(BF), "fsdp", scatter_dimension=0, tiled=True)
            return lax.psum(share, "rep").astype(F32)

        att = jnp.concatenate(attended, axis=1)
        t_down = total(tn(act, second_low, 768, 768))
        t_up = total(tn(normed_low, pre_low, 768, 768))
        t_out = total(tn(att, first_low, 768, 768))
        t_in = jnp.concatenate([tn(x, d, 768, 768) for d in parts], axis=1)
        t_in = total(t_in.reshape(model, -1, 3, 128).transpose(0, 2, 1, 3).reshape(model, 3 * model))
        small = [
            total(v.reshape(-1))
            for v in (jnp.concatenate([vbq, vbv], axis=1), vob, vg1, vs1, vub, vdb, vg2, vs2)
        ]
    b_in, b_out, b_g1, b_s1, b_up, b_down, b_g2, b_s2 = small
    return (
        output.reshape(hidden_states.shape),
        input_grad.reshape(hidden_states.shape),
        t_in, b_in, t_out, b_out, b_g1, b_s1, t_up, b_up, t_down, b_down, b_g2, b_s2,
    )


def solution(mesh):
    return jax.shard_map(
        local,
        mesh=mesh,
        in_specs=(
            P(("fsdp", "rep"), None, None),
            P(("fsdp", "rep")),
            P(("fsdp", "rep"), None, None),
            P("fsdp", None),
            P("fsdp"),
            P("fsdp", None),
            P("fsdp"),
            P("fsdp"),
            P("fsdp"),
            P("fsdp", None),
            P("fsdp"),
            P("fsdp", None),
            P("fsdp"),
            P("fsdp"),
            P("fsdp"),
        ),
        out_specs=(
            P(("fsdp", "rep"), None, None),
            P(("fsdp", "rep"), None, None),
            P("fsdp", None),
            P("fsdp"),
            P("fsdp", None),
            P("fsdp"),
            P("fsdp"),
            P("fsdp"),
            P("fsdp", None),
            P("fsdp"),
            P("fsdp", None),
            P("fsdp"),
            P("fsdp"),
            P("fsdp"),
        ),
        check_vma=False,
    )
```

```python
import functools
import math

import jax
import jax.numpy as jnp
from jax import lax
from jax.experimental import pallas as pl
from jax.experimental.pallas import tpu as pltpu
from jax.sharding import PartitionSpec as P

HEADS = 12
BF = jnp.bfloat16
F32 = jnp.float32
NT = (((1,), (1,)), ((), ()))
TN = (((0,), (0,)), ((), ()))
CW = 384
THIRDS = 3
LINE = 4
TINY = 128
AXES = ("fsdp", "rep")


def dg(a, b, dims):
    return lax.dot_general(a, b, dims, preferred_element_type=F32)


def mm(a, b):
    return jnp.dot(a, b, preferred_element_type=F32)


def params():
    return pltpu.CompilerParams(vmem_limit_bytes=60 * 1024 * 1024)


def cost(us):
    return pl.CostEstimate(flops=int(us * 1.15e9), bytes_accessed=int(us * 1e6), transcendentals=0)


def flat_index(z, y, c, x):
    return (z * 4 + y * 2 + c) * 2 + x


def permutation(target):
    pairs = []
    for z in range(LINE):
        for y in range(2):
            for c in range(2):
                for x in range(2):
                    pairs.append((flat_index(z, y, c, x), flat_index(*target(z, y, c, x))))
    return pairs


def to_core(z, y, c, x):
    return (z, y, 1 - c, x)


def to_x(z, y, c, x):
    return (z, y, c, 1 - x)


def to_first(z, y, c, x):
    return (z, y, c, 1 - x) if c == 0 else (z, 1 - y, c, x)


def to_second(z, y, c, x):
    return (z, 1 - y, c, x) if c == 0 else (z, y, c, 1 - x)


def to_line(step):
    return lambda z, y, c, x: ((z + step) % LINE, y, c, x)


def move(value, target):
    return lax.ppermute(value, AXES, permutation(target))


def after(values, *earlier):
    return lax.optimization_barrier((values, earlier))[0]


def along_line(half):
    return [half] + [move(half, to_line(k)) for k in range(1, LINE)]


def in_order(parts):
    here = lax.axis_index("fsdp") // 4
    return jnp.stack([lax.select_n((here - chip) & (LINE - 1), *parts) for chip in range(LINE)])


def over_core(parts):
    return tuple(parts) + tuple(move(part, to_core) for part in parts)


def add_core(keep, got):
    keep, got = keep.astype(F32), got.astype(F32)
    return (keep[1] + got[1]).astype(BF), (keep[0] + got[0]).astype(BF)


def add_kernel(keep, got, go, stay):
    total = keep[...].astype(F32) + got[...].astype(F32)
    stay[...] = total[0].astype(BF)
    go[...] = total[1].astype(BF)


def add_wide(keep, got):
    _, second, line, rows, width = keep.shape
    both = pl.BlockSpec((2, 1, line, rows, width), lambda i: (0, i, 0, 0, 0))
    one = pl.BlockSpec((1, line, rows, width), lambda i: (i, 0, 0, 0))
    return pl.pallas_call(
        add_kernel,
        grid=(second,),
        in_specs=[both, both],
        out_specs=[one, one],
        out_shape=[jax.ShapeDtypeStruct(keep.shape[1:], BF)] * 2,
        compiler_params=params(),
        cost_estimate=cost(4),
        name="add_wide",
    )(keep, got)


def add_last(stay, got):
    return (stay.astype(F32) + got.astype(F32)).astype(BF)


def add_line(low, parts):
    total = low[0].astype(F32)
    for part in parts:
        total = total + part.astype(F32)
    return total.astype(BF)


def move_line(low):
    return [move(low[k], to_line(k)) for k in range(1, LINE)]


FIELDS = (((0, 0, 96), (4, 1, 192)), tuple((n, i, 48) for i, n in enumerate((1, 2, 3, 5, 6, 7))))


def rows_of(width):
    return [(i, at, min(TINY, width - at)) for i, at in enumerate(range(0, width, TINY))]


def pack_kernel(pos, inw, outw, upw, downw, *refs):
    vectors, (one, two, three) = refs[:8], refs[8:]

    def fill(x):
        third = inw.shape[1] // 3
        for t in range(THIRDS):
            for part in range(3):
                start = part * third + (2 * t + x) * 128
                piece = inw[:, start : start + 128]
                one[:, t * CW + part * 128 : t * CW + (part + 1) * 128] = piece
        row = lax.broadcasted_iota(jnp.int32, (48, TINY), 0)
        block = jnp.zeros((48, TINY), F32)
        for place, top, size in FIELDS[x]:
            for i, at, n in rows_of(size):
                piece = vectors[place][at : at + n].astype(F32).reshape(1, n)
                if n < TINY:
                    piece = jnp.concatenate([piece, jnp.zeros((1, TINY - n), F32)], axis=1)
                block = jnp.where(row == top + i, jnp.broadcast_to(piece, (48, TINY)), block)
        one[:, THIRDS * CW :] = block.astype(BF)
        two[:, :CW] = outw[:, x * CW : (x + 1) * CW]
        width = upw.shape[1] // 2
        two[:, CW:] = upw[:, x * width : (x + 1) * width]
        three[...] = downw[:, x * CW : (x + 1) * CW]

    @pl.when(pos[3] == 0)
    def _():
        fill(0)

    @pl.when(pos[3] == 1)
    def _():
        fill(1)


def pack(pos, weights, vectors):
    shapes = [
        (48, weights[0].shape[1] // 2 + TINY),
        (48, weights[1].shape[1] // 2 + weights[2].shape[1] // 2),
        (weights[3].shape[0], CW),
    ]
    arrays = tuple(weights) + tuple(vectors)
    full = lambda a: pl.BlockSpec(a, lambda i, p: (0,) * len(a))
    return pl.pallas_call(
        pack_kernel,
        grid_spec=pltpu.PrefetchScalarGridSpec(
            num_scalar_prefetch=1,
            grid=(1,),
            in_specs=[full(a.shape) for a in arrays],
            out_specs=[full(a) for a in shapes],
        ),
        out_shape=[jax.ShapeDtypeStruct(a, BF) for a in shapes],
        compiler_params=params(),
        name="pack",
    )(pos, *arrays)


def sources(pos):
    y, c, x = pos[1], pos[2], pos[3]
    found = []
    for other in range(2):
        core = c ^ 1 if other else c
        swap = core == 0
        for first in range(2):
            for second in range(2):
                dx = jnp.where(swap, first, second)
                dy = jnp.where(swap, second, first)
                found.append((other * 4 + second * 2 + first, (y ^ dy) * 2 + core, x ^ dx))
    return found


def fetch(pos, buffers, target, rows, column, width, sem, stride=None, start=0):
    stride = width if stride is None else stride
    return [
        pltpu.make_async_copy(
            buffers[buffer].at[:, :, pl.ds(column, width)],
            target.at[
                :,
                pl.ds(pl.multiple_of(place * rows, 16), rows),
                pl.ds(pl.multiple_of(start + x * stride, 128), width),
            ],
            sem,
        )
        for buffer, place, x in sources(pos)
    ]


def fetch_in(pos, buffers, target, sem):
    copies = []
    for t in range(THIRDS):
        copies += fetch(pos, buffers, target, 48, t * CW, CW, sem, None, 2 * CW * t)
    return copies


def fetch_tiny(pos, buffers, target, column, sem):
    return [
        pltpu.make_async_copy(
            buffers[buffer].at[:, pl.ds(0, 16), pl.ds(column, TINY)], target.at[x, :, place], sem
        )
        for buffer, place, x in sources(pos)
    ]


def flat(ref, start=0, width=None):
    width = ref.shape[-1] if width is None else width
    return ref[:, :, start : start + width].reshape(-1, width) if len(ref.shape) == 3 else ref[:, start : start + width]


def run_all(copies):
    for copy in copies:
        copy.start()
    for copy in copies:
        copy.wait()


def spots(length, size, axis):
    shape = (length, TINY) if axis == 0 else (TINY, length)
    entry = lax.broadcasted_iota(jnp.int32, shape, axis).astype(F32)
    lane = lax.broadcasted_iota(jnp.int32, shape, 1 - axis).astype(F32)
    inner = entry - jnp.floor((entry + 0.5) * (1.0 / size)) * size
    return [
        jnp.where((lane + at == inner) & (lane < n), 1.0, 0.0).astype(BF) for _, at, n in rows_of(size)
    ]


def owned(shards, length):
    size = length // shards
    start = lax.broadcasted_iota(jnp.int32, (shards, length), 0) * size
    entry = lax.broadcasted_iota(jnp.int32, (shards, length), 1)
    return (entry >= start) & (entry < start + size)


def unpack_vectors(tiny, targets):
    shards = tiny.shape[1] * tiny.shape[2]
    made = {}
    for half in range(2):
        for place, top, size in FIELDS[half]:
            total = shards * size
            if size not in made:
                made[size] = spots(total, size, 1), owned(shards, total)
            each, mask = made[size]
            tiled = sum(mm(tiny[half, :, :, top + i, :].reshape(shards, TINY), spot) for i, spot in enumerate(each))
            targets[place][...] = jnp.sum(jnp.where(mask, tiled, 0.0), axis=0, keepdims=True)


def place_tile(pos, held, keep, send, rows, line):
    z, y, c, x = pos[0], pos[1], pos[2], pos[3]
    for relative, out in enumerate((keep, send)):
        core = c ^ relative
        swap = core == 0
        for first in range(2):
            for second in range(2):
                dx = jnp.where(swap, first, second)
                dy = jnp.where(swap, second, first)
                for slot, chip in line:
                    shard = chip * 4 + (y ^ dy) * 2 + core
                    start = pl.multiple_of(shard * rows, 16)
                    out[first, second, slot] = held[x ^ dx, pl.ds(start, rows), :]


def whole_line(pos):
    return [(k, (pos[0] + k) & (LINE - 1)) for k in range(LINE)]


def hold(held, tile):
    width = tile.shape[1] // 2
    held[0] = tile[:, :width].astype(BF)
    held[1] = tile[:, width:].astype(BF)


def joined(refs):
    return jnp.concatenate([r[...] for r in refs], axis=1)


def tiny_rows(vectors, fields):
    rows = []
    made = {}
    for vector, (_, _, size) in zip(vectors, fields):
        length = vector.shape[1]
        if size not in made:
            made[size] = spots(length, size, 0), owned(16, length)
        each, mask = made[size]
        own = jnp.where(mask, jnp.broadcast_to(vector, mask.shape), 0.0).astype(BF)
        rows += [mm(own, spot) for spot in each]
    count = len(rows)
    rows = jnp.concatenate(rows + [jnp.zeros((16 * (8 - count), TINY), F32)], axis=0).astype(BF)
    to = lax.broadcasted_iota(jnp.int32, (16 * 48, 128), 0)
    of = lax.broadcasted_iota(jnp.int32, (16 * 48, 128), 1)
    lift = jnp.where(to == (of & 15) * 48 + (of >> 4), 1.0, 0.0).astype(BF)
    return mm(lift, rows).astype(BF)


def grad_in_kernel(pos, x, *refs):
    parts, (keep, send, held) = refs[:-3], refs[-3:]
    for i, ref in enumerate(parts):

        @pl.when(pl.program_id(0) == i)
        def _(ref=ref):
            hold(held, dg(x[...], ref[...], TN))

    place_tile(pos, held, keep, send, 48, whole_line(pos))


def grad_last_kernel(pos, x, part, *refs):
    bq, bv, refs = refs[:THIRDS], refs[THIRDS : 2 * THIRDS], refs[2 * THIRDS :]
    upb, outb, g1, s1, downb, g2, s2, keep, send, held = refs
    hold(held, dg(x[...], part[...], TN))
    take = lambda ref: ref.at[:, :, :, :, pl.ds(0, CW)]
    place_tile(pos, held, take(keep), take(send), 48, whole_line(pos))
    groups = ((joined((*bq, *bv)), upb[...]), [r[...] for r in (outb, g1, s1, downb, g2, s2)])
    for half in range(2):
        held[half, :, :TINY] = tiny_rows(groups[half], FIELDS[half])
    take = lambda ref: ref.at[:, :, :, :, pl.ds(CW, TINY)]
    place_tile(pos, held.at[:, :, pl.ds(0, TINY)], take(keep), take(send), 48, whole_line(pos))


def grad_call(kernel, name, pos, arrays, in_specs, grid, block, shape, index, us):
    held = (2, 16 * 48, CW)
    return pl.pallas_call(
        kernel,
        grid_spec=pltpu.PrefetchScalarGridSpec(
            num_scalar_prefetch=1,
            grid=(grid,),
            in_specs=in_specs,
            out_specs=[pl.BlockSpec(block, index)] * 2,
            scratch_shapes=[pltpu.VMEM(held, BF)],
        ),
        out_shape=[jax.ShapeDtypeStruct(shape, BF)] * 2,
        compiler_params=params(),
        cost_estimate=cost(us),
        name=name,
    )(pos, *arrays)


def whole(array):
    return pl.BlockSpec(array.shape, lambda j, p: (0,) * array.ndim)


def grad_in(pos, x, parts):
    return grad_call(
        grad_in_kernel, "grad_in", pos, (x, *parts), [whole(a) for a in (x, *parts)], len(parts),
        (2, 2, LINE, 48, CW), (2, 2, LINE, 48, CW * len(parts)), lambda j, p: (0, 0, 0, 0, j), 5,
    )


def grad_last(pos, x, part, vectors):
    arrays = (x, part, *vectors)
    shape = (2, 2, LINE, 48, CW + TINY)
    return grad_call(
        grad_last_kernel, "grad_last", pos, arrays, [whole(a) for a in arrays], 1,
        shape, shape, lambda j, p: (0, 0, 0, 0, 0), 4,
    )


def halves(pos, mine, got):
    swap = pos[3] == 0
    return jnp.where(swap, mine, got).astype(F32), jnp.where(swap, got, mine).astype(F32)


def finish_down_kernel(pos, mine, got, down):
    for x, half in enumerate(halves(pos, mine[...], got[...])):
        down[:, CW * x : CW * (x + 1)] = half


def finish_kernel(pos, mine_u, got_u, mine, got, mine_last, got_last, out, up, weight, *vectors):
    width = up.shape[1] // 2
    third = weight.shape[1] // 3
    for x, half in enumerate(halves(pos, mine_u[...], got_u[...])):
        out[:, CW * x : CW * (x + 1)] = half[:, :CW]
        up[:, width * x : width * (x + 1)] = half[:, CW:]
    more = halves(pos, mine[...], got[...])
    for x, last in enumerate(halves(pos, mine_last[...], got_last[...])):
        for t in range(THIRDS):
            for part in range(3):
                start = part * third + (2 * t + x) * 128
                if t < THIRDS - 1:
                    piece = more[x][:, t * CW + part * 128 : t * CW + (part + 1) * 128]
                else:
                    piece = last[:, part * 128 : (part + 1) * 128]
                weight[:, start : start + 128] = piece
        for place, top, size in FIELDS[x]:
            for i, at, n in rows_of(size):
                vectors[place][:, at : at + n] = last[top + i : top + i + 1, CW : CW + n]


def finish(kernel, name, pos, sums, shapes):
    full = lambda shape: pl.BlockSpec(shape, lambda i, p: (0, 0))
    return pl.pallas_call(
        kernel,
        grid_spec=pltpu.PrefetchScalarGridSpec(
            num_scalar_prefetch=1,
            grid=(1,),
            in_specs=[pl.BlockSpec(memory_space=pltpu.VMEM)] * len(sums),
            out_specs=[full(shape) for shape in shapes],
        ),
        out_shape=[jax.ShapeDtypeStruct(shape, F32) for shape in shapes],
        compiler_params=params(),
        name=name,
    )(pos, *sums)


def pair_bias(bias):
    model = bias.shape[1] // 2
    parts = []
    for pair in range(model // 128):
        at = pair * 128
        parts += [bias[:, at : at + 128], jnp.zeros((1, 128), F32), bias[:, model + at : model + at + 128]]
    return jnp.concatenate(parts, axis=1)


def qkv_rows(x, weight, bias, outs):
    y = mm(x[...], flat(weight))
    scale = 1.0 / math.sqrt(x.shape[1] // HEADS)
    for t, out in enumerate(outs):
        width = out.shape[1]
        for at in range(0, width, 128):
            here = y[:, t * width + at : t * width + at + 128]
            place = t * width + at
            if at // 128 % 3 != 1:
                here = here + bias[:, place : place + 128]
            here = here.astype(BF)
            out[:, at : at + 128] = here * jnp.asarray(scale, BF) if at // 128 % 3 == 0 else here


def qkv_fetch_kernel(pos, x, *refs):
    buffers, outs, refs = refs[:8], refs[8 : 8 + THIRDS], refs[8 + THIRDS :]
    vectors, (weight, tiny, bias, sem, sem_tiny) = refs[:8], refs[8:]

    @pl.when(pl.program_id(0) == 0)
    def _():
        copies = fetch_in(pos, buffers, weight, sem)
        small = fetch_tiny(pos, buffers, tiny, THIRDS * CW, sem_tiny)
        for copy in small + copies:
            copy.start()
        for copy in small:
            copy.wait()
        unpack_vectors(tiny, vectors)
        bias[...] = pair_bias(vectors[0][...])
        for copy in copies:
            copy.wait()

    qkv_rows(x, weight, bias, outs)


def qkv_fetch(pos, x, buffers, shards, block=256):
    tokens, model = x.shape
    vec = lambda n: (pl.BlockSpec((1, n), lambda i, p: (0, 0)), jax.ShapeDtypeStruct((1, n), F32))
    vecs = [vec(model * n) for n in (2, 1, 1, 1, 4, 1, 1, 1)]
    return pl.pallas_call(
        qkv_fetch_kernel,
        grid_spec=pltpu.PrefetchScalarGridSpec(
            num_scalar_prefetch=1,
            grid=(tokens // block,),
            in_specs=[pl.BlockSpec((block, model), lambda i, p: (i, 0))]
            + [pl.BlockSpec(memory_space=pl.ANY)] * 8,
            out_specs=[pl.BlockSpec((block, 2 * CW), lambda i, p: (i, 0))] * THIRDS + [v[0] for v in vecs],
            scratch_shapes=[
                pltpu.VMEM((LINE, model // LINE, 3 * model), BF),
                pltpu.VMEM((2, LINE, shards // LINE, 16, TINY), BF),
                pltpu.VMEM((1, 3 * model), F32),
                pltpu.SemaphoreType.DMA,
                pltpu.SemaphoreType.DMA,
            ],
        ),
        out_shape=[jax.ShapeDtypeStruct((tokens, 2 * CW), BF)] * THIRDS + [v[1] for v in vecs],
        compiler_params=params(),
        cost_estimate=cost(10),
        name="qkv_fetch",
    )(pos, x, *buffers)


def qkv_plain_kernel(x, weight, bias, *outs):
    qkv_rows(x, weight, bias, outs)


def qkv(x, weight, bias, block=256):
    tokens, model = x.shape
    full = lambda a: pl.BlockSpec(a.shape, lambda i: (0, 0))
    return pl.pallas_call(
        qkv_plain_kernel,
        grid=(tokens // block,),
        in_specs=[pl.BlockSpec((block, model), lambda i: (i, 0)), full(weight), full(bias)],
        out_specs=[pl.BlockSpec((block, 2 * CW), lambda i: (i, 0))] * THIRDS,
        out_shape=[jax.ShapeDtypeStruct((tokens, 2 * CW), BF)] * THIRDS,
        compiler_params=params(),
    )(x, weight, bias)


def aug(q,k,h,bias,lane):
    own=(lane>=64) if h else (lane<64)
    j0=0 if h else 64
    z=jnp.zeros_like(q)
    one=jnp.where(lane==j0,jnp.ones_like(q),z)
    qa=jnp.where(own,q,one)
    ka=jnp.where(own,k,jnp.where(lane==j0,bias,z))
    return qa,ka,own
def attn_fwd_kernel(cnt,q_ref,k_ref,v_ref,o_ref,l_ref):
    p=pl.program_id(0)
    q=q_ref[...];k=k_ref[...];v=v_ref[...]
    S=q.shape[0]
    lane=lax.broadcasted_iota(jnp.int32,q.shape,1)
    row=lax.broadcasted_iota(jnp.int32,q.shape,0)
    bias=jnp.where(row<cnt[p],0.0,-1e30).astype(BF)
    vt=v.T
    outs=[]
    for h in range(2):
        qa,ka,own=aug(q,k,h,bias,lane)
        s=dg(ka,qa,NT)
        m=jnp.max(s,axis=0,keepdims=True)
        e=jnp.exp(s-m)
        l=jnp.sum(e,axis=0,keepdims=True)
        ot=mm(vt[64*h:64*h+64],e.astype(BF))
        outs.append(ot*(1.0/l))
        l_ref[0,0,h:h+1,:]=m+jnp.log(l)
    o_ref[...]=jnp.concatenate(outs,axis=0).T.astype(BF)
def attn_fwd(rows, counts, pages):
    tokens, width = rows.shape
    length, pairs = tokens // pages, width // CW
    block = lambda o: pl.BlockSpec((length, 128), lambda p, h, c: (p, 3 * h + o))
    return pl.pallas_call(
        attn_fwd_kernel,
        grid_spec=pltpu.PrefetchScalarGridSpec(
            num_scalar_prefetch=1,
            grid=(pages, pairs),
            in_specs=[block(0), block(1), block(2)],
            out_specs=[
                pl.BlockSpec((length, 128), lambda p, h, c: (p, h)),
                pl.BlockSpec((1, 1, 2, length), lambda p, h, c: (p, h, 0, 0)),
            ],
        ),
        out_shape=[
            jax.ShapeDtypeStruct((tokens, pairs * 128), BF),
            jax.ShapeDtypeStruct((pages, pairs, 2, length), F32),
        ],
        compiler_params=params(),
        cost_estimate=cost(3.5 * pairs),
        name="attn_fwd",
    )(counts, rows, rows, rows)


def attn_bwd_plain_kernel(*refs):
    attn_bwd_kernel(pl.program_id(1), *refs)


def attn_bwd_kernel(p,cnt,q_ref,k_ref,v_ref,g_ref,o_ref,l_ref,d_ref,bq_ref,bv_ref):
    q=q_ref[...];k=k_ref[...];v=v_ref[...];g=g_ref[...]
    lane=lax.broadcasted_iota(jnp.int32,q.shape,1)
    row=lax.broadcasted_iota(jnp.int32,q.shape,0)
    bias=jnp.where(row<cnt[p],0.0,-1e30).astype(BF)
    prod=g.astype(F32)*o_ref[...].astype(F32)
    hi=prod.astype(BF); lo=(prod-hi.astype(F32)).astype(BF)
    r8=lax.broadcasted_iota(jnp.int32,(16,128),0); l8=lax.broadcasted_iota(jnp.int32,(16,128),1)
    sel=jnp.where(r8==l8//64,1.0,0.0).astype(BF)
    delta=dg(sel,hi,NT)+dg(sel,lo,NT)
    kt=k.T
    dv=[];dk=[];dqt=[]
    for h in range(2):
        qa,ka,own=aug(q,k,h,bias,lane)
        s=dg(ka,qa,NT)
        pr=jnp.exp(s-l_ref[0,0,h:h+1,:])
        va=jnp.where(own,v,jnp.zeros_like(v))
        dp=dg(va,g,NT)
        ds=(pr*(dp-delta[h:h+1])).astype(BF)
        dv.append(mm(pr.astype(BF),g)); dk.append(mm(ds,q))
        dqt.append(mm(kt[64*h:64*h+64],ds))
    first=lane<64
    dvv=jnp.where(first,dv[0],dv[1])
    dq=jnp.concatenate(dqt,axis=0).T*0.125
    d_ref[:,:128]=dq.astype(BF); d_ref[:,256:]=dvv.astype(BF)
    d_ref[:,128:256]=jnp.where(first,dk[0],dk[1]).astype(BF)
    sq=jnp.sum(dq,axis=0,keepdims=True); sv=jnp.sum(dvv,axis=0,keepdims=True)
    @pl.when(p==0)
    def _():
        bq_ref[...]=sq; bv_ref[...]=sv
    @pl.when(p>0)
    def _():
        bq_ref[...]+=sq; bv_ref[...]+=sv
def attn_bwd(rows, counts, grad, out, totals, pages, at):
    tokens, width = rows.shape
    length, pairs = tokens // pages, width // CW
    block = lambda o: pl.BlockSpec((length, 128), lambda h, p, c: (p, 3 * h + o))
    line = pl.BlockSpec((1, 128), lambda h, p, c: (0, h))
    return pl.pallas_call(
        attn_bwd_plain_kernel,
        grid_spec=pltpu.PrefetchScalarGridSpec(
            num_scalar_prefetch=1,
            grid=(pairs, pages),
            in_specs=[
                block(0),
                block(1),
                block(2),
                pl.BlockSpec((length, 128), lambda h, p, c: (p, h + at)),
                pl.BlockSpec((length, 128), lambda h, p, c: (p, h)),
                pl.BlockSpec((1, 1, 2, length), lambda h, p, c: (p, h, 0, 0)),
            ],
            out_specs=[pl.BlockSpec((length, CW), lambda h, p, c: (p, h))] + [line] * 2,
        ),
        out_shape=[jax.ShapeDtypeStruct((tokens, width), BF)]
        + [jax.ShapeDtypeStruct((1, pairs * 128), F32)] * 2,
        compiler_params=params(),
        cost_estimate=cost(4.5 * pairs),
        name="attn_bwd",
    )(counts, rows, rows, rows, grad, out, totals)


def back_kernel(last, pos, cnt, q, k, v, g, o, l, x_all, prev_all, *refs):
    more = refs[: 2 * (THIRDS - 1) + 7] if last else ()
    d, bq, bv, keep, send, xs, prev, ds, held, *sems = refs[len(more) :]
    step = pl.program_id(0)
    pages = xs.shape[0] // q.shape[0]
    work = ds.shape[1] // CW * pages
    copies = [pltpu.make_async_copy(x_all, xs, sems[0])]
    if not last:
        copies.append(pltpu.make_async_copy(prev_all, prev, sems[1]))

    @pl.when(step == 0)
    def _():
        for copy in copies:
            copy.start()

    @pl.when(step < work)
    def _():
        pair, page = step // pages, step % pages
        rows = pl.ds(pl.multiple_of(page * q.shape[0], 16), q.shape[0])
        here = ds.at[rows, pl.ds(pl.multiple_of(pair * CW, 128), CW)]
        lane = pl.ds(pl.multiple_of(pair * 128, 128), 128)
        attn_bwd_kernel(page, cnt, q, k, v, g, o, l, here, bq.at[:, lane], bv.at[:, lane])
        d[...] = here[...]

    @pl.when(step == work)
    def _():
        for copy in copies:
            copy.wait()

    if last:

        @pl.when(step == work)
        def _():
            hold(held, dg(xs[...], ds[...], TN))
            take = lambda ref: ref.at[:, :, :, :, pl.ds(0, CW)]
            place_tile(pos, held, take(keep), take(send), 48, whole_line(pos))
            half = THIRDS - 1
            biases = (*more[:half], bq, *more[half : 2 * half], bv)
            upb, outb, g1, s1, downb, g2, s2 = more[2 * half :]
            groups = ((joined(biases), upb[...]), [r[...] for r in (outb, g1, s1, downb, g2, s2)])
            for n in range(2):
                held[n, :, :TINY] = tiny_rows(groups[n], FIELDS[n])
            take = lambda ref: ref.at[:, :, :, :, pl.ds(CW, TINY)]
            place_tile(pos, held.at[:, :, pl.ds(0, TINY)], take(keep), take(send), 48, whole_line(pos))

    else:
        for i, ref in enumerate((prev, ds)):

            @pl.when(step == work + i)
            def _(ref=ref):
                hold(held, dg(xs[...], ref[...], TN))
                place_tile(pos, held, keep, send, 48, whole_line(pos))


def back_third(pos, counts, rows, grad, out, totals, pages, at, x, prev, vectors=None):
    tokens, width = rows.shape
    model = x.shape[1]
    length, pairs = tokens // pages, width // CW
    work = pairs * pages
    last = vectors is not None
    pair = lambda i: jnp.minimum(i, work - 1) // pages
    page = lambda i: jnp.minimum(i, work - 1) % pages
    part = lambda o: pl.BlockSpec((length, 128), lambda i, p, c: (page(i), 3 * pair(i) + o))
    full = lambda a: pl.BlockSpec(a.shape, lambda i, p, c: (0, 0))
    line = pl.BlockSpec((1, pairs * 128), lambda i, p, c: (0, 0))
    any_space = pl.BlockSpec(memory_space=pl.ANY)
    wide = CW + TINY if last else CW
    grads = pl.BlockSpec((2, 2, LINE, 48, wide), lambda i, p, c: (0, 0, 0, 0, jnp.maximum(i - work, 0)))
    shape = (2, 2, LINE, 48, wide if last else 2 * CW)
    vectors = tuple(vectors or ())
    return pl.pallas_call(
        functools.partial(back_kernel, last),
        grid_spec=pltpu.PrefetchScalarGridSpec(
            num_scalar_prefetch=2,
            grid=(work + (1 if last else 2),),
            in_specs=[
                part(0),
                part(1),
                part(2),
                pl.BlockSpec((length, 128), lambda i, p, c: (page(i), pair(i) + at)),
                pl.BlockSpec((length, 128), lambda i, p, c: (page(i), pair(i))),
                pl.BlockSpec((1, 1, 2, length), lambda i, p, c: (page(i), pair(i), 0, 0)),
                any_space,
                any_space,
            ]
            + [full(a) for a in vectors],
            out_specs=[pl.BlockSpec((length, CW), lambda i, p, c: (page(i), pair(i)))]
            + [line] * 2
            + [grads] * 2,
            scratch_shapes=[
                pltpu.VMEM((tokens, model), BF),
                pltpu.VMEM((tokens, width), BF),
                pltpu.VMEM((tokens, width), BF),
                pltpu.VMEM((2, 16 * 48, CW), BF),
                pltpu.SemaphoreType.DMA,
                pltpu.SemaphoreType.DMA,
            ],
        ),
        out_shape=[jax.ShapeDtypeStruct((tokens, width), BF)]
        + [jax.ShapeDtypeStruct((1, pairs * 128), F32)] * 2
        + [jax.ShapeDtypeStruct(shape, BF)] * 2,
        compiler_params=params(),
        cost_estimate=cost(13),
        name="back_last" if last else "back_third",
    )(pos, counts, rows, rows, rows, grad, out, totals, x, prev, *vectors)


def norm(t):
    m=jnp.mean(t,axis=-1,keepdims=True); c=t-m
    v=jnp.mean(c*c,axis=-1,keepdims=True); inv=lax.rsqrt(v+1e-12)
    return c*inv,inv
def norm_back(e,hat,inv):
    return inv*(e-jnp.mean(e,axis=-1,keepdims=True)-hat*jnp.mean(e*hat,axis=-1,keepdims=True))
def col(t): return jnp.sum(t,axis=0,keepdims=True)
C=768
def rows_at(ref, start, count):
    if len(ref.shape) == 2:
        return ref[start : start + count, :]
    each = ref.shape[1]
    return ref[start // each, start % each : start % each + count, :]


def main_fetch_kernel(pos, *refs):
    att, (x, cot), refs = refs[:-49], refs[-49:-47], refs[-47:]
    two, three, refs = refs[:8], refs[8:16], refs[16:]
    vecs, (out, gf, ga), sums, refs = refs[:7], refs[7:10], refs[10:17], refs[17:]
    keep_d, send_d, keep_u, send_u, refs = *refs[:4], refs[4:]
    slope, ow, uw, dw, big, wide, held, *sems = refs
    act, pre = big.at[0], big.at[1]
    low, back, first, attended = (wide.at[n] for n in range(4))
    step = pl.program_id(0)
    rows = x.shape[0]
    blocks = act.shape[0] // rows
    copies = (
        fetch(pos, two, ow, 48, 0, CW, sems[0]),
        fetch(pos, two, uw, 48, CW, uw.shape[2] // 2, sems[1]),
        fetch(pos, three, dw, dw.shape[1] // 4, 0, CW, sems[2]),
    )

    @pl.when(step == 0)
    def _():
        for group in copies:
            for copy in group:
                copy.start()

    def ready(place):
        @pl.when(step == 0)
        def _():
            for copy in copies[place]:
                copy.wait()

    @pl.when(step < blocks)
    def _():
        here = pl.ds(pl.multiple_of(step * rows, 16), rows)
        attended[here, :] = joined(att)
        main_kernel(
            att, x, cot, ow, uw, dw, *vecs, out,
            act.at[here, :], back.at[here, :], low.at[here, :], pre.at[here, :], first.at[here, :],
            gf, ga, *sums, slope, ready,
        )

    @pl.when((step >= blocks) & (step < blocks + LINE))
    def _():
        chip = (pos[0] + step - blocks) & (LINE - 1)
        columns = act.shape[1] // LINE
        here = pl.ds(pl.multiple_of(chip * columns, 128), columns)
        hold(held, dg(act[:, here], back[...], TN))
        place_tile(pos, held, keep_d, send_d, held.shape[1] // 4, [(0, 0)])

    @pl.when(step == blocks + LINE)
    def _():
        hold(held, dg(attended[...], first[...], TN))
        place_tile(pos, held, keep_u, send_u, 48, whole_line(pos))

    @pl.when(step > blocks + LINE)
    def _():
        at = pl.multiple_of((step - blocks - LINE - 1) * CW, 128)
        right = pl.multiple_of(at + pre.shape[1] // 2, 128)
        columns = jnp.concatenate([pre[:, pl.ds(at, CW)], pre[:, pl.ds(right, CW)]], axis=1)
        hold(held, dg(low[...], columns, TN))
        place_tile(pos, held, keep_u, send_u, 48, whole_line(pos))


def main_fetch(pos, att, x, cot, weights, vecs, rows=512):
    T, D = x.shape
    FF = vecs[3].shape[1]
    blocks, ups = T // rows, FF // 2 // CW
    rb = lambda n: pl.BlockSpec((rows, n), lambda i, p: (jnp.minimum(i, blocks - 1), 0))
    full = lambda a: pl.BlockSpec(a.shape, lambda i, p: (0, 0))
    vec = lambda n: (pl.BlockSpec((1, n), lambda i, p: (0, 0)), jax.ShapeDtypeStruct((1, n), F32))
    vs = [vec(n) for n in (D, D, D, FF, D, D, D)]
    down = pl.BlockSpec(
        (2, 2, 1, FF // 16, CW), lambda i, p: (0, 0, jnp.clip(i - blocks, 0, LINE - 1), 0, 0)
    )
    up = pl.BlockSpec(
        (2, 2, LINE, 48, CW), lambda i, p: (0, 0, 0, 0, jnp.clip(i - blocks - LINE, 0, ups))
    )
    shapes = [(2, 2, LINE, FF // 16, CW)] * 2 + [(2, 2, LINE, 48, CW * (1 + ups))] * 2
    return pl.pallas_call(
        main_fetch_kernel,
        grid_spec=pltpu.PrefetchScalarGridSpec(
            num_scalar_prefetch=1,
            grid=(blocks + LINE + 1 + ups,),
            in_specs=[rb(a.shape[1]) for a in (*att, x, cot)]
            + [pl.BlockSpec(memory_space=pl.ANY)] * len(weights)
            + [full(v) for v in vecs],
            out_specs=[rb(D)] * 3 + [v[0] for v in vs] + [down, down, up, up],
            scratch_shapes=[
                pltpu.VMEM((rows, FF), BF),
                pltpu.VMEM((LINE, D // LINE, D), BF),
                pltpu.VMEM((LINE, D // LINE, FF), BF),
                pltpu.VMEM((LINE, FF // LINE, D), BF),
                pltpu.VMEM((2, T, FF), BF),
                pltpu.VMEM((4, T, D), BF),
                pltpu.VMEM((2, 16 * 48, CW), BF),
            ]
            + [pltpu.SemaphoreType.DMA] * 3,
        ),
        out_shape=[jax.ShapeDtypeStruct((T, D), t) for t in (BF, F32, BF)]
        + [v[1] for v in vs]
        + [jax.ShapeDtypeStruct(a, BF) for a in shapes],
        compiler_params=params(),
        cost_estimate=cost(58),
        name="main",
    )(pos, *att, x, cot, *weights, *vecs)


def main_plain_kernel(*refs):
    main_kernel(refs[:-28], *refs[-28:])


def main_kernel(att,x,cot,ow,uw,dw,ob,g1,s1,ub,db,g2,s2,
                lo_ref,act_ref,sl_ref,nl_ref,pl_ref,fl_ref,gf_ref,ga_ref,
                vg2,vs2,vdb,vub,vg1,vs1,vob,slope,ready=lambda place: None):
    i=pl.program_id(0)
    FF=uw.shape[-1]
    ready(0)
    fs=x[...].astype(F32)+mm(joined(att),flat(ow))+ob[...]
    fh,fi=norm(fs)
    normed=fh*g1[...]+s1[...]
    nl=normed.astype(BF); nl_ref[...]=nl
    acc=normed+db[...]
    ready(1)
    for j in range(0,FF,C):
        pre=mm(nl,flat(uw,j,C))+ub[:,j:j+C]
        phi=0.5*(1.0+lax.erf(pre*(1.0/math.sqrt(2.0))))
        a=(pre*phi).astype(BF)
        act_ref[:,j:j+C]=a
        slope[:,j:j+C]=(phi+pre*jnp.exp(-0.5*pre*pre)*(1.0/math.sqrt(2.0*math.pi))).astype(slope.dtype)
        if j==0: ready(2)
        acc=acc+mm(a,rows_at(dw,j,C))
    sh,si=norm(acc)
    lo_ref[...]=(sh*g2[...]+s2[...]).astype(BF)
    gr=cot[...].astype(F32)
    gs=norm_back(gr*g2[...],sh,si)
    sl=gs.astype(BF); sl_ref[...]=sl
    gn=gs
    ubs=[]
    for j in range(0,FF,C):
        gp=dg(sl,rows_at(dw,j,C),NT)*slope[:,j:j+C]
        ubs.append(col(gp))
        gpl=gp.astype(BF); pl_ref[:,j:j+C]=gpl
        gn=gn+dg(gpl,flat(uw,j,C),NT)
    gf=norm_back(gn*g1[...],fh,fi)
    fl=gf.astype(BF); fl_ref[...]=fl; gf_ref[...]=gf
    ga_ref[...]=dg(fl,flat(ow),NT).astype(BF)
    vals=[(vg2,col(gr*sh)),(vs2,col(gr)),(vdb,col(gs)),(vub,jnp.concatenate(ubs,1)),(vg1,col(gn*fh)),(vs1,col(gn)),(vob,col(gf))]
    @pl.when(i==0)
    def _():
        for r,v in vals: r[...]=v
    @pl.when(i>0)
    def _():
        for r,v in vals: r[...]+=v
def main(att, x, cot, weights, vecs, R=256):
    T, D = x.shape
    FF = vecs[3].shape[1]
    rb = lambda n: pl.BlockSpec((R, n), lambda i: (i, 0))
    full = lambda a: pl.BlockSpec(a.shape, lambda i: (0, 0))
    sds = lambda n, t=BF: jax.ShapeDtypeStruct((T, n), t)
    vec = lambda n: (pl.BlockSpec((1, n), lambda i: (0, 0)), jax.ShapeDtypeStruct((1, n), F32))
    vs = [vec(n) for n in (D, D, D, FF, D, D, D)]
    return pl.pallas_call(
        main_plain_kernel,
        grid=(T // R,),
        in_specs=[rb(a.shape[1]) for a in (*att, x, cot)] + [full(w) for w in weights] + [full(v) for v in vecs],
        out_specs=[rb(D), rb(FF), rb(D), rb(D), rb(FF), rb(D), rb(D), rb(D)] + [v[0] for v in vs],
        out_shape=[sds(D), sds(FF), sds(D), sds(D), sds(FF), sds(D), sds(D, F32), sds(D)] + [v[1] for v in vs],
        scratch_shapes=[pltpu.VMEM((R, FF), F32)],
        compiler_params=params(),
        name="main",
    )(*att, x, cot, *weights, *vecs)


def tn_kernel(a,b,o): o[...]=dg(a[...],b[...],TN).astype(BF)
def tn(a,b,bm,bn):
    T,M=a.shape;N=b.shape[1]
    return pl.pallas_call(tn_kernel,grid=(M//bm,N//bn),
      in_specs=[pl.BlockSpec((T,bm),lambda i,j:(0,i)),pl.BlockSpec((T,bn),lambda i,j:(0,j))],
      out_specs=pl.BlockSpec((bm,bn),lambda i,j:(i,j)),out_shape=jax.ShapeDtypeStruct((M,N),BF),compiler_params=params())(a,b)
def ig_kernel(gf, parts, w, o):
    o[...] = (gf[...] + dg(joined(parts), flat(w), NT)).astype(BF)


def ig_plain_kernel(gf, *refs):
    ig_kernel(gf, refs[:-2], refs[-2], refs[-1])


def ig_fetch_kernel(pos, gf, *refs):
    parts, buffers, (o, weight, sem) = refs[:-11], refs[-11:-3], refs[-3:]

    @pl.when(pl.program_id(0) == 0)
    def _():
        run_all(fetch_in(pos, buffers, weight, sem))

    ig_kernel(gf, parts, weight, o)


def ig(parts, gf, weights, pos=None, R=256):
    T, D = gf.shape
    rb = lambda n: pl.BlockSpec((R, n), lambda i, *p: (i, 0))
    fetched = pos is not None
    return pl.pallas_call(
        ig_fetch_kernel if fetched else ig_plain_kernel,
        grid_spec=pltpu.PrefetchScalarGridSpec(
            num_scalar_prefetch=1 if fetched else 0,
            grid=(T // R,),
            in_specs=[rb(a.shape[1]) for a in (gf, *parts)]
            + [pl.BlockSpec(memory_space=pl.ANY) if fetched else pl.BlockSpec(w.shape, lambda i, *p: (0, 0)) for w in weights],
            out_specs=rb(D),
            scratch_shapes=[pltpu.VMEM((LINE, D // LINE, 3 * D), BF), pltpu.SemaphoreType.DMA] if fetched else [],
        ),
        out_shape=jax.ShapeDtypeStruct((T, D), BF),
        compiler_params=params(),
        cost_estimate=cost(10),
        name="ig",
    )(*([pos] if fetched else []), gf, *parts, *weights)


def local(
    hidden_states,
    page_counts,
    cotangent,
    attn_in_weight,
    attn_in_bias,
    attn_out_weight,
    attn_out_bias,
    first_gain,
    first_shift,
    up_weight,
    up_bias,
    down_weight,
    down_bias,
    second_gain,
    second_shift,
):
    pages, length, model = hidden_states.shape
    hidden = up_weight.shape[1]
    x = hidden_states.reshape(-1, model)
    grad_rows = cotangent.reshape(-1, model)
    weights = (attn_in_weight, attn_out_weight, up_weight, down_weight)
    vectors = (
        attn_in_bias,
        attn_out_bias,
        first_gain,
        first_shift,
        up_bias,
        down_bias,
        second_gain,
        second_shift,
    )
    lined = lax.axis_size("fsdp") == 4 * LINE and lax.axis_size("rep") == 2
    pairs = HEADS // 2 // THIRDS
    forward = [None] * THIRDS
    backward = [None] * THIRDS

    def ahead(t, rows):
        forward[t] = attn_fwd(rows, page_counts, pages)

    def back(t, rows):
        backward[t] = attn_bwd(rows, page_counts, grad_att, *forward[t], pages, pairs * t)

    if lined:
        index = lax.axis_index("fsdp")
        pos = jnp.stack([index // 4, index // 2 % 2, index % 2, lax.axis_index("rep")]).astype(jnp.int32)
        one, two, three = pack(pos, weights, vectors)
        line_one = in_order(along_line(one))
        second_one = move(line_one, to_second)
        first_one = move(line_one, to_first)
        parts_two = along_line(after(two, line_one))
        parts_three = along_line(after(three, line_one))
        both_one = move(after(second_one, *parts_two[1:]), to_first)
        in_w = over_core((line_one, first_one, second_one, both_one))
        line_two = in_order(parts_two)
        second_two = move(line_two, to_second)
        first_two = move(line_two, to_first)
        outs = qkv_fetch(pos, x, after(in_w, line_two), 16)
        rows, full = outs[:THIRDS], outs[THIRDS:]
        line_three = in_order(after(parts_three, rows))
        second_three = move(line_three, to_second)
        first_three = move(line_three, to_first)
        ahead(0, after(rows[0], line_three))
        both_two = move(after(second_two, forward[0]), to_first)
        ahead(1, after(rows[1], forward[0], second_two))
        both_three = move(after(second_three, forward[1]), to_first)
        early = [move(part, to_core) for part in after((line_two,), forward[0])]
        ready = (line_two, first_two, second_two, line_three, first_three, second_three)
        moved = [move(part, to_core) for part in after(ready[1:], forward[1])]
        ahead(2, after(rows[2], forward[1], second_three, first_three, *early))
        ready += (*early, *moved)
        last = over_core(after((both_two, both_three), forward[2]))
        later = (*ready[0:3], last[0], *ready[6:9], last[2], *ready[3:6], last[1], *ready[9:12], last[3])
    else:
        pos = None
        gathered = lambda a: lax.all_gather(a, "fsdp", axis=0, tiled=True)
        in_w = gathered(attn_in_weight).reshape(model, 3, -1, 128)
        in_w = (in_w.transpose(0, 2, 1, 3).reshape(model, 3 * model),)
        full = [gathered(v).astype(F32).reshape(1, -1) for v in vectors]
        later = tuple(gathered(w) for w in weights[1:])
        rows = qkv(x, in_w[0], pair_bias(full[0]))
        for t in range(THIRDS):
            ahead(t, rows[t])
    attended = [f[0] for f in forward]
    if lined:
        (
            output, grad_first, grad_att, vg2, vs2, vdb, vub, vg1, vs1, vob,
            keep_d, send_d, keep_u, send_u,
        ) = main_fetch(pos, attended, x, grad_rows, later, full[1:])
        core_d = move(send_d, to_core)
        core_u = move(send_u, to_core)
        back(0, rows[0])
        go_d, stay_d = add_wide(*after((keep_d, core_d), backward[0]))
        first_d = move(go_d, to_first)
        go_u, stay_u = add_wide(*after((keep_u, core_u), go_d))
        first_u = move(go_u, to_first)
        *backward[1], keep_i, send_i = back_third(
            pos, page_counts, after(rows[1], go_u, stay_u), grad_att, *forward[1], pages, pairs, x, backward[0][0]
        )
        go_d, stay_d = add_core(*after((stay_d, first_d), backward[1]))
        second_d = move(go_d, to_second)
        core_i = move(send_i, to_core)
        back(2, after(rows[2], keep_i))
        parts = tuple(b[0] for b in backward)
        vbq = [b[1] for b in backward]
        vbv = [b[2] for b in backward]
        go_u, stay_u = add_core(*after((stay_u, first_u), backward[2]))
        second_u = move(go_u, to_second)
        go_i, stay_i = add_wide(*after((keep_i, core_i), go_u, stay_u))
        first_i = move(go_i, to_first)
        low_d = add_last(*after((stay_d, second_d), go_i))
        line_d = move_line(low_d)
        keep_l, send_l = grad_last(
            pos, x, after(parts[2], go_i, stay_i, low_d), (*vbq, *vbv, vub, vob, vg1, vs1, vdb, vg2, vs2)
        )
        core_l = move(send_l, to_core)
        mine_d = add_line(low_d, after(line_d, keep_l))
        low_u = add_last(*after((stay_u, second_u), mine_d))
        line_u = move_line(low_u)
        go_l, stay_l = add_core(keep_l, after(core_l, low_u))
        first_l = move(go_l, to_first)
        go_i, stay_i = add_core(*after((stay_i, first_i), go_l, stay_l))
        second_i = move(go_i, to_second)
        input_grad = ig(parts, after(grad_first, go_i, stay_i), in_w, pos)
        mine_u = add_line(low_u, after(line_u, input_grad))
        low_i = add_last(*after((stay_i, second_i), mine_u))
        line_i = move_line(low_i)
        go_l, stay_l = add_core(*after((stay_l, first_l), low_i))
        second_l = move(go_l, to_second)
        got_d = move(after(mine_d, go_l), to_x)
        low_l = add_last(*after((stay_l, second_l), go_l))
        mine_i = add_line(low_i, after(line_i, low_l))
        line_l = move_line(after(low_l, mine_i))
        got_u = move(after(mine_u, mine_i), to_x)
        got_i = move(mine_i, to_x)
        (t_down,) = finish(
            finish_down_kernel, "finish_down", pos, (mine_d, after(got_d, low_l)), [down_weight.shape]
        )
        mine_l = add_line(low_l, after(line_l, t_down))
        got_l = move(mine_l, to_x)
        shapes = [attn_out_weight.shape, up_weight.shape, attn_in_weight.shape]
        shapes += [(1, v.shape[0]) for v in vectors]
        t_out, t_up, t_in, *small = finish(
            finish_kernel, "finish", pos, (mine_u, got_u, mine_i, got_i, mine_l, got_l), shapes
        )
        small = [b.reshape(-1) for b in small]
    else:
        (
            output, act, second_low, normed_low, pre_low, first_low, grad_first, grad_att,
            vg2, vs2, vdb, vub, vg1, vs1, vob,
        ) = main(attended, x, grad_rows, later, full[1:])
        for t in range(THIRDS):
            back(t, rows[t])
        parts = tuple(b[0] for b in backward)
        vbq = jnp.concatenate([b[1] for b in backward], axis=1)
        vbv = jnp.concatenate([b[2] for b in backward], axis=1)
        input_grad = ig(parts, grad_first, in_w)

        def total(a):
            share = lax.psum_scatter(a.astype(BF), "fsdp", scatter_dimension=0, tiled=True)
            return lax.psum(share, "rep").astype(F32)

        att = jnp.concatenate(attended, axis=1)
        t_down = total(tn(act, second_low, 768, 768))
        t_up = total(tn(normed_low, pre_low, 768, 768))
        t_out = total(tn(att, first_low, 768, 768))
        t_in = jnp.concatenate([tn(x, d, 768, 768) for d in parts], axis=1)
        t_in = total(t_in.reshape(model, -1, 3, 128).transpose(0, 2, 1, 3).reshape(model, 3 * model))
        small = [
            total(v.reshape(-1))
            for v in (jnp.concatenate([vbq, vbv], axis=1), vob, vg1, vs1, vub, vdb, vg2, vs2)
        ]
    b_in, b_out, b_g1, b_s1, b_up, b_down, b_g2, b_s2 = small
    return (
        output.reshape(hidden_states.shape),
        input_grad.reshape(hidden_states.shape),
        t_in, b_in, t_out, b_out, b_g1, b_s1, t_up, b_up, t_down, b_down, b_g2, b_s2,
    )


def solution(mesh):
    return jax.shard_map(
        local,
        mesh=mesh,
        in_specs=(
            P(("fsdp", "rep"), None, None),
            P(("fsdp", "rep")),
            P(("fsdp", "rep"), None, None),
            P("fsdp", None),
            P("fsdp"),
            P("fsdp", None),
            P("fsdp"),
            P("fsdp"),
            P("fsdp"),
            P("fsdp", None),
            P("fsdp"),
            P("fsdp", None),
            P("fsdp"),
            P("fsdp"),
            P("fsdp"),
        ),
        out_specs=(
            P(("fsdp", "rep"), None, None),
            P(("fsdp", "rep"), None, None),
            P("fsdp", None),
            P("fsdp"),
            P("fsdp", None),
            P("fsdp"),
            P("fsdp"),
            P("fsdp"),
            P("fsdp", None),
            P("fsdp"),
            P("fsdp", None),
            P("fsdp"),
            P("fsdp"),
            P("fsdp"),
        ),
        check_vma=False,
    )
```

```python
import math

import jax
import jax.numpy as jnp
from jax import lax
from jax.experimental import pallas as pl
from jax.experimental.pallas import tpu as pltpu
from jax.sharding import PartitionSpec as P

HEADS = 12
BF = jnp.bfloat16
F32 = jnp.float32
NT = (((1,), (1,)), ((), ()))
TN = (((0,), (0,)), ((), ()))
CW = 384
THIRDS = 3
LINE = 4
TINY = 128
AXES = ("fsdp", "rep")


def dg(a, b, dims):
    return lax.dot_general(a, b, dims, preferred_element_type=F32)


def mm(a, b):
    return jnp.dot(a, b, preferred_element_type=F32)


def params():
    return pltpu.CompilerParams(vmem_limit_bytes=60 * 1024 * 1024)


def cost(us):
    return pl.CostEstimate(flops=int(us * 1.15e9), bytes_accessed=int(us * 1e6), transcendentals=0)


def flat_index(z, y, c, x):
    return (z * 4 + y * 2 + c) * 2 + x


def permutation(target):
    pairs = []
    for z in range(LINE):
        for y in range(2):
            for c in range(2):
                for x in range(2):
                    pairs.append((flat_index(z, y, c, x), flat_index(*target(z, y, c, x))))
    return pairs


def to_core(z, y, c, x):
    return (z, y, 1 - c, x)


def to_x(z, y, c, x):
    return (z, y, c, 1 - x)


def to_first(z, y, c, x):
    return (z, y, c, 1 - x) if c == 0 else (z, 1 - y, c, x)


def to_second(z, y, c, x):
    return (z, 1 - y, c, x) if c == 0 else (z, y, c, 1 - x)


def to_line(step):
    return lambda z, y, c, x: ((z + step) % LINE, y, c, x)


def move(value, target):
    return lax.ppermute(value, AXES, permutation(target))


def after(values, *earlier):
    return lax.optimization_barrier((values, earlier))[0]


def along_line(half):
    return [half] + [move(half, to_line(k)) for k in range(1, LINE)]


def in_order(parts):
    here = lax.axis_index("fsdp") // 4
    return jnp.stack([lax.select_n((here - chip) & (LINE - 1), *parts) for chip in range(LINE)])


def over_core(parts):
    return tuple(parts) + tuple(move(part, to_core) for part in parts)


def add_core(keep, got):
    keep, got = keep.astype(F32), got.astype(F32)
    return (keep[1] + got[1]).astype(BF), (keep[0] + got[0]).astype(BF)


def add_kernel(keep, got, go, stay):
    total = keep[...].astype(F32) + got[...].astype(F32)
    stay[...] = total[0].astype(BF)
    go[...] = total[1].astype(BF)


def add_wide(keep, got):
    _, second, line, rows, width = keep.shape
    both = pl.BlockSpec((2, 1, line, rows, width), lambda i: (0, i, 0, 0, 0))
    one = pl.BlockSpec((1, line, rows, width), lambda i: (i, 0, 0, 0))
    return pl.pallas_call(
        add_kernel,
        grid=(second,),
        in_specs=[both, both],
        out_specs=[one, one],
        out_shape=[jax.ShapeDtypeStruct(keep.shape[1:], BF)] * 2,
        compiler_params=params(),
        cost_estimate=cost(4),
        name="add_wide",
    )(keep, got)


def add_last(stay, got):
    return (stay.astype(F32) + got.astype(F32)).astype(BF)


def add_line(low, parts):
    total = low[0].astype(F32)
    for part in parts:
        total = total + part.astype(F32)
    return total.astype(BF)


def move_line(low):
    return [move(low[k], to_line(k)) for k in range(1, LINE)]


FIELDS = (((0, 0, 96), (4, 1, 192)), tuple((n, i, 48) for i, n in enumerate((1, 2, 3, 5, 6, 7))))


def rows_of(width):
    return [(i, at, min(TINY, width - at)) for i, at in enumerate(range(0, width, TINY))]


def pack_kernel(pos, inw, outw, upw, downw, *refs):
    vectors, (one, two, three) = refs[:8], refs[8:]

    def fill(x):
        third = inw.shape[1] // 3
        for t in range(THIRDS):
            for part in range(3):
                start = part * third + (2 * t + x) * 128
                piece = inw[:, start : start + 128]
                one[:, t * CW + part * 128 : t * CW + (part + 1) * 128] = piece
        row = lax.broadcasted_iota(jnp.int32, (48, TINY), 0)
        block = jnp.zeros((48, TINY), F32)
        for place, top, size in FIELDS[x]:
            for i, at, n in rows_of(size):
                piece = vectors[place][at : at + n].astype(F32).reshape(1, n)
                if n < TINY:
                    piece = jnp.concatenate([piece, jnp.zeros((1, TINY - n), F32)], axis=1)
                block = jnp.where(row == top + i, jnp.broadcast_to(piece, (48, TINY)), block)
        one[:, THIRDS * CW :] = block.astype(BF)
        two[:, :CW] = outw[:, x * CW : (x + 1) * CW]
        width = upw.shape[1] // 2
        two[:, CW:] = upw[:, x * width : (x + 1) * width]
        three[...] = downw[:, x * CW : (x + 1) * CW]

    @pl.when(pos[3] == 0)
    def _():
        fill(0)

    @pl.when(pos[3] == 1)
    def _():
        fill(1)


def pack(pos, weights, vectors):
    shapes = [
        (48, weights[0].shape[1] // 2 + TINY),
        (48, weights[1].shape[1] // 2 + weights[2].shape[1] // 2),
        (weights[3].shape[0], CW),
    ]
    arrays = tuple(weights) + tuple(vectors)
    full = lambda a: pl.BlockSpec(a, lambda i, p: (0,) * len(a))
    return pl.pallas_call(
        pack_kernel,
        grid_spec=pltpu.PrefetchScalarGridSpec(
            num_scalar_prefetch=1,
            grid=(1,),
            in_specs=[full(a.shape) for a in arrays],
            out_specs=[full(a) for a in shapes],
        ),
        out_shape=[jax.ShapeDtypeStruct(a, BF) for a in shapes],
        compiler_params=params(),
        name="pack",
    )(pos, *arrays)


def sources(pos):
    y, c, x = pos[1], pos[2], pos[3]
    found = []
    for other in range(2):
        core = c ^ 1 if other else c
        swap = core == 0
        for first in range(2):
            for second in range(2):
                dx = jnp.where(swap, first, second)
                dy = jnp.where(swap, second, first)
                found.append((other * 4 + second * 2 + first, (y ^ dy) * 2 + core, x ^ dx))
    return found


def fetch(pos, buffers, target, rows, column, width, sem, stride=None, start=0):
    stride = width if stride is None else stride
    return [
        pltpu.make_async_copy(
            buffers[buffer].at[:, :, pl.ds(column, width)],
            target.at[
                :,
                pl.ds(pl.multiple_of(place * rows, 16), rows),
                pl.ds(pl.multiple_of(start + x * stride, 128), width),
            ],
            sem,
        )
        for buffer, place, x in sources(pos)
    ]


def fetch_in(pos, buffers, target, sem):
    copies = []
    for t in range(THIRDS):
        copies += fetch(pos, buffers, target, 48, t * CW, CW, sem, None, 2 * CW * t)
    return copies


def fetch_tiny(pos, buffers, target, column, sem):
    return [
        pltpu.make_async_copy(
            buffers[buffer].at[:, pl.ds(0, 16), pl.ds(column, TINY)], target.at[x, :, place], sem
        )
        for buffer, place, x in sources(pos)
    ]


def flat(ref, start=0, width=None):
    width = ref.shape[-1] if width is None else width
    return ref[:, :, start : start + width].reshape(-1, width) if len(ref.shape) == 3 else ref[:, start : start + width]


def run_all(copies):
    for copy in copies:
        copy.start()
    for copy in copies:
        copy.wait()


def spots(length, size, axis):
    shape = (length, TINY) if axis == 0 else (TINY, length)
    entry = lax.broadcasted_iota(jnp.int32, shape, axis).astype(F32)
    lane = lax.broadcasted_iota(jnp.int32, shape, 1 - axis).astype(F32)
    inner = entry - jnp.floor((entry + 0.5) * (1.0 / size)) * size
    return [
        jnp.where((lane + at == inner) & (lane < n), 1.0, 0.0).astype(BF) for _, at, n in rows_of(size)
    ]


def owned(shards, length):
    size = length // shards
    start = lax.broadcasted_iota(jnp.int32, (shards, length), 0) * size
    entry = lax.broadcasted_iota(jnp.int32, (shards, length), 1)
    return (entry >= start) & (entry < start + size)


def unpack_vectors(tiny, targets):
    shards = tiny.shape[1] * tiny.shape[2]
    made = {}
    for half in range(2):
        for place, top, size in FIELDS[half]:
            total = shards * size
            if size not in made:
                made[size] = spots(total, size, 1), owned(shards, total)
            each, mask = made[size]
            tiled = sum(mm(tiny[half, :, :, top + i, :].reshape(shards, TINY), spot) for i, spot in enumerate(each))
            targets[place][...] = jnp.sum(jnp.where(mask, tiled, 0.0), axis=0, keepdims=True)


def place_tile(pos, held, keep, send, rows, line):
    z, y, c, x = pos[0], pos[1], pos[2], pos[3]
    for relative, out in enumerate((keep, send)):
        core = c ^ relative
        swap = core == 0
        for first in range(2):
            for second in range(2):
                dx = jnp.where(swap, first, second)
                dy = jnp.where(swap, second, first)
                for slot, chip in line:
                    shard = chip * 4 + (y ^ dy) * 2 + core
                    start = pl.multiple_of(shard * rows, 16)
                    out[first, second, slot] = held[x ^ dx, pl.ds(start, rows), :]


def whole_line(pos):
    return [(k, (pos[0] + k) & (LINE - 1)) for k in range(LINE)]


def hold(held, tile):
    width = tile.shape[1] // 2
    held[0] = tile[:, :width].astype(BF)
    held[1] = tile[:, width:].astype(BF)


def joined(refs):
    return jnp.concatenate([r[...] for r in refs], axis=1)


def tiny_rows(vectors, fields):
    rows = []
    made = {}
    for vector, (_, _, size) in zip(vectors, fields):
        length = vector.shape[1]
        if size not in made:
            made[size] = spots(length, size, 0), owned(16, length)
        each, mask = made[size]
        own = jnp.where(mask, jnp.broadcast_to(vector, mask.shape), 0.0).astype(BF)
        rows += [mm(own, spot) for spot in each]
    count = len(rows)
    rows = jnp.concatenate(rows + [jnp.zeros((16 * (8 - count), TINY), F32)], axis=0).astype(BF)
    to = lax.broadcasted_iota(jnp.int32, (16 * 48, 128), 0)
    of = lax.broadcasted_iota(jnp.int32, (16 * 48, 128), 1)
    lift = jnp.where(to == (of & 15) * 48 + (of >> 4), 1.0, 0.0).astype(BF)
    return mm(lift, rows).astype(BF)


def grad_in_kernel(pos, x, *refs):
    parts, (keep, send, held) = refs[:-3], refs[-3:]
    for i, ref in enumerate(parts):

        @pl.when(pl.program_id(0) == i)
        def _(ref=ref):
            hold(held, dg(x[...], ref[...], TN))

    place_tile(pos, held, keep, send, 48, whole_line(pos))


def grad_last_kernel(pos, x, part, *refs):
    bq, bv, refs = refs[:THIRDS], refs[THIRDS : 2 * THIRDS], refs[2 * THIRDS :]
    upb, outb, g1, s1, downb, g2, s2, keep, send, held = refs
    hold(held, dg(x[...], part[...], TN))
    take = lambda ref: ref.at[:, :, :, :, pl.ds(0, CW)]
    place_tile(pos, held, take(keep), take(send), 48, whole_line(pos))
    groups = ((joined((*bq, *bv)), upb[...]), [r[...] for r in (outb, g1, s1, downb, g2, s2)])
    for half in range(2):
        held[half, :, :TINY] = tiny_rows(groups[half], FIELDS[half])
    take = lambda ref: ref.at[:, :, :, :, pl.ds(CW, TINY)]
    place_tile(pos, held.at[:, :, pl.ds(0, TINY)], take(keep), take(send), 48, whole_line(pos))


def grad_call(kernel, name, pos, arrays, in_specs, grid, block, shape, index, us):
    held = (2, 16 * 48, CW)
    return pl.pallas_call(
        kernel,
        grid_spec=pltpu.PrefetchScalarGridSpec(
            num_scalar_prefetch=1,
            grid=(grid,),
            in_specs=in_specs,
            out_specs=[pl.BlockSpec(block, index)] * 2,
            scratch_shapes=[pltpu.VMEM(held, BF)],
        ),
        out_shape=[jax.ShapeDtypeStruct(shape, BF)] * 2,
        compiler_params=params(),
        cost_estimate=cost(us),
        name=name,
    )(pos, *arrays)


def whole(array):
    return pl.BlockSpec(array.shape, lambda j, p: (0,) * array.ndim)


def grad_in(pos, x, parts):
    return grad_call(
        grad_in_kernel, "grad_in", pos, (x, *parts), [whole(a) for a in (x, *parts)], len(parts),
        (2, 2, LINE, 48, CW), (2, 2, LINE, 48, CW * len(parts)), lambda j, p: (0, 0, 0, 0, j), 5,
    )


def grad_last(pos, x, part, vectors):
    arrays = (x, part, *vectors)
    shape = (2, 2, LINE, 48, CW + TINY)
    return grad_call(
        grad_last_kernel, "grad_last", pos, arrays, [whole(a) for a in arrays], 1,
        shape, shape, lambda j, p: (0, 0, 0, 0, 0), 4,
    )


def halves(pos, mine, got):
    swap = pos[3] == 0
    return jnp.where(swap, mine, got).astype(F32), jnp.where(swap, got, mine).astype(F32)


def finish_down_kernel(pos, mine, got, down):
    for x, half in enumerate(halves(pos, mine[...], got[...])):
        down[:, CW * x : CW * (x + 1)] = half


def finish_kernel(pos, mine_u, got_u, mine, got, mine_last, got_last, out, up, weight, *vectors):
    width = up.shape[1] // 2
    third = weight.shape[1] // 3
    for x, half in enumerate(halves(pos, mine_u[...], got_u[...])):
        out[:, CW * x : CW * (x + 1)] = half[:, :CW]
        up[:, width * x : width * (x + 1)] = half[:, CW:]
    more = halves(pos, mine[...], got[...])
    for x, last in enumerate(halves(pos, mine_last[...], got_last[...])):
        for t in range(THIRDS):
            for part in range(3):
                start = part * third + (2 * t + x) * 128
                if t < THIRDS - 1:
                    piece = more[x][:, t * CW + part * 128 : t * CW + (part + 1) * 128]
                else:
                    piece = last[:, part * 128 : (part + 1) * 128]
                weight[:, start : start + 128] = piece
        for place, top, size in FIELDS[x]:
            for i, at, n in rows_of(size):
                vectors[place][:, at : at + n] = last[top + i : top + i + 1, CW : CW + n]


def finish(kernel, name, pos, sums, shapes):
    full = lambda shape: pl.BlockSpec(shape, lambda i, p: (0, 0))
    return pl.pallas_call(
        kernel,
        grid_spec=pltpu.PrefetchScalarGridSpec(
            num_scalar_prefetch=1,
            grid=(1,),
            in_specs=[pl.BlockSpec(memory_space=pltpu.VMEM)] * len(sums),
            out_specs=[full(shape) for shape in shapes],
        ),
        out_shape=[jax.ShapeDtypeStruct(shape, F32) for shape in shapes],
        compiler_params=params(),
        name=name,
    )(pos, *sums)


def pair_bias(bias):
    model = bias.shape[1] // 2
    parts = []
    for pair in range(model // 128):
        at = pair * 128
        parts += [bias[:, at : at + 128], jnp.zeros((1, 128), F32), bias[:, model + at : model + at + 128]]
    return jnp.concatenate(parts, axis=1)


def qkv_rows(x, weight, bias, outs):
    y = mm(x[...], flat(weight))
    scale = 1.0 / math.sqrt(x.shape[1] // HEADS)
    for t, out in enumerate(outs):
        width = out.shape[1]
        for at in range(0, width, 128):
            here = y[:, t * width + at : t * width + at + 128]
            place = t * width + at
            if at // 128 % 3 != 1:
                here = here + bias[:, place : place + 128]
            here = here.astype(BF)
            out[:, at : at + 128] = here * jnp.asarray(scale, BF) if at // 128 % 3 == 0 else here


def qkv_fetch_kernel(pos, x, *refs):
    buffers, outs, refs = refs[:8], refs[8 : 8 + THIRDS], refs[8 + THIRDS :]
    vectors, (weight, tiny, bias, sem, sem_tiny) = refs[:8], refs[8:]

    @pl.when(pl.program_id(0) == 0)
    def _():
        copies = fetch_in(pos, buffers, weight, sem)
        small = fetch_tiny(pos, buffers, tiny, THIRDS * CW, sem_tiny)
        for copy in small + copies:
            copy.start()
        for copy in small:
            copy.wait()
        unpack_vectors(tiny, vectors)
        bias[...] = pair_bias(vectors[0][...])
        for copy in copies:
            copy.wait()

    qkv_rows(x, weight, bias, outs)


def qkv_fetch(pos, x, buffers, shards, block=256):
    tokens, model = x.shape
    vec = lambda n: (pl.BlockSpec((1, n), lambda i, p: (0, 0)), jax.ShapeDtypeStruct((1, n), F32))
    vecs = [vec(model * n) for n in (2, 1, 1, 1, 4, 1, 1, 1)]
    return pl.pallas_call(
        qkv_fetch_kernel,
        grid_spec=pltpu.PrefetchScalarGridSpec(
            num_scalar_prefetch=1,
            grid=(tokens // block,),
            in_specs=[pl.BlockSpec((block, model), lambda i, p: (i, 0))]
            + [pl.BlockSpec(memory_space=pl.ANY)] * 8,
            out_specs=[pl.BlockSpec((block, 2 * CW), lambda i, p: (i, 0))] * THIRDS + [v[0] for v in vecs],
            scratch_shapes=[
                pltpu.VMEM((LINE, model // LINE, 3 * model), BF),
                pltpu.VMEM((2, LINE, shards // LINE, 16, TINY), BF),
                pltpu.VMEM((1, 3 * model), F32),
                pltpu.SemaphoreType.DMA,
                pltpu.SemaphoreType.DMA,
            ],
        ),
        out_shape=[jax.ShapeDtypeStruct((tokens, 2 * CW), BF)] * THIRDS + [v[1] for v in vecs],
        compiler_params=params(),
        cost_estimate=cost(10),
        name="qkv_fetch",
    )(pos, x, *buffers)


def qkv_plain_kernel(x, weight, bias, *outs):
    qkv_rows(x, weight, bias, outs)


def qkv(x, weight, bias, block=256):
    tokens, model = x.shape
    full = lambda a: pl.BlockSpec(a.shape, lambda i: (0, 0))
    return pl.pallas_call(
        qkv_plain_kernel,
        grid=(tokens // block,),
        in_specs=[pl.BlockSpec((block, model), lambda i: (i, 0)), full(weight), full(bias)],
        out_specs=[pl.BlockSpec((block, 2 * CW), lambda i: (i, 0))] * THIRDS,
        out_shape=[jax.ShapeDtypeStruct((tokens, 2 * CW), BF)] * THIRDS,
        compiler_params=params(),
    )(x, weight, bias)


def aug(q,k,h,bias,lane):
    own=(lane>=64) if h else (lane<64)
    j0=0 if h else 64
    z=jnp.zeros_like(q)
    one=jnp.where(lane==j0,jnp.ones_like(q),z)
    qa=jnp.where(own,q,one)
    ka=jnp.where(own,k,jnp.where(lane==j0,bias,z))
    return qa,ka,own
def attn_fwd_kernel(cnt,q_ref,k_ref,v_ref,o_ref,l_ref):
    p=pl.program_id(0)
    q=q_ref[...];k=k_ref[...];v=v_ref[...]
    S=q.shape[0]
    lane=lax.broadcasted_iota(jnp.int32,q.shape,1)
    row=lax.broadcasted_iota(jnp.int32,q.shape,0)
    bias=jnp.where(row<cnt[p],0.0,-1e30).astype(BF)
    vt=v.T
    outs=[]
    for h in range(2):
        qa,ka,own=aug(q,k,h,bias,lane)
        s=dg(ka,qa,NT)
        m=jnp.max(s,axis=0,keepdims=True)
        e=jnp.exp(s-m)
        l=jnp.sum(e,axis=0,keepdims=True)
        ot=mm(vt[64*h:64*h+64],e.astype(BF))
        outs.append(ot*(1.0/l))
        l_ref[0,0,h:h+1,:]=m+jnp.log(l)
    o_ref[...]=jnp.concatenate(outs,axis=0).T.astype(BF)
def attn_fwd(rows, counts, pages):
    tokens, width = rows.shape
    length, pairs = tokens // pages, width // CW
    block = lambda o: pl.BlockSpec((length, 128), lambda p, h, c: (p, 3 * h + o))
    return pl.pallas_call(
        attn_fwd_kernel,
        grid_spec=pltpu.PrefetchScalarGridSpec(
            num_scalar_prefetch=1,
            grid=(pages, pairs),
            in_specs=[block(0), block(1), block(2)],
            out_specs=[
                pl.BlockSpec((length, 128), lambda p, h, c: (p, h)),
                pl.BlockSpec((1, 1, 2, length), lambda p, h, c: (p, h, 0, 0)),
            ],
        ),
        out_shape=[
            jax.ShapeDtypeStruct((tokens, pairs * 128), BF),
            jax.ShapeDtypeStruct((pages, pairs, 2, length), F32),
        ],
        compiler_params=params(),
        cost_estimate=cost(3.5 * pairs),
        name="attn_fwd",
    )(counts, rows, rows, rows)


def attn_bwd_kernel(cnt,q_ref,k_ref,v_ref,g_ref,o_ref,l_ref,d_ref,bq_ref,bv_ref):
    p=pl.program_id(1)
    q=q_ref[...];k=k_ref[...];v=v_ref[...];g=g_ref[...]
    lane=lax.broadcasted_iota(jnp.int32,q.shape,1)
    row=lax.broadcasted_iota(jnp.int32,q.shape,0)
    bias=jnp.where(row<cnt[p],0.0,-1e30).astype(BF)
    prod=g.astype(F32)*o_ref[...].astype(F32)
    hi=prod.astype(BF); lo=(prod-hi.astype(F32)).astype(BF)
    r8=lax.broadcasted_iota(jnp.int32,(16,128),0); l8=lax.broadcasted_iota(jnp.int32,(16,128),1)
    sel=jnp.where(r8==l8//64,1.0,0.0).astype(BF)
    delta=dg(sel,hi,NT)+dg(sel,lo,NT)
    kt=k.T
    dv=[];dk=[];dqt=[]
    for h in range(2):
        qa,ka,own=aug(q,k,h,bias,lane)
        s=dg(ka,qa,NT)
        pr=jnp.exp(s-l_ref[0,0,h:h+1,:])
        va=jnp.where(own,v,jnp.zeros_like(v))
        dp=dg(va,g,NT)
        ds=(pr*(dp-delta[h:h+1])).astype(BF)
        dv.append(mm(pr.astype(BF),g)); dk.append(mm(ds,q))
        dqt.append(mm(kt[64*h:64*h+64],ds))
    first=lane<64
    dvv=jnp.where(first,dv[0],dv[1])
    dq=jnp.concatenate(dqt,axis=0).T*0.125
    d_ref[:,:128]=dq.astype(BF); d_ref[:,256:]=dvv.astype(BF)
    d_ref[:,128:256]=jnp.where(first,dk[0],dk[1]).astype(BF)
    sq=jnp.sum(dq,axis=0,keepdims=True); sv=jnp.sum(dvv,axis=0,keepdims=True)
    @pl.when(p==0)
    def _():
        bq_ref[...]=sq; bv_ref[...]=sv
    @pl.when(p>0)
    def _():
        bq_ref[...]+=sq; bv_ref[...]+=sv
def attn_bwd(rows, counts, grad, out, totals, pages, at):
    tokens, width = rows.shape
    length, pairs = tokens // pages, width // CW
    block = lambda o: pl.BlockSpec((length, 128), lambda h, p, c: (p, 3 * h + o))
    line = pl.BlockSpec((1, 128), lambda h, p, c: (0, h))
    return pl.pallas_call(
        attn_bwd_kernel,
        grid_spec=pltpu.PrefetchScalarGridSpec(
            num_scalar_prefetch=1,
            grid=(pairs, pages),
            in_specs=[
                block(0),
                block(1),
                block(2),
                pl.BlockSpec((length, 128), lambda h, p, c: (p, h + at)),
                pl.BlockSpec((length, 128), lambda h, p, c: (p, h)),
                pl.BlockSpec((1, 1, 2, length), lambda h, p, c: (p, h, 0, 0)),
            ],
            out_specs=[pl.BlockSpec((length, CW), lambda h, p, c: (p, h))] + [line] * 2,
        ),
        out_shape=[jax.ShapeDtypeStruct((tokens, width), BF)]
        + [jax.ShapeDtypeStruct((1, pairs * 128), F32)] * 2,
        compiler_params=params(),
        cost_estimate=cost(4.5 * pairs),
        name="attn_bwd",
    )(counts, rows, rows, rows, grad, out, totals)


def norm(t):
    m=jnp.mean(t,axis=-1,keepdims=True); c=t-m
    v=jnp.mean(c*c,axis=-1,keepdims=True); inv=lax.rsqrt(v+1e-12)
    return c*inv,inv
def norm_back(e,hat,inv):
    return inv*(e-jnp.mean(e,axis=-1,keepdims=True)-hat*jnp.mean(e*hat,axis=-1,keepdims=True))
def col(t): return jnp.sum(t,axis=0,keepdims=True)
C=768
def rows_at(ref, start, count):
    if len(ref.shape) == 2:
        return ref[start : start + count, :]
    each = ref.shape[1]
    return ref[start // each, start % each : start % each + count, :]


def main_fetch_kernel(pos, *refs):
    att, (x, cot), refs = refs[:-49], refs[-49:-47], refs[-47:]
    two, three, refs = refs[:8], refs[8:16], refs[16:]
    vecs, (out, gf, ga), sums, refs = refs[:7], refs[7:10], refs[10:17], refs[17:]
    keep_d, send_d, keep_u, send_u, refs = *refs[:4], refs[4:]
    slope, ow, uw, dw, big, wide, held, *sems = refs
    act, pre = big.at[0], big.at[1]
    low, back, first, attended = (wide.at[n] for n in range(4))
    step = pl.program_id(0)
    rows = x.shape[0]
    blocks = act.shape[0] // rows
    copies = (
        fetch(pos, two, ow, 48, 0, CW, sems[0]),
        fetch(pos, two, uw, 48, CW, uw.shape[2] // 2, sems[1]),
        fetch(pos, three, dw, dw.shape[1] // 4, 0, CW, sems[2]),
    )

    @pl.when(step == 0)
    def _():
        for group in copies:
            for copy in group:
                copy.start()

    def ready(place):
        @pl.when(step == 0)
        def _():
            for copy in copies[place]:
                copy.wait()

    @pl.when(step < blocks)
    def _():
        here = pl.ds(pl.multiple_of(step * rows, 16), rows)
        attended[here, :] = joined(att)
        main_kernel(
            att, x, cot, ow, uw, dw, *vecs, out,
            act.at[here, :], back.at[here, :], low.at[here, :], pre.at[here, :], first.at[here, :],
            gf, ga, *sums, slope, ready,
        )

    @pl.when((step >= blocks) & (step < blocks + LINE))
    def _():
        chip = (pos[0] + step - blocks) & (LINE - 1)
        columns = act.shape[1] // LINE
        here = pl.ds(pl.multiple_of(chip * columns, 128), columns)
        hold(held, dg(act[:, here], back[...], TN))
        place_tile(pos, held, keep_d, send_d, held.shape[1] // 4, [(0, 0)])

    @pl.when(step == blocks + LINE)
    def _():
        hold(held, dg(attended[...], first[...], TN))
        place_tile(pos, held, keep_u, send_u, 48, whole_line(pos))

    @pl.when(step > blocks + LINE)
    def _():
        at = pl.multiple_of((step - blocks - LINE - 1) * CW, 128)
        right = pl.multiple_of(at + pre.shape[1] // 2, 128)
        columns = jnp.concatenate([pre[:, pl.ds(at, CW)], pre[:, pl.ds(right, CW)]], axis=1)
        hold(held, dg(low[...], columns, TN))
        place_tile(pos, held, keep_u, send_u, 48, whole_line(pos))


def main_fetch(pos, att, x, cot, weights, vecs, rows=512):
    T, D = x.shape
    FF = vecs[3].shape[1]
    blocks, ups = T // rows, FF // 2 // CW
    rb = lambda n: pl.BlockSpec((rows, n), lambda i, p: (jnp.minimum(i, blocks - 1), 0))
    full = lambda a: pl.BlockSpec(a.shape, lambda i, p: (0, 0))
    vec = lambda n: (pl.BlockSpec((1, n), lambda i, p: (0, 0)), jax.ShapeDtypeStruct((1, n), F32))
    vs = [vec(n) for n in (D, D, D, FF, D, D, D)]
    down = pl.BlockSpec(
        (2, 2, 1, FF // 16, CW), lambda i, p: (0, 0, jnp.clip(i - blocks, 0, LINE - 1), 0, 0)
    )
    up = pl.BlockSpec(
        (2, 2, LINE, 48, CW), lambda i, p: (0, 0, 0, 0, jnp.clip(i - blocks - LINE, 0, ups))
    )
    shapes = [(2, 2, LINE, FF // 16, CW)] * 2 + [(2, 2, LINE, 48, CW * (1 + ups))] * 2
    return pl.pallas_call(
        main_fetch_kernel,
        grid_spec=pltpu.PrefetchScalarGridSpec(
            num_scalar_prefetch=1,
            grid=(blocks + LINE + 1 + ups,),
            in_specs=[rb(a.shape[1]) for a in (*att, x, cot)]
            + [pl.BlockSpec(memory_space=pl.ANY)] * len(weights)
            + [full(v) for v in vecs],
            out_specs=[rb(D)] * 3 + [v[0] for v in vs] + [down, down, up, up],
            scratch_shapes=[
                pltpu.VMEM((rows, FF), BF),
                pltpu.VMEM((LINE, D // LINE, D), BF),
                pltpu.VMEM((LINE, D // LINE, FF), BF),
                pltpu.VMEM((LINE, FF // LINE, D), BF),
                pltpu.VMEM((2, T, FF), BF),
                pltpu.VMEM((4, T, D), BF),
                pltpu.VMEM((2, 16 * 48, CW), BF),
            ]
            + [pltpu.SemaphoreType.DMA] * 3,
        ),
        out_shape=[jax.ShapeDtypeStruct((T, D), t) for t in (BF, F32, BF)]
        + [v[1] for v in vs]
        + [jax.ShapeDtypeStruct(a, BF) for a in shapes],
        compiler_params=params(),
        cost_estimate=cost(58),
        name="main",
    )(pos, *att, x, cot, *weights, *vecs)


def main_plain_kernel(*refs):
    main_kernel(refs[:-28], *refs[-28:])


def main_kernel(att,x,cot,ow,uw,dw,ob,g1,s1,ub,db,g2,s2,
                lo_ref,act_ref,sl_ref,nl_ref,pl_ref,fl_ref,gf_ref,ga_ref,
                vg2,vs2,vdb,vub,vg1,vs1,vob,slope,ready=lambda place: None):
    i=pl.program_id(0)
    FF=uw.shape[-1]
    ready(0)
    fs=x[...].astype(F32)+mm(joined(att),flat(ow))+ob[...]
    fh,fi=norm(fs)
    normed=fh*g1[...]+s1[...]
    nl=normed.astype(BF); nl_ref[...]=nl
    acc=normed+db[...]
    ready(1)
    for j in range(0,FF,C):
        pre=mm(nl,flat(uw,j,C))+ub[:,j:j+C]
        phi=0.5*(1.0+lax.erf(pre*(1.0/math.sqrt(2.0))))
        a=(pre*phi).astype(BF)
        act_ref[:,j:j+C]=a
        slope[:,j:j+C]=(phi+pre*jnp.exp(-0.5*pre*pre)*(1.0/math.sqrt(2.0*math.pi))).astype(slope.dtype)
        if j==0: ready(2)
        acc=acc+mm(a,rows_at(dw,j,C))
    sh,si=norm(acc)
    lo_ref[...]=(sh*g2[...]+s2[...]).astype(BF)
    gr=cot[...].astype(F32)
    gs=norm_back(gr*g2[...],sh,si)
    sl=gs.astype(BF); sl_ref[...]=sl
    gn=gs
    ubs=[]
    for j in range(0,FF,C):
        gp=dg(sl,rows_at(dw,j,C),NT)*slope[:,j:j+C]
        ubs.append(col(gp))
        gpl=gp.astype(BF); pl_ref[:,j:j+C]=gpl
        gn=gn+dg(gpl,flat(uw,j,C),NT)
    gf=norm_back(gn*g1[...],fh,fi)
    fl=gf.astype(BF); fl_ref[...]=fl; gf_ref[...]=gf
    ga_ref[...]=dg(fl,flat(ow),NT).astype(BF)
    vals=[(vg2,col(gr*sh)),(vs2,col(gr)),(vdb,col(gs)),(vub,jnp.concatenate(ubs,1)),(vg1,col(gn*fh)),(vs1,col(gn)),(vob,col(gf))]
    @pl.when(i==0)
    def _():
        for r,v in vals: r[...]=v
    @pl.when(i>0)
    def _():
        for r,v in vals: r[...]+=v
def main(att, x, cot, weights, vecs, R=256):
    T, D = x.shape
    FF = vecs[3].shape[1]
    rb = lambda n: pl.BlockSpec((R, n), lambda i: (i, 0))
    full = lambda a: pl.BlockSpec(a.shape, lambda i: (0, 0))
    sds = lambda n, t=BF: jax.ShapeDtypeStruct((T, n), t)
    vec = lambda n: (pl.BlockSpec((1, n), lambda i: (0, 0)), jax.ShapeDtypeStruct((1, n), F32))
    vs = [vec(n) for n in (D, D, D, FF, D, D, D)]
    return pl.pallas_call(
        main_plain_kernel,
        grid=(T // R,),
        in_specs=[rb(a.shape[1]) for a in (*att, x, cot)] + [full(w) for w in weights] + [full(v) for v in vecs],
        out_specs=[rb(D), rb(FF), rb(D), rb(D), rb(FF), rb(D), rb(D), rb(D)] + [v[0] for v in vs],
        out_shape=[sds(D), sds(FF), sds(D), sds(D), sds(FF), sds(D), sds(D, F32), sds(D)] + [v[1] for v in vs],
        scratch_shapes=[pltpu.VMEM((R, FF), F32)],
        compiler_params=params(),
        name="main",
    )(*att, x, cot, *weights, *vecs)


def tn_kernel(a,b,o): o[...]=dg(a[...],b[...],TN).astype(BF)
def tn(a,b,bm,bn):
    T,M=a.shape;N=b.shape[1]
    return pl.pallas_call(tn_kernel,grid=(M//bm,N//bn),
      in_specs=[pl.BlockSpec((T,bm),lambda i,j:(0,i)),pl.BlockSpec((T,bn),lambda i,j:(0,j))],
      out_specs=pl.BlockSpec((bm,bn),lambda i,j:(i,j)),out_shape=jax.ShapeDtypeStruct((M,N),BF),compiler_params=params())(a,b)
def ig_kernel(gf, parts, w, o):
    o[...] = (gf[...] + dg(joined(parts), flat(w), NT)).astype(BF)


def ig_plain_kernel(gf, *refs):
    ig_kernel(gf, refs[:-2], refs[-2], refs[-1])


def ig_fetch_kernel(pos, gf, *refs):
    parts, buffers, (o, weight, sem) = refs[:-11], refs[-11:-3], refs[-3:]

    @pl.when(pl.program_id(0) == 0)
    def _():
        run_all(fetch_in(pos, buffers, weight, sem))

    ig_kernel(gf, parts, weight, o)


def ig(parts, gf, weights, pos=None, R=256):
    T, D = gf.shape
    rb = lambda n: pl.BlockSpec((R, n), lambda i, *p: (i, 0))
    fetched = pos is not None
    return pl.pallas_call(
        ig_fetch_kernel if fetched else ig_plain_kernel,
        grid_spec=pltpu.PrefetchScalarGridSpec(
            num_scalar_prefetch=1 if fetched else 0,
            grid=(T // R,),
            in_specs=[rb(a.shape[1]) for a in (gf, *parts)]
            + [pl.BlockSpec(memory_space=pl.ANY) if fetched else pl.BlockSpec(w.shape, lambda i, *p: (0, 0)) for w in weights],
            out_specs=rb(D),
            scratch_shapes=[pltpu.VMEM((LINE, D // LINE, 3 * D), BF), pltpu.SemaphoreType.DMA] if fetched else [],
        ),
        out_shape=jax.ShapeDtypeStruct((T, D), BF),
        compiler_params=params(),
        cost_estimate=cost(10),
        name="ig",
    )(*([pos] if fetched else []), gf, *parts, *weights)


def local(
    hidden_states,
    page_counts,
    cotangent,
    attn_in_weight,
    attn_in_bias,
    attn_out_weight,
    attn_out_bias,
    first_gain,
    first_shift,
    up_weight,
    up_bias,
    down_weight,
    down_bias,
    second_gain,
    second_shift,
):
    pages, length, model = hidden_states.shape
    hidden = up_weight.shape[1]
    x = hidden_states.reshape(-1, model)
    grad_rows = cotangent.reshape(-1, model)
    weights = (attn_in_weight, attn_out_weight, up_weight, down_weight)
    vectors = (
        attn_in_bias,
        attn_out_bias,
        first_gain,
        first_shift,
        up_bias,
        down_bias,
        second_gain,
        second_shift,
    )
    lined = lax.axis_size("fsdp") == 4 * LINE and lax.axis_size("rep") == 2
    pairs = HEADS // 2 // THIRDS
    forward = [None] * THIRDS
    backward = [None] * THIRDS

    def ahead(t, rows):
        forward[t] = attn_fwd(rows, page_counts, pages)

    def back(t, rows):
        backward[t] = attn_bwd(rows, page_counts, grad_att, *forward[t], pages, pairs * t)

    if lined:
        index = lax.axis_index("fsdp")
        pos = jnp.stack([index // 4, index // 2 % 2, index % 2, lax.axis_index("rep")]).astype(jnp.int32)
        one, two, three = pack(pos, weights, vectors)
        line_one = in_order(along_line(one))
        second_one = move(line_one, to_second)
        first_one = move(line_one, to_first)
        parts_two = along_line(after(two, line_one))
        parts_three = along_line(after(three, line_one))
        both_one = move(after(second_one, *parts_two[1:]), to_first)
        in_w = over_core((line_one, first_one, second_one, both_one))
        line_two = in_order(parts_two)
        second_two = move(line_two, to_second)
        first_two = move(line_two, to_first)
        outs = qkv_fetch(pos, x, after(in_w, line_two), 16)
        rows, full = outs[:THIRDS], outs[THIRDS:]
        line_three = in_order(after(parts_three, rows))
        second_three = move(line_three, to_second)
        first_three = move(line_three, to_first)
        ahead(0, after(rows[0], line_three))
        both_two = move(after(second_two, forward[0]), to_first)
        ahead(1, after(rows[1], forward[0], second_two))
        both_three = move(after(second_three, forward[1]), to_first)
        early = [move(part, to_core) for part in after((line_two,), forward[0])]
        ready = (line_two, first_two, second_two, line_three, first_three, second_three)
        moved = [move(part, to_core) for part in after(ready[1:], forward[1])]
        ahead(2, after(rows[2], forward[1], second_three, first_three, *early))
        ready += (*early, *moved)
        last = over_core(after((both_two, both_three), forward[2]))
        later = (*ready[0:3], last[0], *ready[6:9], last[2], *ready[3:6], last[1], *ready[9:12], last[3])
    else:
        pos = None
        gathered = lambda a: lax.all_gather(a, "fsdp", axis=0, tiled=True)
        in_w = gathered(attn_in_weight).reshape(model, 3, -1, 128)
        in_w = (in_w.transpose(0, 2, 1, 3).reshape(model, 3 * model),)
        full = [gathered(v).astype(F32).reshape(1, -1) for v in vectors]
        later = tuple(gathered(w) for w in weights[1:])
        rows = qkv(x, in_w[0], pair_bias(full[0]))
        for t in range(THIRDS):
            ahead(t, rows[t])
    attended = [f[0] for f in forward]
    if lined:
        (
            output, grad_first, grad_att, vg2, vs2, vdb, vub, vg1, vs1, vob,
            keep_d, send_d, keep_u, send_u,
        ) = main_fetch(pos, attended, x, grad_rows, later, full[1:])
        core_d = move(send_d, to_core)
        core_u = move(send_u, to_core)
        back(0, rows[0])
        go_d, stay_d = add_wide(*after((keep_d, core_d), backward[0]))
        first_d = move(go_d, to_first)
        go_u, stay_u = add_wide(*after((keep_u, core_u), go_d))
        first_u = move(go_u, to_first)
        back(1, after(rows[1], go_u, stay_u))
        go_d, stay_d = add_core(*after((stay_d, first_d), backward[1]))
        second_d = move(go_d, to_second)
        keep_i, send_i = grad_in(pos, x, after((backward[0][0], backward[1][0]), go_d, stay_d))
        core_i = move(send_i, to_core)
        back(2, after(rows[2], keep_i))
        parts = tuple(b[0] for b in backward)
        vbq = [b[1] for b in backward]
        vbv = [b[2] for b in backward]
        go_u, stay_u = add_core(*after((stay_u, first_u), backward[2]))
        second_u = move(go_u, to_second)
        go_i, stay_i = add_wide(*after((keep_i, core_i), go_u, stay_u))
        first_i = move(go_i, to_first)
        low_d = add_last(*after((stay_d, second_d), go_i))
        line_d = move_line(low_d)
        keep_l, send_l = grad_last(
            pos, x, after(parts[2], go_i, stay_i, low_d), (*vbq, *vbv, vub, vob, vg1, vs1, vdb, vg2, vs2)
        )
        core_l = move(send_l, to_core)
        mine_d = add_line(low_d, after(line_d, keep_l))
        low_u = add_last(*after((stay_u, second_u), mine_d))
        line_u = move_line(low_u)
        go_l, stay_l = add_core(keep_l, after(core_l, low_u))
        first_l = move(go_l, to_first)
        go_i, stay_i = add_core(*after((stay_i, first_i), go_l, stay_l))
        second_i = move(go_i, to_second)
        input_grad = ig(parts, after(grad_first, go_i, stay_i), in_w, pos)
        mine_u = add_line(low_u, after(line_u, input_grad))
        low_i = add_last(*after((stay_i, second_i), mine_u))
        line_i = move_line(low_i)
        go_l, stay_l = add_core(*after((stay_l, first_l), low_i))
        second_l = move(go_l, to_second)
        got_d = move(after(mine_d, go_l), to_x)
        low_l = add_last(*after((stay_l, second_l), go_l))
        mine_i = add_line(low_i, after(line_i, low_l))
        line_l = move_line(after(low_l, mine_i))
        got_u = move(after(mine_u, mine_i), to_x)
        got_i = move(mine_i, to_x)
        (t_down,) = finish(
            finish_down_kernel, "finish_down", pos, (mine_d, after(got_d, low_l)), [down_weight.shape]
        )
        mine_l = add_line(low_l, after(line_l, t_down))
        got_l = move(mine_l, to_x)
        shapes = [attn_out_weight.shape, up_weight.shape, attn_in_weight.shape]
        shapes += [(1, v.shape[0]) for v in vectors]
        t_out, t_up, t_in, *small = finish(
            finish_kernel, "finish", pos, (mine_u, got_u, mine_i, got_i, mine_l, got_l), shapes
        )
        small = [b.reshape(-1) for b in small]
    else:
        (
            output, act, second_low, normed_low, pre_low, first_low, grad_first, grad_att,
            vg2, vs2, vdb, vub, vg1, vs1, vob,
        ) = main(attended, x, grad_rows, later, full[1:])
        for t in range(THIRDS):
            back(t, rows[t])
        parts = tuple(b[0] for b in backward)
        vbq = jnp.concatenate([b[1] for b in backward], axis=1)
        vbv = jnp.concatenate([b[2] for b in backward], axis=1)
        input_grad = ig(parts, grad_first, in_w)

        def total(a):
            share = lax.psum_scatter(a.astype(BF), "fsdp", scatter_dimension=0, tiled=True)
            return lax.psum(share, "rep").astype(F32)

        att = jnp.concatenate(attended, axis=1)
        t_down = total(tn(act, second_low, 768, 768))
        t_up = total(tn(normed_low, pre_low, 768, 768))
        t_out = total(tn(att, first_low, 768, 768))
        t_in = jnp.concatenate([tn(x, d, 768, 768) for d in parts], axis=1)
        t_in = total(t_in.reshape(model, -1, 3, 128).transpose(0, 2, 1, 3).reshape(model, 3 * model))
        small = [
            total(v.reshape(-1))
            for v in (jnp.concatenate([vbq, vbv], axis=1), vob, vg1, vs1, vub, vdb, vg2, vs2)
        ]
    b_in, b_out, b_g1, b_s1, b_up, b_down, b_g2, b_s2 = small
    return (
        output.reshape(hidden_states.shape),
        input_grad.reshape(hidden_states.shape),
        t_in, b_in, t_out, b_out, b_g1, b_s1, t_up, b_up, t_down, b_down, b_g2, b_s2,
    )


def solution(mesh):
    return jax.shard_map(
        local,
        mesh=mesh,
        in_specs=(
            P(("fsdp", "rep"), None, None),
            P(("fsdp", "rep")),
            P(("fsdp", "rep"), None, None),
            P("fsdp", None),
            P("fsdp"),
            P("fsdp", None),
            P("fsdp"),
            P("fsdp"),
            P("fsdp"),
            P("fsdp", None),
            P("fsdp"),
            P("fsdp", None),
            P("fsdp"),
            P("fsdp"),
            P("fsdp"),
        ),
        out_specs=(
            P(("fsdp", "rep"), None, None),
            P(("fsdp", "rep"), None, None),
            P("fsdp", None),
            P("fsdp"),
            P("fsdp", None),
            P("fsdp"),
            P("fsdp"),
            P("fsdp"),
            P("fsdp", None),
            P("fsdp"),
            P("fsdp", None),
            P("fsdp"),
            P("fsdp"),
            P("fsdp"),
        ),
        check_vma=False,
    )
```
